128 devices in a mesh: freq: 8 (over z_hi, y), shot: 16 (over z_lo, x, core).
Axes of the slice: x: 4, y: 4, z: 4 (z_hi: 2, z_lo: 2; z = z_hi * 2 + z_lo), core: 2. Of those that a mesh axis runs over, the one named last changes fastest.
Arguments:
- source_field: bfloat16 [16, 16, 2, 128, 4096], P('freq', 'shot'), may hold values from -6 to 6
- receiver_field: bfloat16 [16, 16, 2, 128, 4096], P('freq', 'shot'), may hold values from -6 to 6
- angular_freq: float32 [16], P('freq'), may hold values from 2 to 40
- x_correction: bfloat16 [16, 2, 128, 128], P('freq'), may hold values from -0.25 to 0.25
- y_correction: bfloat16 [16, 2, 128, 128], P('freq'), may hold values from -0.25 to 0.25
- velocity: float32 [16, 128, 4096], P('shot'), may hold values from -1.2 to 1.2
- slab_owner: int32 [2], replicated, may hold values from 0 to 15, as said below
- apertures: int32 [16, 2], P('shot'), may hold values from 0 to 63
- tile_order: int32 [64], replicated, may hold values from 0 to 63, each once
Outputs:
- source_out: bfloat16 [16, 16, 2, 128, 4096], P('freq', 'shot')
- receiver_out: bfloat16 [16, 16, 2, 128, 4096], P('freq', 'shot')
- image: float32 [64, 2, 8192], P('shot', None, 'freq')
The draws below stay inside these ranges and needn't reach their ends.
Inputs may be any that keep to these rules, and one draw needn't show every extreme that they name: `slab_owner`: the 2 entries are all different. `tile_order`: a permutation of all tiles.
All inputs are finite; a program needn't handle non-finite values.
Results may differ from the reference program's by a relative error of at most 0.0094.
Values sent between devices are 32-bit elements; how exact they have to be, the bound alone decides.
No kernel may reach another device: no remote copies, remote signals or barrier semaphores. Data moves between devices by JAX's collectives and lax.ppermute only.
A program may use at most 128 MiB of HBM per device.

```python
import math
import jax
import jax.numpy as jnp
import numpy as np
from jax import lax

NX = 4096
YW = 128
BLOCK = 128
DEPTH = 2
APER = 2
FREQS = 16
SHOTS = 16
TILES = 64
TX = 64


def draw_slab_owner(key, part):
    key = jax.random.fold_in(key, 11)
    shuffle_key, place_key = jax.random.split(key)
    others = jax.random.permutation(shuffle_key, SHOTS - 1).astype(jnp.int32)
    others = jnp.concatenate([others, jnp.zeros((1,), jnp.int32)])
    place = jax.random.randint(place_key, (), 0, DEPTH).astype(jnp.int32)
    steps = jnp.arange(DEPTH, dtype=jnp.int32)
    before = others[steps]
    after = others[jnp.maximum(steps - 1, 0)]
    picked = jnp.where(steps < place, before, after)
    picked = jnp.where(steps == place, jnp.int32(SHOTS - 1), picked)
    return picked.astype(jnp.int32)


def place_ends(values, own_key, low, largest):
    longest = values.shape.index(max(values.shape))
    spots = []
    for shift in (0, 1):
        where = [jax.random.randint(jax.random.fold_in(own_key, axis), (), 0, length) for axis, length in enumerate(values.shape)]
        where[longest] = (where[longest] + shift) % values.shape[longest]
        spots.append(tuple(where))
    return values.at[spots[0]].set(low).at[spots[1]].set(largest)


def level_of(rng, dims, pieces, least, largest):
    loudness, own = 1.0, jax.random.fold_in(rng, 6)
    for axis_at, blocks in pieces:
        steps = jnp.exp(jax.random.uniform(jax.random.fold_in(own, axis_at), (blocks,), jnp.float32, least / len(pieces), largest / len(pieces)))
        loudness = loudness * jnp.repeat(steps, dims[axis_at] // blocks).reshape([-1 if axis == axis_at else 1 for axis in range(len(dims))])
    return loudness


def rank_bounds(count, slope):
    weights = [(1 << 20) // math.isqrt(standing ** slope) + 1 for standing in range(1, count + 1)]
    spread = 1 + sum(weights) // (1 << 30)
    return np.cumsum(np.array([max(1, weight // spread) for weight in weights]))


def ranked_ids(stream_key, dims, amount, skew):
    grid = rank_bounds(amount, skew)
    pick = jax.random.randint(jax.random.fold_in(stream_key, 1), dims, 0, int(grid[amount - 1]))
    rank = jnp.searchsorted(jnp.asarray(grid, jnp.int32), pick, side="right")
    return jax.random.permutation(jax.random.fold_in(stream_key, 2), amount)[rank].astype(jnp.int32)


def bell_draw(rng, extent, deviation, reach, cuts=(), held_as=jnp.bfloat16):
    loudness = level_of(rng, extent, cuts, -0.22, 0.18) if cuts else 1.0
    entries = jax.random.normal(rng, extent, jnp.float32) * deviation * loudness
    return jnp.minimum(jnp.maximum(entries, -reach), reach).astype(held_as)


def setup_inputs(seed: int = 0) -> dict:
    keys = jax.random.split(jax.random.key(seed), 10)
    return {
        "source_field": bell_draw(keys[0], (FREQS, SHOTS, 2, YW, NX), 1.0, 6.0, ((0, 8), (1, 16))),
        "receiver_field": bell_draw(keys[1], (FREQS, SHOTS, 2, YW, NX), 1.0, 6.0, ((0, 8), (1, 16))),
        "angular_freq": jnp.clip(jnp.exp(math.log(40.0) - 2.9957323 * jax.random.uniform(keys[2], (FREQS,), jnp.float32) ** level_of(keys[2], (FREQS,), ((0, 8),), -0.2, 0.2)), 2.0, 40.0),
        "x_correction": bell_draw(keys[3], (FREQS, 2, BLOCK, BLOCK), (4 * BLOCK) ** -0.5, 0.25, ((0, 8),)),
        "y_correction": bell_draw(keys[4], (FREQS, 2, BLOCK, BLOCK), (4 * BLOCK) ** -0.5, 0.25, ((0, 8),)),
        "velocity": bell_draw(keys[5], (SHOTS, YW, NX), 0.2, 1.2, ((0, 16),), jnp.float32),
        "slab_owner": draw_slab_owner(jax.random.fold_in(keys[9], 71), 0),
        "apertures": place_ends(ranked_ids(keys[7], (SHOTS, APER), TILES, 2), jax.random.fold_in(keys[7], 3), 0, TILES - 1).astype(jnp.int32),
        "tile_order": jax.random.permutation(keys[8], TILES).astype(jnp.int32),
    }


def lens(field, phase_angle, conj_sign):
    real_part = field[..., 0, :, :].astype(jnp.float32)
    imag_part = field[..., 1, :, :].astype(jnp.float32)
    cosine = jnp.cos(phase_angle)
    sine = conj_sign * jnp.sin(phase_angle)
    new_real = real_part * cosine - imag_part * sine
    new_imag = real_part * sine + imag_part * cosine
    return jnp.stack([new_real, new_imag], axis=-3).astype(jnp.bfloat16)


def sweep_x(field, correction, conj_sign):
    shape = field.shape
    width = correction.shape[-1]
    blocks = field.astype(jnp.float32).reshape(shape[:-1] + (shape[-1] // width, width))
    real_part = blocks[:, 0]
    imag_part = blocks[:, 1]
    c_real = correction[0].astype(jnp.float32)
    c_imag = correction[1].astype(jnp.float32)
    new_real = real_part + jnp.einsum('synk,kj->synj', real_part, c_real) - conj_sign * jnp.einsum('synk,kj->synj', imag_part, c_imag)
    new_imag = imag_part + jnp.einsum('synk,kj->synj', imag_part, c_real) + conj_sign * jnp.einsum('synk,kj->synj', real_part, c_imag)
    return jnp.stack([new_real, new_imag], axis=1).reshape(shape).astype(jnp.bfloat16)


def sweep_y(field, correction, conj_sign):
    shape = field.shape
    width = correction.shape[-1]
    blocks = field.astype(jnp.float32).reshape(shape[:2] + (shape[2] // width, width, shape[3]))
    real_part = blocks[:, 0]
    imag_part = blocks[:, 1]
    c_real = correction[0].astype(jnp.float32)
    c_imag = correction[1].astype(jnp.float32)
    new_real = real_part + jnp.einsum('snkx,kj->snjx', real_part, c_real) - conj_sign * jnp.einsum('snkx,kj->snjx', imag_part, c_imag)
    new_imag = imag_part + jnp.einsum('snkx,kj->snjx', imag_part, c_real) + conj_sign * jnp.einsum('snkx,kj->snjx', real_part, c_imag)
    return jnp.stack([new_real, new_imag], axis=1).reshape(shape).astype(jnp.bfloat16)


def reference(source_field, receiver_field, angular_freq, x_correction, y_correction, velocity, slab_owner, apertures, tile_order):
    slabs = [velocity[slab_owner[depth_step]] for depth_step in range(DEPTH)]

    def one_frequency(carry, inputs):
        source, receiver, angular, x_corr, y_corr = inputs
        totals = []
        for depth_step in range(DEPTH):
            phase_angle = angular * slabs[depth_step]
            source = sweep_y(sweep_x(lens(source, phase_angle, 1.0), x_corr, 1.0), y_corr, 1.0)
            receiver = sweep_y(sweep_x(lens(receiver, phase_angle, -1.0), x_corr, -1.0), y_corr, -1.0)
            image_term = source[:, 0].astype(jnp.float32) * receiver[:, 0].astype(jnp.float32) + source[:, 1].astype(jnp.float32) * receiver[:, 1].astype(jnp.float32)
            totals.append(carry[depth_step] + image_term)
        return tuple(totals), (source, receiver)

    start = tuple(jnp.zeros((SHOTS, YW, NX), jnp.float32) for depth_step in range(DEPTH))
    totals, outputs = lax.scan(one_frequency, start, (source_field, receiver_field, angular_freq, x_correction, y_correction))
    source_out, receiver_out = outputs
    match_table = (apertures[:, :, None] == tile_order[None, None, :]).astype(jnp.float32)
    shot_index = jnp.arange(SHOTS)[:, None]
    images = []
    for depth_step in range(DEPTH):
        image_term = totals[depth_step] / FREQS
        blocks = jnp.transpose(image_term.reshape(SHOTS, YW, TILES, TX), (0, 2, 1, 3))
        picked = blocks[shot_index, apertures]
        images.append(jnp.einsum('sap,sayx->pyx', match_table, picked, precision=lax.Precision.HIGHEST))
    image = jnp.stack(images, axis=1).reshape(TILES, DEPTH, YW * TX)
    return source_out, receiver_out, image
```

```python
import functools
import math

import jax
import jax.numpy as jnp
from jax import lax
from jax.experimental import pallas as pl
from jax.experimental.pallas import tpu as pltpu
from jax.sharding import PartitionSpec as P

DEPTH = 2
TILE_DEV = 4
BLOCK = 128
SIN = (4.442867755889893, -7.307443618774414, 3.594788074493408, -0.7843739986419678)
COS = (1.4142135381698608, -6.978850841522217, 5.7394609451293945, -1.8835630416870117, 0.31069818139076233)


def poly(u, coefs):
    total = coefs[-1] * u + coefs[-2]
    for c in coefs[-3::-1]:
        total = total * u + c
    return total


def sincos(turns):
    r = turns - jnp.round(turns)
    u = r * r
    s = r * poly(u, SIN)
    c = poly(u, COS)
    return s * c, 1.0 - s * s


def quad(a, b, c, d):
    a, b, c, d = (v.astype(jnp.bfloat16) for v in (a, b, c, d))
    return jnp.concatenate([jnp.concatenate([a, b], 1), jnp.concatenate([c, d], 1)], 0)


def advance(parts, phases, wx, wy):
    freqs, blocks = len(parts), len(parts[0])
    height, width = parts[0][0][0].shape
    out = [[None] * blocks for _ in range(freqs)]
    for f in range(freqs):
        for b in range(blocks):
            sr, si, rr, ri = parts[f][b]
            sin, cos = sincos(phases[f][b])
            out[f][b] = (sr * cos - si * sin, sr * sin + si * cos, rr * cos - ri * sin, rr * sin + ri * cos)
    for f in range(freqs):
        left = jnp.concatenate([quad(*out[f][b]) for b in range(blocks)], 0)
        prod = jnp.dot(left, wx[f], preferred_element_type=jnp.float32)
        for b in range(blocks):
            x = prod[b * 2 * height : (b + 1) * 2 * height]
            sr, si, rr, ri = out[f][b]
            out[f][b] = (
                sr + x[:height, :width],
                si + x[:height, width:],
                rr + x[height:, :width],
                ri + x[height:, width:],
            )
    for f in range(freqs):
        right = jnp.concatenate([quad(v[0], v[2], v[1], v[3]) for v in out[f]], 1)
        prod = jnp.dot(wy[f], right, preferred_element_type=jnp.float32)
        for b in range(blocks):
            y = prod[:, b * 2 * width : (b + 1) * 2 * width]
            sr, si, rr, ri = out[f][b]
            out[f][b] = (
                sr + y[:height, :width],
                si + y[height:, :width],
                rr + y[:height, width:],
                ri + y[height:, width:],
            )
    return out


def load_parts(src, rcv, cols):
    f32 = jnp.float32
    return [
        [
            (
                src[f, 0, 0, :, c].astype(f32),
                src[f, 0, 1, :, c].astype(f32),
                rcv[f, 0, 0, :, c].astype(f32),
                -rcv[f, 0, 1, :, c].astype(f32),
            )
            for c in cols
        ]
        for f in range(src.shape[0])
    ]


def march_body(where, turns, slab, wx, wy, src, rcv, *rest):
    so, ro = rest[-2:]
    freqs = src.shape[0]
    cols = [slice(c, c + BLOCK) for c in range(0, src.shape[-1], BLOCK)]
    parts = load_parts(src, rcv, cols)
    for d in range(slab.shape[1]):
        phases = [[slab[0, d, :, c] * turns[f] for c in cols] for f in range(freqs)]
        parts = advance(parts, phases, wx, wy)
    for f in range(freqs):
        for b, c in enumerate(cols):
            sr, si, rr, ri = parts[f][b]
            so[f, 0, 0, :, c] = sr.astype(so.dtype)
            so[f, 0, 1, :, c] = si.astype(so.dtype)
            ro[f, 0, 0, :, c] = rr.astype(ro.dtype)
            ro[f, 0, 1, :, c] = (-ri).astype(ro.dtype)


def march(where, turns, slabs, wx, wy, src, rcv, done=()):
    count, steps, height, cols = slabs.shape
    freqs = src.shape[0]
    field = pl.BlockSpec((freqs, 1, 2, height, cols), lambda i, w: (0, 0, 0, 0, w[i]))
    whole = lambda a: pl.BlockSpec(a.shape, lambda i, w: (0,) * a.ndim)
    args = [turns, slabs, wx, wy, src, rcv]
    in_specs = [
        pl.BlockSpec(memory_space=pltpu.SMEM),
        pl.BlockSpec((1, steps, height, cols), lambda i, w: (i, 0, 0, 0)),
        whole(wx),
        whole(wy),
        field,
        field,
    ]
    alias = {len(args) + 1 + i: i for i in range(len(done))}
    cells = count * cols * height * freqs
    return pl.pallas_call(
        march_body,
        grid_spec=pltpu.PrefetchScalarGridSpec(
            num_scalar_prefetch=1,
            grid=(count,),
            in_specs=in_specs + [pl.BlockSpec(memory_space=pl.ANY)] * len(done),
            out_specs=[field, field],
        ),
        out_shape=[jax.ShapeDtypeStruct(src.shape, src.dtype), jax.ShapeDtypeStruct(rcv.shape, rcv.dtype)],
        input_output_aliases=alias,
        cost_estimate=pl.CostEstimate(
            flops=cells * steps * 4 * 2 * 4 * BLOCK, bytes_accessed=cells * 16, transcendentals=0
        ),
        compiler_params=pltpu.CompilerParams(vmem_limit_bytes=48 * 1024 * 1024),
    )(where, *args, *done)


def image_body(tiles, slot, turns, wx, wy, src, rcv, *rest, scale, per):
    slabs, out, held, sem = rest[:-3], rest[-3], rest[-2], rest[-1]
    i = pl.program_id(0)
    column = pl.multiple_of(lax.rem(lax.div(tiles[i], 2), per) * BLOCK, BLOCK)
    for k, slab in enumerate(slabs):

        @pl.when(slot[i] == k)
        def _():
            pltpu.make_async_copy(slab.at[:, :, pl.ds(column, BLOCK)], held, sem).start()

    pltpu.make_async_copy(slabs[0].at[:, :, pl.ds(0, BLOCK)], held, sem).wait()
    freqs = src.shape[0]
    parts = load_parts(src, rcv, [slice(0, BLOCK)])
    half = BLOCK // 2
    odd = lax.rem(tiles[i], 2) == 1
    for d in range(held.shape[0]):
        parts = advance(parts, [[held[d] * turns[f]] for f in range(freqs)], wx, wy)
        term = sum(p[0][0] * p[0][2] - p[0][1] * p[0][3] for p in parts) * scale
        out[0, d] = jnp.where(odd, term[:, half:], term[:, :half])


def image_terms(tiles, slot, turns, wx, wy, src, rcv, slabs, scale):
    steps, height, cols = slabs[0].shape
    freqs = src.shape[0]
    field = pl.BlockSpec((freqs, 1, 2, height, BLOCK), lambda i, t, s: (0, 0, 0, 0, lax.div(t[i], 2)))
    whole = lambda a: pl.BlockSpec(a.shape, lambda i, t, s: (0,) * a.ndim)
    return pl.pallas_call(
        functools.partial(image_body, scale=scale, per=cols // BLOCK),
        grid_spec=pltpu.PrefetchScalarGridSpec(
            num_scalar_prefetch=2,
            grid=(tiles.shape[0],),
            in_specs=[pl.BlockSpec(memory_space=pltpu.SMEM), whole(wx), whole(wy), field, field]
            + [pl.BlockSpec(memory_space=pl.ANY)] * len(slabs),
            out_specs=pl.BlockSpec((1, steps, height, BLOCK // 2), lambda i, t, s: (i, 0, 0, 0)),
            scratch_shapes=[pltpu.VMEM((steps, height, BLOCK), jnp.float32), pltpu.SemaphoreType.DMA],
        ),
        out_shape=jax.ShapeDtypeStruct((tiles.shape[0], steps, height, BLOCK // 2), jnp.float32),
        compiler_params=pltpu.CompilerParams(vmem_limit_bytes=48 * 1024 * 1024),
    )(tiles, slot, turns, wx, wy, src, rcv, *slabs)


def sweep_weights(xc, yc):
    xr, xi = xc[:, 0], xc[:, 1]
    yr, yi = jnp.swapaxes(yc[:, 0], 1, 2), jnp.swapaxes(yc[:, 1], 1, 2)
    join = lambda a, b, c, d: jnp.concatenate([jnp.concatenate([a, b], 2), jnp.concatenate([c, d], 2)], 1)
    return join(xr, xi, -xi, xr), join(yr, -yi, yi, yr)


AXES = ("freq", "shot")
YS = 4
XS = 4
CORES = 2


def pairs(mesh_shape, move):
    freq, shot = mesh_shape
    at = lambda zh, y, zl, x, c: ((zh * YS + y) * shot) + (zl * XS + x) * CORES + c
    out = []
    for zh in range(freq // YS):
        for y in range(YS):
            for zl in range(shot // (XS * CORES)):
                for x in range(XS):
                    for c in range(CORES):
                        out.append((at(zh, y, zl, x, c), at(*move(zh, y, zl, x, c))))
    return out


def place(blocks, axis, size):
    shape = list(blocks[0][1].shape)
    shape[axis] = size
    whole = jnp.zeros(shape, blocks[0][1].dtype)
    for index, block in blocks:
        whole = lax.dynamic_update_slice_in_dim(whole, block, index, axis)
    return whole


def local(
    source_field,
    receiver_field,
    angular_freq,
    x_correction,
    y_correction,
    velocity,
    slab_owner,
    apertures,
    tile_order,
):
    freqs_dev, shots = lax.axis_size("freq"), lax.axis_size("shot")
    freq_total = angular_freq.shape[0] * freqs_dev
    height, width = velocity.shape[1:]
    f_id, s_id = lax.axis_index("freq"), lax.axis_index("shot")
    zh, y = f_id // YS, f_id % YS
    zl, x, core = s_id // (XS * CORES), (s_id // CORES) % XS, s_id % CORES
    zhs, zls = freqs_dev // YS, shots // (XS * CORES)
    first = core == 0
    cols = width // (CORES * XS)
    rows = height // (zls * zhs * XS)
    send = lambda v, move: lax.ppermute(v, AXES, pairs((freqs_dev, shots), move))

    half = width // CORES
    slab = velocity[0].reshape(zls, zhs, XS, rows, width)
    slab = lax.dynamic_index_in_dim(slab, zh, 1, keepdims=False)
    to_first = lax.dynamic_slice_in_dim(slab, y * cols, cols, 3)
    to_second = lax.dynamic_index_in_dim(slab, y, 1, keepdims=False)[..., half:]
    to_second = jnp.swapaxes(to_second.reshape(zls, rows, XS, cols), 1, 2)
    outgoing = jnp.stack([to_first, to_second], axis=2).reshape(shots, rows, cols)
    arrived = lax.all_to_all(outgoing, "shot", 0, 0, tiled=True)
    mine = jnp.stack([lax.dynamic_index_in_dim(arrived, slab_owner[d], 0, keepdims=False) for d in range(DEPTH)])

    mine = mine[:, None]
    other = send(mine, lambda zh, y, zl, x, c: (zh, y, 1 - zl, x, c))
    mine = place([(zl, mine), (1 - zl, other)], 1, zls)[:, :, None]
    other = send(mine, lambda zh, y, zl, x, c: (1 - zh, y, zl, x, c))
    mine = place([(zh, mine), (1 - zh, other)], 2, zhs)[:, :, :, None]
    third = jnp.where(first, x, y)
    turn = lambda k: lambda zh, y, zl, x, c: (zh, y, zl, (x + k) % XS, c) if c == 0 else (zh, (y + k) % YS, zl, x, c)
    others = [((third + XS - k) % XS, send(mine, turn(k))) for k in (1, 3, 2)]
    own = place([(third, mine)] + others, 3, XS).reshape(DEPTH, height, cols)

    column = jnp.where(first, y, x)
    partner_column = jnp.where(first, x, y)
    shift = lambda k: lambda zh, y, zl, x, c: (zh, (y + k) % YS, zl, x, c) if c == 0 else (zh, y, zl, (x + k) % XS, c)
    swap = lambda zh, y, zl, x, c: (zh, y, zl, x, 1 - c)
    slabs, where = [], []
    for k in (0, 1, 3, 2):
        block = own if k == 0 else send(own, shift(k))
        slabs += [block, send(block, swap)]
        where += [core * XS + (column + XS - k) % XS, (1 - core) * XS + (partner_column + XS - k) % XS]

    wx, wy = sweep_weights(x_correction, y_correction)
    turns = angular_freq * (0.5 / math.pi)
    places = jnp.stack(where).astype(jnp.int32)
    fields = ()
    for k in range(0, len(slabs), 2):
        fields = march(
            places[k : k + 2], turns, jnp.stack(slabs[k : k + 2]), wx, wy, source_field, receiver_field, tuple(fields)
        )

    tiles = apertures[0]
    tile_width = width // (TILE_DEV * shots)
    held = (tiles * tile_width) // cols
    slot = jnp.argmax(places[None, :] == held[:, None], axis=1).astype(jnp.int32)
    terms = image_terms(tiles, slot, turns, wx, wy, source_field, receiver_field, slabs, 1.0 / freq_total)
    parts = terms.reshape(terms.shape[0], DEPTH, freqs_dev, -1)
    parts = lax.all_to_all(parts, "freq", 2, 2, tiled=True)
    summed = jnp.sum(parts, axis=2)
    match = (tile_order[:, None] == tiles[None, :]).astype(jnp.float32)
    dense = jnp.sum(match[:, :, None, None] * summed[None], axis=1)
    dense = lax.all_to_all(dense, "shot", 0, 0, tiled=True)
    image = jnp.sum(dense.reshape((shots, TILE_DEV) + dense.shape[1:]), axis=0)
    return (*fields, image)


def solution(mesh):
    in_specs = (
        P("freq", "shot", None, None, None),
        P("freq", "shot", None, None, None),
        P("freq"),
        P("freq", None, None, None),
        P("freq", None, None, None),
        P("shot", None, None),
        P(),
        P("shot", None),
        P(),
    )
    out_specs = (
        P("freq", "shot", None, None, None),
        P("freq", "shot", None, None, None),
        P("shot", None, "freq"),
    )
    return jax.shard_map(local, mesh=mesh, in_specs=in_specs, out_specs=out_specs, check_vma=False)
```

```python
import functools
import math

import jax
import jax.numpy as jnp
from jax import lax
from jax.experimental import pallas as pl
from jax.experimental.pallas import tpu as pltpu
from jax.sharding import PartitionSpec as P

DEPTH = 2
TILE_DEV = 4
BLOCK = 128
TILE = 512
VMEM = 48 * 1024 * 1024
SIN = (4.442867755889893, -7.307443618774414, 3.594788074493408, -0.7843739986419678)
COS = (1.4142135381698608, -6.978850841522217, 5.7394609451293945, -1.8835630416870117, 0.31069818139076233)


def poly(u, coefs):
    total = coefs[-1] * u + coefs[-2]
    for c in coefs[-3::-1]:
        total = total * u + c
    return total


def sincos(turns):
    r = turns - jnp.round(turns)
    u = r * r
    s = r * poly(u, SIN)
    c = poly(u, COS)
    return s * c, 1.0 - s * s


def quad(a, b, c, d):
    a, b, c, d = (v.astype(jnp.bfloat16) for v in (a, b, c, d))
    return jnp.concatenate([jnp.concatenate([a, b], 1), jnp.concatenate([c, d], 1)], 0)


def advance(parts, phases, wx, wy):
    freqs, blocks = len(parts), len(parts[0])
    height, width = parts[0][0][0].shape
    out = [[None] * blocks for _ in range(freqs)]
    for f in range(freqs):
        for b in range(blocks):
            sr, si, rr, ri = parts[f][b]
            sin, cos = sincos(phases[f][b])
            out[f][b] = (sr * cos - si * sin, sr * sin + si * cos, rr * cos - ri * sin, rr * sin + ri * cos)
    for f in range(freqs):
        left = jnp.concatenate([quad(*out[f][b]) for b in range(blocks)], 0)
        prod = jnp.dot(left, wx[f], preferred_element_type=jnp.float32)
        for b in range(blocks):
            x = prod[b * 2 * height : (b + 1) * 2 * height]
            sr, si, rr, ri = out[f][b]
            out[f][b] = (
                sr + x[:height, :width],
                si + x[:height, width:],
                rr + x[height:, :width],
                ri + x[height:, width:],
            )
    for f in range(freqs):
        right = jnp.concatenate([quad(v[0], v[2], v[1], v[3]) for v in out[f]], 1)
        prod = jnp.dot(wy[f], right, preferred_element_type=jnp.float32)
        for b in range(blocks):
            y = prod[:, b * 2 * width : (b + 1) * 2 * width]
            sr, si, rr, ri = out[f][b]
            out[f][b] = (
                sr + y[:height, :width],
                si + y[height:, :width],
                rr + y[:height, width:],
                ri + y[height:, width:],
            )
    return out


def load_parts(src, rcv, cols):
    f32 = jnp.float32
    return [
        [
            (
                src[f, 0, 0, :, c].astype(f32),
                src[f, 0, 1, :, c].astype(f32),
                rcv[f, 0, 0, :, c].astype(f32),
                -rcv[f, 0, 1, :, c].astype(f32),
            )
            for c in cols
        ]
        for f in range(src.shape[0])
    ]


def slab_view(slab, d, cols):
    rows = slab[:, d, :, cols]
    return rows.reshape(rows.shape[0] * rows.shape[1], rows.shape[2])


def march_body(where, turns, wx, wy, src, rcv, *rest, count, per):
    slabs, so, ro = rest[:count], rest[-2], rest[-1]
    freqs, tile = src.shape[0], src.shape[-1]
    cols = [slice(c, c + BLOCK) for c in range(0, tile, BLOCK)]
    i = pl.program_id(0)

    def run(slab, offset):
        parts = load_parts(src, rcv, cols)
        for d in range(slab.shape[1]):
            views = [slab_view(slab, d, slice(offset + c.start, offset + c.stop)) for c in cols]
            parts = advance(parts, [[v * turns[f] for v in views] for f in range(freqs)], wx, wy)
        for f in range(freqs):
            for b, c in enumerate(cols):
                sr, si, rr, ri = parts[f][b]
                so[f, 0, 0, :, c] = sr.astype(so.dtype)
                so[f, 0, 1, :, c] = si.astype(so.dtype)
                ro[f, 0, 0, :, c] = rr.astype(ro.dtype)
                ro[f, 0, 1, :, c] = (-ri).astype(ro.dtype)

    for k, slab in enumerate(slabs):
        for part in range(per):

            @pl.when(i == k * per + part)
            def _():
                run(slab, part * tile)


def march(where, turns, slabs, wx, wy, src, rcv, done=()):
    count, cols = len(slabs), slabs[0].shape[-1]
    freqs, height = src.shape[0], src.shape[3]
    tile = min(cols, TILE)
    per = cols // tile
    field = pl.BlockSpec((freqs, 1, 2, height, tile), lambda i, w: (0, 0, 0, 0, w[lax.div(i, per)] * per + lax.rem(i, per)))
    whole = lambda a: pl.BlockSpec(a.shape, lambda i, w: (0,) * a.ndim)
    args = [turns, wx, wy, src, rcv, *slabs]
    in_specs = [pl.BlockSpec(memory_space=pltpu.SMEM), whole(wx), whole(wy), field, field] + [whole(s) for s in slabs]
    alias = {len(args) + 1 + i: i for i in range(len(done))}
    cells = count * cols * height * freqs
    return pl.pallas_call(
        functools.partial(march_body, count=count, per=per),
        grid_spec=pltpu.PrefetchScalarGridSpec(
            num_scalar_prefetch=1,
            grid=(count * per,),
            in_specs=in_specs + [pl.BlockSpec(memory_space=pl.ANY)] * len(done),
            out_specs=[field, field],
        ),
        out_shape=[jax.ShapeDtypeStruct(src.shape, src.dtype), jax.ShapeDtypeStruct(rcv.shape, rcv.dtype)],
        input_output_aliases=alias,
        cost_estimate=pl.CostEstimate(
            flops=cells * DEPTH * 4 * 2 * 4 * BLOCK * 3, bytes_accessed=cells * 16, transcendentals=0
        ),
        compiler_params=pltpu.CompilerParams(vmem_limit_bytes=VMEM),
    )(where, *args, *done)


def image_body(tiles, slot, turns, wx, wy, *rest, scale, per, aper, count):
    fields, slabs, out, held, sems = rest[: 2 * aper], rest[2 * aper : -3], rest[-3], rest[-2], rest[-1]
    copies = []
    for a in range(aper):
        column = pl.multiple_of(lax.rem(lax.div(tiles[a], 2), per) * BLOCK, BLOCK)
        for k, slab in enumerate(slabs):

            @pl.when(slot[a] == k)
            def _():
                pltpu.make_async_copy(slab.at[:, :, :, pl.ds(column, BLOCK)], held.at[a], sems.at[a]).start()

    for a in range(aper):
        pltpu.make_async_copy(slabs[0].at[:, :, :, pl.ds(0, BLOCK)], held.at[a], sems.at[a]).wait()
    freqs = fields[0].shape[0]
    cols = [slice(0, BLOCK)]
    loaded = [load_parts(fields[2 * a], fields[2 * a + 1], cols) for a in range(aper)]
    parts = [[loaded[a][f][0] for a in range(aper)] for f in range(freqs)]
    half = BLOCK // 2
    for d in range(held.shape[2]):
        views = [slab_view(held.at[a], d, slice(0, BLOCK)) for a in range(aper)]
        parts = advance(parts, [[v * turns[f] for v in views] for f in range(freqs)], wx, wy)
        picked = []
        for a in range(aper):
            sr, si, rr, ri = parts[0][a]
            term = sr * rr - si * ri
            for f in range(1, freqs):
                sr, si, rr, ri = parts[f][a]
                term += sr * rr - si * ri
            odd = lax.rem(tiles[a], 2) == 1
            picked.append(jnp.where(odd, term[:, half:], term[:, :half]) * scale)
        both = jnp.concatenate(picked, 1)
        out[:, d] = both.reshape(count, both.shape[0] // count, both.shape[1])


def image_terms(tiles, slot, turns, wx, wy, src, rcv, slabs, scale, count):
    steps, cols = slabs[0].shape[1], slabs[0].shape[-1]
    freqs, height = src.shape[0], src.shape[3]
    aper = tiles.shape[0]
    whole = lambda a: pl.BlockSpec(a.shape, lambda i, t, s: (0,) * a.ndim)
    field = lambda a: pl.BlockSpec((freqs, 1, 2, height, BLOCK), lambda i, t, s: (0, 0, 0, 0, lax.div(t[a], 2)))
    lanes = aper * BLOCK // 2
    shape = (count, steps, height // count, lanes)
    return pl.pallas_call(
        functools.partial(image_body, scale=scale, per=cols // BLOCK, aper=aper, count=count),
        grid_spec=pltpu.PrefetchScalarGridSpec(
            num_scalar_prefetch=2,
            grid=(1,),
            in_specs=[pl.BlockSpec(memory_space=pltpu.SMEM), whole(wx), whole(wy)]
            + [field(a) for a in range(aper) for _ in range(2)]
            + [pl.BlockSpec(memory_space=pl.ANY)] * len(slabs),
            out_specs=pl.BlockSpec(shape, lambda i, t, s: (0, 0, 0, 0)),
            scratch_shapes=[
                pltpu.VMEM((aper,) + slabs[0].shape[:3] + (BLOCK,), jnp.float32),
                pltpu.SemaphoreType.DMA((aper,)),
            ],
        ),
        out_shape=jax.ShapeDtypeStruct(shape, jnp.float32),
        cost_estimate=pl.CostEstimate(
            flops=aper * BLOCK * height * freqs * steps * 4 * 2 * 4 * BLOCK * 3, bytes_accessed=1 << 21, transcendentals=0
        ),
        compiler_params=pltpu.CompilerParams(vmem_limit_bytes=VMEM),
    )(tiles, slot, turns, wx, wy, *[v for _ in range(aper) for v in (src, rcv)], *slabs)


def deal_body(tiles, order, parts, out, *, per):
    total = jnp.sum(parts[...], axis=0)
    half = BLOCK // 2
    swapped = jnp.concatenate([total[..., half:], total[..., :half]], -1)
    low = lax.broadcasted_iota(jnp.int32, total.shape, 2) < half
    zero = jnp.zeros_like(total)
    for j in range(out.shape[0]):
        for q in range(per // 2):
            p = j * per + 2 * q
            straight = (low & (order[p] == tiles[0])) | (~low & (order[p + 1] == tiles[1]))
            crossed = (low & (order[p] == tiles[1])) | (~low & (order[p + 1] == tiles[0]))
            out[j, :, :, q * BLOCK : (q + 1) * BLOCK] = jnp.where(straight, total, zero) + jnp.where(crossed, swapped, zero)


def deal(tiles, order, parts, shots):
    per = order.shape[0] // shots
    _, steps, lines, lanes = parts.shape
    return pl.pallas_call(
        functools.partial(deal_body, per=per),
        in_specs=[pl.BlockSpec(memory_space=pltpu.SMEM)] * 2 + [pl.BlockSpec(memory_space=pltpu.VMEM)],
        out_specs=pl.BlockSpec(memory_space=pltpu.VMEM),
        out_shape=jax.ShapeDtypeStruct((shots, steps, lines, per * BLOCK // 2), jnp.float32),
    )(tiles, order, parts)


def sweep_weights(xc, yc):
    xr, xi = xc[:, 0], xc[:, 1]
    yr, yi = jnp.swapaxes(yc[:, 0], 1, 2), jnp.swapaxes(yc[:, 1], 1, 2)
    join = lambda a, b, c, d: jnp.concatenate([jnp.concatenate([a, b], 2), jnp.concatenate([c, d], 2)], 1)
    return join(xr, xi, -xi, xr), join(yr, -yi, yi, yr)


AXES = ("freq", "shot")
YS = 4
XS = 4
CORES = 2


def pairs(mesh_shape, move):
    freq, shot = mesh_shape
    at = lambda zh, y, zl, x, c: ((zh * YS + y) * shot) + (zl * XS + x) * CORES + c
    out = []
    for zh in range(freq // YS):
        for y in range(YS):
            for zl in range(shot // (XS * CORES)):
                for x in range(XS):
                    for c in range(CORES):
                        out.append((at(zh, y, zl, x, c), at(*move(zh, y, zl, x, c))))
    return out


def row_groups(mesh_shape):
    freq, shot = mesh_shape
    zhs, zls = freq // YS, shot // (XS * CORES)
    at = lambda zh, y, zl, x, c: ((zh * YS + y) * shot) + (zl * XS + x) * CORES + c
    every = [(zl, zh) for zl in range(zls) for zh in range(zhs)]
    out = [[at(zh, y, zl, x, 0) for zl, zh in every for x in range(XS)] for y in range(YS)]
    return out + [[at(zh, y, zl, x, 1) for zl, zh in every for y in range(YS)] for x in range(XS)]


def local(
    source_field,
    receiver_field,
    angular_freq,
    x_correction,
    y_correction,
    velocity,
    slab_owner,
    apertures,
    tile_order,
):
    freqs_dev, shots = lax.axis_size("freq"), lax.axis_size("shot")
    freq_total = angular_freq.shape[0] * freqs_dev
    height, width = velocity.shape[1:]
    f_id, s_id = lax.axis_index("freq"), lax.axis_index("shot")
    zh, y = lax.div(f_id, YS), lax.rem(f_id, YS)
    zl, x, core = lax.div(s_id, XS * CORES), lax.rem(lax.div(s_id, CORES), XS), lax.rem(s_id, CORES)
    zhs, zls = freq // YS, shot // (XS * CORES)
    at = lambda zh, y, zl, x, c: ((zh * YS + y) * shot) + (zl * XS + x) * CORES + c
    every = [(zl, zh) for zl in range(zls) for zh in range(zhs)]
    out = [[at(zh, y, zl, x, 0) for zl, zh in every for x in range(XS)] for y in range(YS)]
    return out + [[at(zh, y, zl, x, 1) for zl, zh in every for y in range(YS)] for x in range(XS)]


def local(
    source_field,
    receiver_field,
    angular_freq,
    x_correction,
    y_correction,
    velocity,
    slab_owner,
    apertures,
    tile_order,
):
    freqs_dev, shots = lax.axis_size("freq"), lax.axis_size("shot")
    freq_total = angular_freq.shape[0] * freqs_dev
    height, width = velocity.shape[1:]
    f_id, s_id = lax.axis_index("freq"), lax.axis_index("shot")
    zh, y = f_id // YS, f_id % YS
    zl, x, core = s_id // (XS * CORES), (s_id // CORES) % XS, s_id % CORES
    zhs, zls = freqs_dev // YS, shots // (XS * CORES)
    first = core == 0
    cols = width // (CORES * XS)
    rows = height // (zls * zhs * XS)
    send = lambda v, move: lax.ppermute(v, AXES, pairs((freqs_dev, shots), move))

    half = width // CORES
    slab = velocity[0].reshape(zls, zhs, XS, rows, width)
    slab = lax.dynamic_index_in_dim(slab, zh, 1, keepdims=False)
    to_first = lax.dynamic_slice_in_dim(slab, y * cols, cols, 3)
    to_second = lax.dynamic_index_in_dim(slab, y, 1, keepdims=False)[..., half:]
    to_second = jnp.swapaxes(to_second.reshape(zls, rows, XS, cols), 1, 2)
    outgoing = jnp.stack([to_first, to_second], axis=2).reshape(shots, rows, cols)
    arrived = lax.all_to_all(outgoing, "shot", 0, 0, tiled=True)
    mine = jnp.stack([lax.dynamic_index_in_dim(arrived, slab_owner[d], 0, keepdims=False) for d in range(DEPTH)])

    groups = row_groups((freqs_dev, shots))
    members = len(groups[0])
    own = jnp.broadcast_to(mine[None], (members,) + mine.shape)
    own = lax.all_to_all(own, AXES, 0, 0, axis_index_groups=groups, tiled=True)

    column = jnp.where(first, y, x)
    partner_column = jnp.where(first, x, y)
    shift = lambda k: lambda zh, y, zl, x, c: (zh, (y + k) % YS, zl, x, c) if c == 0 else (zh, y, zl, (x + k) % XS, c)
    swap = lambda zh, y, zl, x, c: (zh, y, zl, x, 1 - c)
    place = lambda k: core * XS + lax.rem(column + XS - k, XS)
    partner_place = lambda k: (1 - core) * XS + lax.rem(partner_column + XS - k, XS)
    wx, wy = sweep_weights(x_correction, y_correction)
    turns = angular_freq * (0.5 / math.pi)
    src = pltpu.with_memory_space_constraint(source_field, pltpu.HBM)
    rcv = pltpu.with_memory_space_constraint(receiver_field, pltpu.HBM)

    def forward(places, slabs, done=()):
        return march(jnp.stack(places).astype(jnp.int32), turns, slabs, wx, wy, src, rcv, tuple(done))

    own_p = send(own, swap)
    s1, s3, s2 = (send(own, shift(k)) for k in (1, 3, 2))
    fields = forward([place(0), partner_place(0)], [own, own_p])
    s1, s3, *fields = lax.optimization_barrier((s1, s3, *fields))
    s1_p, s3_p = send(s1, swap), send(s3, swap)
    fields = forward([place(1), place(3)], [s1, s3], fields)
    s2, *fields = lax.optimization_barrier((s2, *fields))
    s2_p = send(s2, swap)
    fields = forward([partner_place(1)], [s1_p], fields)
    s2_p, s3_p, *fields = lax.optimization_barrier((s2_p, s3_p, *fields))

    tiles = apertures[0]
    held = lax.div(tiles * (width // (TILE_DEV * shots)), cols)
    slabs = [own, own_p, s1, s3, s2, s1_p, s3_p, s2_p]
    places = jnp.stack([place(0), partner_place(0), place(1), place(3), place(2)] + [partner_place(k) for k in (1, 3, 2)])
    slot = jnp.argmax(places[None, :] == held[:, None], axis=1).astype(jnp.int32)
    terms = image_terms(tiles, slot, turns, wx, wy, src, rcv, slabs, 1.0 / freq_total, freqs_dev)
    terms = lax.all_to_all(terms, "freq", 0, 0, tiled=True)
    fields = forward([partner_place(3), place(2)], [s3_p, s2], fields)
    terms, *fields = lax.optimization_barrier((terms, *fields))
    dense = lax.all_to_all(deal(tiles, tile_order, terms, shots), "shot", 0, 0, tiled=True)
    fields = forward([partner_place(2)], [s2_p], fields)
    image = jnp.sum(dense, axis=0)
    image = image.reshape(DEPTH, image.shape[1], TILE_DEV, -1)
    image = jnp.transpose(image, (2, 0, 1, 3)).reshape(TILE_DEV, DEPTH, -1)
    return (*fields, image)


def solution(mesh):
    in_specs = (
        P("freq", "shot", None, None, None),
        P("freq", "shot", None, None, None),
        P("freq"),
        P("freq", None, None, None),
        P("freq", None, None, None),
        P("shot", None, None),
        P(),
        P("shot", None),
        P(),
    )
    out_specs = (
        P("freq", "shot", None, None, None),
        P("freq", "shot", None, None, None),
        P("shot", None, "freq"),
    )
    return jax.shard_map(local, mesh=mesh, in_specs=in_specs, out_specs=out_specs, check_vma=False)
```

```python
import functools
import math

import jax
import jax.numpy as jnp
from jax import lax
from jax.experimental import pallas as pl
from jax.experimental.pallas import tpu as pltpu
from jax.sharding import PartitionSpec as P

DEPTH = 2
TILE_DEV = 4
BLOCK = 128
TILE = 512
VMEM = 24 * 1024 * 1024
SIN = (4.442867755889893, -7.307443618774414, 3.594788074493408, -0.7843739986419678)
COS = (1.4142135381698608, -6.978850841522217, 5.7394609451293945, -1.8835630416870117, 0.31069818139076233)


def poly(u, coefs):
    total = coefs[-1] * u + coefs[-2]
    for c in coefs[-3::-1]:
        total = total * u + c
    return total


def sincos(turns):
    r = turns - jnp.round(turns)
    u = r * r
    s = r * poly(u, SIN)
    c = poly(u, COS)
    return s * c, 1.0 - s * s


def quad(a, b, c, d):
    a, b, c, d = (v.astype(jnp.bfloat16) for v in (a, b, c, d))
    return jnp.concatenate([jnp.concatenate([a, b], 1), jnp.concatenate([c, d], 1)], 0)


def advance(parts, phases, wx, wy):
    freqs, blocks = len(parts), len(parts[0])
    height, width = parts[0][0][0].shape
    out = [[None] * blocks for _ in range(freqs)]
    for f in range(freqs):
        for b in range(blocks):
            sr, si, rr, ri = parts[f][b]
            sin, cos = sincos(phases[f][b])
            out[f][b] = (sr * cos - si * sin, sr * sin + si * cos, rr * cos - ri * sin, rr * sin + ri * cos)
    for f in range(freqs):
        left = jnp.concatenate([quad(*out[f][b]) for b in range(blocks)], 0)
        prod = jnp.dot(left, wx[f], preferred_element_type=jnp.float32)
        for b in range(blocks):
            x = prod[b * 2 * height : (b + 1) * 2 * height]
            sr, si, rr, ri = out[f][b]
            out[f][b] = (
                sr + x[:height, :width],
                si + x[:height, width:],
                rr + x[height:, :width],
                ri + x[height:, width:],
            )
    for f in range(freqs):
        right = jnp.concatenate([quad(v[0], v[2], v[1], v[3]) for v in out[f]], 1)
        prod = jnp.dot(wy[f], right, preferred_element_type=jnp.float32)
        for b in range(blocks):
            y = prod[:, b * 2 * width : (b + 1) * 2 * width]
            sr, si, rr, ri = out[f][b]
            out[f][b] = (
                sr + y[:height, :width],
                si + y[height:, :width],
                rr + y[:height, width:],
                ri + y[height:, width:],
            )
    return out


def load_parts(src, rcv, cols):
    f32 = jnp.float32
    return [
        [
            (
                src[f, 0, 0, :, c].astype(f32),
                src[f, 0, 1, :, c].astype(f32),
                rcv[f, 0, 0, :, c].astype(f32),
                -rcv[f, 0, 1, :, c].astype(f32),
            )
            for c in cols
        ]
        for f in range(src.shape[0])
    ]


def slab_view(slab, d, cols):
    rows = slab[:, d, :, cols]
    return rows.reshape(rows.shape[0] * rows.shape[1], rows.shape[2])


def march_body(where, turns, wx, wy, src, rcv, *rest, count, per):
    slabs, so, ro = rest[:count], rest[-2], rest[-1]
    freqs, tile = src.shape[0], src.shape[-1]
    cols = [slice(c, c + BLOCK) for c in range(0, tile, BLOCK)]
    i = pl.program_id(0)

    def run(slab, offset):
        parts = load_parts(src, rcv, cols)
        for d in range(slab.shape[1]):
            views = [slab_view(slab, d, slice(offset + c.start, offset + c.stop)) for c in cols]
            parts = advance(parts, [[v * turns[f] for v in views] for f in range(freqs)], wx, wy)
        for f in range(freqs):
            for b, c in enumerate(cols):
                sr, si, rr, ri = parts[f][b]
                so[f, 0, 0, :, c] = sr.astype(so.dtype)
                so[f, 0, 1, :, c] = si.astype(so.dtype)
                ro[f, 0, 0, :, c] = rr.astype(ro.dtype)
                ro[f, 0, 1, :, c] = (-ri).astype(ro.dtype)

    for k, slab in enumerate(slabs):
        for part in range(per):

            @pl.when(i == k * per + part)
            def _():
                run(slab, part * tile)


def march(where, turns, slabs, wx, wy, src, rcv, done=()):
    count, cols = len(slabs), slabs[0].shape[-1]
    freqs, height = src.shape[0], src.shape[3]
    tile = min(cols, TILE)
    per = cols // tile
    field = pl.BlockSpec((freqs, 1, 2, height, tile), lambda i, w: (0, 0, 0, 0, w[lax.div(i, per)] * per + lax.rem(i, per)))
    whole = lambda a: pl.BlockSpec(a.shape, lambda i, w: (0,) * a.ndim)
    args = [turns, wx, wy, src, rcv, *slabs]
    in_specs = [pl.BlockSpec(memory_space=pltpu.SMEM), whole(wx), whole(wy), field, field] + [whole(s) for s in slabs]
    alias = {len(args) + 1 + i: i for i in range(len(done))}
    cells = count * cols * height * freqs
    return pl.pallas_call(
        functools.partial(march_body, count=count, per=per),
        grid_spec=pltpu.PrefetchScalarGridSpec(
            num_scalar_prefetch=1,
            grid=(count * per,),
            in_specs=in_specs + [pl.BlockSpec(memory_space=pl.ANY)] * len(done),
            out_specs=[field, field],
        ),
        out_shape=[jax.ShapeDtypeStruct(src.shape, src.dtype), jax.ShapeDtypeStruct(rcv.shape, rcv.dtype)],
        input_output_aliases=alias,
        cost_estimate=pl.CostEstimate(
            flops=cells * DEPTH * 4 * 2 * 4 * BLOCK * 3, bytes_accessed=cells * 16, transcendentals=0
        ),
        compiler_params=pltpu.CompilerParams(vmem_limit_bytes=VMEM),
    )(where, *args, *done)


def image_body(tiles, slot, turns, wx, wy, *rest, scale, per, aper, count):
    fields, slabs = rest[: 2 * aper], rest[2 * aper : -4]
    out, held, lines, sems = rest[-4:]
    copies = []
    for a in range(aper):
        column = pl.multiple_of(lax.rem(lax.div(tiles[a], 2), per) * BLOCK, BLOCK)
        for k, slab in enumerate(slabs):

            @pl.when(slot[a] == k)
            def _():
                pltpu.make_async_copy(slab.at[:, :, :, pl.ds(column, BLOCK)], held.at[a], sems.at[a]).start()

    for a in range(aper):
        pltpu.make_async_copy(slabs[0].at[:, :, :, pl.ds(0, BLOCK)], held.at[a], sems.at[a]).wait()
    freqs = fields[0].shape[0]
    cols = [slice(0, BLOCK)]
    loaded = [load_parts(fields[2 * a], fields[2 * a + 1], cols) for a in range(aper)]
    parts = [[loaded[a][f][0] for a in range(aper)] for f in range(freqs)]
    half = BLOCK // 2
    for d in range(held.shape[2]):
        views = [slab_view(held.at[a], d, slice(0, BLOCK)) for a in range(aper)]
        parts = advance(parts, [[v * turns[f] for v in views] for f in range(freqs)], wx, wy)
        for a in range(aper):
            sr, si, rr, ri = parts[0][a]
            term = sr * rr - si * ri
            for f in range(1, freqs):
                sr, si, rr, ri = parts[f][a]
                term += sr * rr - si * ri
            odd = lax.rem(tiles[a], 2) == 1
            lines[a, :, :half] = jnp.where(odd, term[:, half:], term[:, :half]) * scale
            pairs_of = lines.shape[1] // 2
            even_odd = [lines[a, pl.ds(k, pairs_of, stride=2), :half] for k in range(2)]
            both = jnp.concatenate(even_odd, 1)
            out[:, a, d] = both.reshape(count, pairs_of // count, BLOCK)


def image_terms(tiles, slot, turns, wx, wy, src, rcv, slabs, scale, count):
    steps, cols = slabs[0].shape[1], slabs[0].shape[-1]
    freqs, height = src.shape[0], src.shape[3]
    aper = tiles.shape[0]
    whole = lambda a: pl.BlockSpec(a.shape, lambda i, t, s: (0,) * a.ndim)
    field = lambda a: pl.BlockSpec((freqs, 1, 2, height, BLOCK), lambda i, t, s: (0, 0, 0, 0, lax.div(t[a], 2)))
    shape = (count, aper, steps, height // 2 // count, BLOCK)
    return pl.pallas_call(
        functools.partial(image_body, scale=scale, per=cols // BLOCK, aper=aper, count=count),
        grid_spec=pltpu.PrefetchScalarGridSpec(
            num_scalar_prefetch=2,
            grid=(1,),
            in_specs=[pl.BlockSpec(memory_space=pltpu.SMEM), whole(wx), whole(wy)]
            + [field(a) for a in range(aper) for _ in range(2)]
            + [pl.BlockSpec(memory_space=pl.ANY)] * len(slabs),
            out_specs=pl.BlockSpec(shape, lambda i, t, s: (0,) * len(shape)),
            scratch_shapes=[
                pltpu.VMEM((aper,) + slabs[0].shape[:3] + (BLOCK,), jnp.float32),
                pltpu.VMEM((aper, height, BLOCK), jnp.float32),
                pltpu.SemaphoreType.DMA((aper,)),
            ],
        ),
        out_shape=jax.ShapeDtypeStruct(shape, jnp.float32),
        cost_estimate=pl.CostEstimate(
            flops=aper * BLOCK * height * freqs * steps * 4 * 2 * 4 * BLOCK * 3, bytes_accessed=1 << 21, transcendentals=0
        ),
        compiler_params=pltpu.CompilerParams(vmem_limit_bytes=VMEM),
    )(tiles, slot, turns, wx, wy, *[v for _ in range(aper) for v in (src, rcv)], *slabs)


def deal_body(tiles, parts, out):
    total = jnp.sum(parts[...], axis=0)
    ids = [jnp.full((1, BLOCK), tiles[a], jnp.int32).astype(jnp.float32) for a in range(tiles.shape[0])]
    spare = out.shape[1] - total.shape[0] - len(ids)
    total = jnp.concatenate([total] + ids + [jnp.zeros((spare, BLOCK), jnp.float32)], 0)
    for j in range(out.shape[0]):
        out[j] = total


def deal(tiles, parts, shots):
    rows = parts.shape[1] + 8
    return pl.pallas_call(
        deal_body,
        in_specs=[pl.BlockSpec(memory_space=pltpu.SMEM), pl.BlockSpec(memory_space=pltpu.VMEM)],
        out_specs=pl.BlockSpec(memory_space=pltpu.VMEM),
        out_shape=jax.ShapeDtypeStruct((shots, rows, BLOCK), jnp.float32),
    )(tiles, parts)


def collect_body(entries, parts, out, *, aper):
    steps = out.shape[1]
    rows = out.shape[2] // BLOCK
    size = steps * rows
    for p in range(out.shape[0]):
        total = jnp.zeros((size, BLOCK), jnp.float32)
        for s in range(parts.shape[0]):
            for a in range(aper):
                at = aper * size + a
                named = parts[s, at : at + 1].astype(jnp.int32) == entries[p]
                total += jnp.where(named, parts[s, a * size : (a + 1) * size], 0.0)
        for d in range(steps):
            for r in range(rows):
                out[p, d, r * BLOCK : (r + 1) * BLOCK] = total[d * rows + r]


def collect(entries, parts, aper, steps, length):
    return pl.pallas_call(
        functools.partial(collect_body, aper=aper),
        in_specs=[pl.BlockSpec(memory_space=pltpu.SMEM), pl.BlockSpec(memory_space=pltpu.VMEM)],
        out_specs=pl.BlockSpec(memory_space=pltpu.VMEM),
        out_shape=jax.ShapeDtypeStruct((entries.shape[0], steps, length), jnp.float32),
    )(entries, parts)


def cut_body(spot, slab, out, sems, *, cols):
    y = spot[0]
    xs = out.shape[1]
    copies = [
        pltpu.make_async_copy(
            slab.at[:, :, :, pl.ds(pl.multiple_of(y * cols, BLOCK), cols)], out.at[:, :, 0], sems.at[xs]
        )
    ]
    for x in range(xs):
        copies.append(
            pltpu.make_async_copy(slab.at[:, y, :, pl.ds((xs + x) * cols, cols)], out.at[:, x, 1], sems.at[x])
        )
    for c in copies:
        c.start()
    for c in copies:
        c.wait()


def cut(y, slab, cols):
    zls, xs, rows, _ = slab.shape
    return pl.pallas_call(
        functools.partial(cut_body, cols=cols),
        in_specs=[pl.BlockSpec(memory_space=pltpu.SMEM), pl.BlockSpec(memory_space=pltpu.HBM)],
        out_specs=pl.BlockSpec(memory_space=pltpu.HBM),
        out_shape=jax.ShapeDtypeStruct((zls, xs, CORES, rows, cols), slab.dtype),
        scratch_shapes=[pltpu.SemaphoreType.DMA((xs + 1,))],
    )(y, slab)


def sweep_weights(xc, yc):
    xr, xi = xc[:, 0], xc[:, 1]
    yr, yi = jnp.swapaxes(yc[:, 0], 1, 2), jnp.swapaxes(yc[:, 1], 1, 2)
    join = lambda a, b, c, d: jnp.concatenate([jnp.concatenate([a, b], 2), jnp.concatenate([c, d], 2)], 1)
    return join(xr, xi, -xi, xr), join(yr, -yi, yi, yr)


AXES = ("freq", "shot")
YS = 4
XS = 4
CORES = 2


def pairs(mesh_shape, move):
    freq, shot = mesh_shape
    at = lambda zh, y, zl, x, c: ((zh * YS + y) * shot) + (zl * XS + x) * CORES + c
    out = []
    for zh in range(freq // YS):
        for y in range(YS):
            for zl in range(shot // (XS * CORES)):
                for x in range(XS):
                    for c in range(CORES):
                        out.append((at(zh, y, zl, x, c), at(*move(zh, y, zl, x, c))))
    return out


def row_groups(mesh_shape):
    freq, shot = mesh_shape
    zhs, zls = freq // YS, shot // (XS * CORES)
    at = lambda zh, y, zl, x, c: ((zh * YS + y) * shot) + (zl * XS + x) * CORES + c
    out = [[at(zh, y, zl, x, 0) for zl in range(zls) for x in range(XS)] for zh in range(zhs) for y in range(YS)]
    return out + [[at(zh, y, zl, x, 1) for zl in range(zls) for y in range(YS)] for zh in range(zhs) for x in range(XS)]


def local(
    source_field,
    receiver_field,
    angular_freq,
    x_correction,
    y_correction,
    velocity,
    slab_owner,
    apertures,
    tile_order,
):
    freqs_dev, shots = lax.axis_size("freq"), lax.axis_size("shot")
    freq_total = angular_freq.shape[0] * freqs_dev
    height, width = velocity.shape[1:]
    f_id, s_id = lax.axis_index("freq"), lax.axis_index("shot")
    y = lax.rem(f_id, YS)
    zl, x, core = lax.div(s_id, XS * CORES), lax.rem(lax.div(s_id, CORES), XS), lax.rem(s_id, CORES)
    zhs, zls = freq // YS, shot // (XS * CORES)
    at = lambda zh, y, zl, x, c: ((zh * YS + y) * shot) + (zl * XS + x) * CORES + c
    every = [(zl, zh) for zl in range(zls) for zh in range(zhs)]
    out = [[at(zh, y, zl, x, 0) for zl, zh in every for x in range(XS)] for y in range(YS)]
    return out + [[at(zh, y, zl, x, 1) for zl, zh in every for y in range(YS)] for x in range(XS)]


def local(
    source_field,
    receiver_field,
    angular_freq,
    x_correction,
    y_correction,
    velocity,
    slab_owner,
    apertures,
    tile_order,
):
    freqs_dev, shots = lax.axis_size("freq"), lax.axis_size("shot")
    freq_total = angular_freq.shape[0] * freqs_dev
    height, width = velocity.shape[1:]
    f_id, s_id = lax.axis_index("freq"), lax.axis_index("shot")
    zh, y = f_id // YS, f_id % YS
    zl, x, core = s_id // (XS * CORES), (s_id // CORES) % XS, s_id % CORES
    zhs, zls = freqs_dev // YS, shots // (XS * CORES)
    first = core == 0
    cols = width // (CORES * XS)
    rows = height // (zls * XS)
    send = lambda v, move: lax.ppermute(v, AXES, pairs((freqs_dev, shots), move))

    outgoing = cut(y[None], velocity.reshape(zls, XS, rows, width), cols).reshape(shots, rows, cols)
    arrived = lax.all_to_all(outgoing, "shot", 0, 0, tiled=True)
    mine = jnp.stack([lax.dynamic_index_in_dim(arrived, slab_owner[d], 0, keepdims=False) for d in range(DEPTH)])

    groups = row_groups((freqs_dev, shots))
    members = len(groups[0])
    own = jnp.broadcast_to(mine[None], (members,) + mine.shape)
    own = lax.all_to_all(own, AXES, 0, 0, axis_index_groups=groups, tiled=True)

    column = jnp.where(first, y, x)
    partner_column = jnp.where(first, x, y)
    shift = lambda k: lambda zh, y, zl, x, c: (zh, (y + k) % YS, zl, x, c) if c == 0 else (zh, y, zl, (x + k) % XS, c)
    swap = lambda zh, y, zl, x, c: (zh, y, zl, x, 1 - c)
    place = lambda k: core * XS + lax.rem(column + XS - k, XS)
    partner_place = lambda k: (1 - core) * XS + lax.rem(partner_column + XS - k, XS)
    wx, wy = sweep_weights(x_correction, y_correction)
    turns = angular_freq * (0.5 / math.pi)
    src = pltpu.with_memory_space_constraint(source_field, pltpu.HBM)
    rcv = pltpu.with_memory_space_constraint(receiver_field, pltpu.HBM)

    def forward(places, slabs, done=()):
        return march(jnp.stack(places).astype(jnp.int32), turns, slabs, wx, wy, src, rcv, tuple(done))

    own_p = send(own, swap)
    s1, s3 = send(own, shift(1)), send(own, shift(3))
    later, own_p = lax.optimization_barrier((own, own_p))
    s2 = send(later, shift(2))
    fields = forward([place(0), partner_place(0)], [own, own_p])
    s1, s3, *fields = lax.optimization_barrier((s1, s3, *fields))
    s1_p, s3_p = send(s1, swap), send(s3, swap)
    fields = forward([place(1), place(3)], [s1, s3], fields)
    s2, *fields = lax.optimization_barrier((s2, *fields))
    s2_p = send(s2, swap)

    tiles = apertures[0]
    held = lax.div(tiles * (width // (TILE_DEV * shots)), cols)
    slabs = [own, own_p, s1, s3, s2, s1_p, s3_p, s2_p]
    places = jnp.stack([place(0), partner_place(0), place(1), place(3), place(2)] + [partner_place(k) for k in (1, 3, 2)])
    slot = jnp.argmax(places[None, :] == held[:, None], axis=1).astype(jnp.int32)
    terms = image_terms(tiles, slot, turns, wx, wy, src, rcv, slabs, 1.0 / freq_total, freqs_dev)
    length = terms.shape[3] * terms.shape[4]
    terms = lax.all_to_all(terms.reshape(freqs_dev, -1, BLOCK), "freq", 0, 0, tiled=True)
    fields = forward([partner_place(1), partner_place(3)], [s1_p, s3_p], fields)
    terms, *fields = lax.optimization_barrier((terms, *fields))
    dealt = lax.all_to_all(deal(tiles, terms, shots), "shot", 0, 0, tiled=True)
    fields = forward([place(2), partner_place(2)], [s2, s2_p], fields)
    entries = lax.dynamic_slice_in_dim(tile_order, s_id * TILE_DEV, TILE_DEV)
    image = collect(entries, dealt, tiles.shape[0], DEPTH, length)
    return (*fields, image)


def solution(mesh):
    in_specs = (
        P("freq", "shot", None, None, None),
        P("freq", "shot", None, None, None),
        P("freq"),
        P("freq", None, None, None),
        P("freq", None, None, None),
        P("shot", None, None),
        P(),
        P("shot", None),
        P(),
    )
    out_specs = (
        P("freq", "shot", None, None, None),
        P("freq", "shot", None, None, None),
        P("shot", None, "freq"),
    )
    return jax.shard_map(local, mesh=mesh, in_specs=in_specs, out_specs=out_specs, check_vma=False)
```

```python
import functools
import math

import jax
import jax.numpy as jnp
from jax import lax
from jax.experimental import pallas as pl
from jax.experimental.pallas import tpu as pltpu
from jax.sharding import PartitionSpec as P

DEPTH = 2
TILE_DEV = 4
BLOCK = 128
TILE = 512
VMEM = 24 * 1024 * 1024
NEAREST = 12582912.0
SIN = (4.442867755889893, -7.307443618774414, 3.594788074493408, -0.7843739986419678)
COS = (1.4142135381698608, -6.978850841522217, 5.7394609451293945, -1.8835630416870117, 0.31069818139076233)


def poly(u, coefs):
    total = coefs[-1] * u + coefs[-2]
    for c in coefs[-3::-1]:
        total = total * u + c
    return total


def sincos(turns):
    r = turns - ((turns + NEAREST) - NEAREST)
    u = r * r
    s = r * poly(u, SIN)
    c = poly(u, COS)
    return s * c, 1.0 - s * s


def rounded(parts):
    return tuple(v.astype(jnp.bfloat16) for v in parts)


def widened(parts):
    return tuple(v.astype(jnp.float32) for v in parts)


def quad(a, b, c, d):
    return jnp.concatenate([jnp.concatenate([a, b], 1), jnp.concatenate([c, d], 1)], 0)


def advance(parts, phases, wx, wy):
    freqs, blocks = len(parts), len(parts[0])
    height, width = parts[0][0][0].shape
    out = [[None] * blocks for _ in range(freqs)]
    for f in range(freqs):
        for b in range(blocks):
            sr, si, rr, ri = widened(parts[f][b])
            sin, cos = sincos(phases[f][b])
            out[f][b] = rounded(
                (sr * cos - si * sin, sr * sin + si * cos, rr * cos - ri * sin, rr * sin + ri * cos)
            )
    for f in range(freqs):
        left = jnp.concatenate([quad(*out[f][b]) for b in range(blocks)], 0)
        prod = jnp.dot(left, wx[f], preferred_element_type=jnp.float32)
        for b in range(blocks):
            x = prod[b * 2 * height : (b + 1) * 2 * height]
            sr, si, rr, ri = widened(out[f][b])
            out[f][b] = rounded(
                (
                    sr + x[:height, :width],
                    si + x[:height, width:],
                    rr + x[height:, :width],
                    ri + x[height:, width:],
                )
            )
    for f in range(freqs):
        right = jnp.concatenate([quad(v[0], v[2], v[1], v[3]) for v in out[f]], 1)
        prod = jnp.dot(wy[f], right, preferred_element_type=jnp.float32)
        for b in range(blocks):
            y = prod[:, b * 2 * width : (b + 1) * 2 * width]
            sr, si, rr, ri = widened(out[f][b])
            out[f][b] = (
                sr + y[:height, :width],
                si + y[height:, :width],
                rr + y[:height, width:],
                ri + y[height:, width:],
            )
    return out


def load_parts(src, rcv, starts):
    at = [pl.ds(pl.multiple_of(c, BLOCK), BLOCK) for c in starts]
    return [
        [(src[f, 0, 0, :, c], src[f, 0, 1, :, c], rcv[f, 0, 0, :, c], -rcv[f, 0, 1, :, c]) for c in at]
        for f in range(src.shape[0])
    ]


def slab_view(slab, d, cols):
    rows = slab[:, d, :, cols]
    return rows.reshape(rows.shape[0] * rows.shape[1], rows.shape[2])


def march_body(where, turns, wx, wy, src, rcv, *rest, count):
    slabs, so, ro = rest[:count], rest[-2], rest[-1]
    freqs, tile = src.shape[0], so.shape[-1]
    cols = [slice(c, c + BLOCK) for c in range(0, tile, BLOCK)]
    i = pl.program_id(0)

    def run(slab):
        parts = load_parts(src, rcv, [where[i] * tile + c.start for c in cols])
        for d in range(slab.shape[1]):
            views = [slab_view(slab, d, c) for c in cols]
            parts = advance(parts, [[v * turns[f] for v in views] for f in range(freqs)], wx, wy)
        for f in range(freqs):
            for b, c in enumerate(cols):
                sr, si, rr, ri = parts[f][b]
                so[f, 0, 0, :, c] = sr.astype(so.dtype)
                so[f, 0, 1, :, c] = si.astype(so.dtype)
                ro[f, 0, 0, :, c] = rr.astype(ro.dtype)
                ro[f, 0, 1, :, c] = (-ri).astype(ro.dtype)

    for k, slab in enumerate(slabs):

        @pl.when(i == k)
        def _():
            run(slab)


def march(where, turns, slabs, wx, wy, src, rcv, done=()):
    count, cols = len(slabs), slabs[0].shape[-1]
    freqs, height = src.shape[0], src.shape[3]
    field = pl.BlockSpec((freqs, 1, 2, height, cols), lambda i, w: (0, 0, 0, 0, w[i]))
    args = [turns, wx, wy, src, rcv, *slabs]
    in_specs = [pl.BlockSpec(memory_space=pltpu.SMEM)] + [pl.BlockSpec(memory_space=pltpu.VMEM)] * (len(args) - 1)
    alias = {len(args) + 1 + i: i for i in range(len(done))}
    cells = count * cols * height * freqs
    return pl.pallas_call(
        functools.partial(march_body, count=count),
        grid_spec=pltpu.PrefetchScalarGridSpec(
            num_scalar_prefetch=1,
            grid=(count,),
            in_specs=in_specs + [pl.BlockSpec(memory_space=pl.ANY)] * len(done),
            out_specs=[field, field],
        ),
        out_shape=[jax.ShapeDtypeStruct(src.shape, src.dtype), jax.ShapeDtypeStruct(rcv.shape, rcv.dtype)],
        input_output_aliases=alias,
        cost_estimate=pl.CostEstimate(
            flops=cells * DEPTH * 4 * 2 * 4 * BLOCK * 3, bytes_accessed=cells * 16, transcendentals=0
        ),
        compiler_params=pltpu.CompilerParams(vmem_limit_bytes=VMEM),
    )(where, *args, *done)


def image_body(tiles, slot, turns, wx, wy, src, rcv, *rest, scale, per, count):
    slabs, out, held, lines = rest[:-3], rest[-3], rest[-2], rest[-1]
    aper = tiles.shape[0]
    for a in range(aper):
        column = pl.multiple_of(lax.rem(lax.div(tiles[a], 2), per) * BLOCK, BLOCK)
        for k, slab in enumerate(slabs):

            @pl.when(slot[a] == k)
            def _():
                held[a] = slab[:, :, :, pl.ds(column, BLOCK)]

    freqs = src.shape[0]
    parts = load_parts(src, rcv, [lax.div(tiles[a], 2) * BLOCK for a in range(aper)])
    half = BLOCK // 2
    for d in range(held.shape[2]):
        views = [slab_view(held.at[a], d, slice(0, BLOCK)) for a in range(aper)]
        parts = advance(parts, [[v * turns[f] for v in views] for f in range(freqs)], wx, wy)
        for a in range(aper):
            sr, si, rr, ri = parts[0][a]
            term = sr * rr - si * ri
            for f in range(1, freqs):
                sr, si, rr, ri = parts[f][a]
                term += sr * rr - si * ri
            odd = lax.rem(tiles[a], 2) == 1
            lines[a, :, :half] = jnp.where(odd, term[:, half:], term[:, :half]) * scale
            pairs_of = lines.shape[1] // 2
            even_odd = [lines[a, pl.ds(k, pairs_of, stride=2), :half] for k in range(2)]
            both = jnp.concatenate(even_odd, 1)
            out[:, a, d] = both.reshape(count, pairs_of // count, BLOCK)


def image_terms(tiles, slot, turns, wx, wy, src, rcv, slabs, scale, count):
    steps, cols = slabs[0].shape[1], slabs[0].shape[-1]
    freqs, height = src.shape[0], src.shape[3]
    aper = tiles.shape[0]
    shape = (count, aper, steps, height // 2 // count, BLOCK)
    return pl.pallas_call(
        functools.partial(image_body, scale=scale, per=cols // BLOCK, count=count),
        in_specs=[pl.BlockSpec(memory_space=pltpu.SMEM)] * 3
        + [pl.BlockSpec(memory_space=pltpu.VMEM)] * (4 + len(slabs)),
        out_specs=pl.BlockSpec(memory_space=pltpu.VMEM),
        out_shape=jax.ShapeDtypeStruct(shape, jnp.float32),
        scratch_shapes=[
            pltpu.VMEM((aper,) + slabs[0].shape[:3] + (BLOCK,), jnp.float32),
            pltpu.VMEM((aper, height, BLOCK), jnp.float32),
        ],
        cost_estimate=pl.CostEstimate(
            flops=aper * BLOCK * height * freqs * steps * 4 * 2 * 4 * BLOCK * 3, bytes_accessed=1 << 21, transcendentals=0
        ),
        compiler_params=pltpu.CompilerParams(vmem_limit_bytes=VMEM),
    )(tiles, slot, turns, wx, wy, src, rcv, *slabs)


def deal_body(tiles, parts, out):
    total = jnp.sum(parts[...], axis=0)
    ids = [jnp.full((1, BLOCK), tiles[a], jnp.int32).astype(jnp.float32) for a in range(tiles.shape[0])]
    spare = out.shape[1] - total.shape[0] - len(ids)
    total = jnp.concatenate([total] + ids + [jnp.zeros((spare, BLOCK), jnp.float32)], 0)
    for j in range(out.shape[0]):
        out[j] = total


def deal(tiles, parts, shots):
    rows = parts.shape[1] + 8
    return pl.pallas_call(
        deal_body,
        in_specs=[pl.BlockSpec(memory_space=pltpu.SMEM), pl.BlockSpec(memory_space=pltpu.VMEM)],
        out_specs=pl.BlockSpec(memory_space=pltpu.VMEM),
        out_shape=jax.ShapeDtypeStruct((shots, rows, BLOCK), jnp.float32),
    )(tiles, parts)


def collect_body(entries, parts, out, *, aper):
    steps = out.shape[1]
    rows = out.shape[2] // BLOCK
    size = steps * rows
    for p in range(out.shape[0]):
        total = jnp.zeros((size, BLOCK), jnp.float32)
        for s in range(parts.shape[0]):
            for a in range(aper):
                at = aper * size + a
                named = parts[s, at : at + 1].astype(jnp.int32) == entries[p]
                total += jnp.where(named, parts[s, a * size : (a + 1) * size], 0.0)
        for d in range(steps):
            for r in range(rows):
                out[p, d, r * BLOCK : (r + 1) * BLOCK] = total[d * rows + r]


def collect(entries, parts, aper, steps, length):
    return pl.pallas_call(
        functools.partial(collect_body, aper=aper),
        in_specs=[pl.BlockSpec(memory_space=pltpu.SMEM), pl.BlockSpec(memory_space=pltpu.VMEM)],
        out_specs=pl.BlockSpec(memory_space=pltpu.VMEM),
        out_shape=jax.ShapeDtypeStruct((entries.shape[0], steps, length), jnp.float32),
    )(entries, parts)


def cut_body(spot, slab, out, sems, *, cols):
    y = spot[0]
    xs = out.shape[1]
    copies = [
        pltpu.make_async_copy(
            slab.at[:, :, :, pl.ds(pl.multiple_of(y * cols, BLOCK), cols)], out.at[:, :, 0], sems.at[xs]
        )
    ]
    for x in range(xs):
        copies.append(
            pltpu.make_async_copy(slab.at[:, y, :, pl.ds((xs + x) * cols, cols)], out.at[:, x, 1], sems.at[x])
        )
    for c in copies:
        c.start()
    for c in copies:
        c.wait()


def cut(y, slab, cols):
    zls, xs, rows, _ = slab.shape
    slab = pltpu.with_memory_space_constraint(slab, pltpu.HBM)
    return pl.pallas_call(
        functools.partial(cut_body, cols=cols),
        in_specs=[pl.BlockSpec(memory_space=pltpu.SMEM), pl.BlockSpec(memory_space=pltpu.HBM)],
        out_specs=pl.BlockSpec(memory_space=pltpu.VMEM),
        out_shape=jax.ShapeDtypeStruct((zls, xs, CORES, rows, cols), slab.dtype),
        scratch_shapes=[pltpu.SemaphoreType.DMA((xs + 1,))],
    )(y, slab)


def stage_body(*refs):
    count = len(refs) // 2
    sems = refs[-1]
    copies = [pltpu.make_async_copy(refs[i], refs[count + i], sems.at[i]) for i in range(count)]
    for c in copies:
        c.start()
    for c in copies:
        c.wait()


def stage(*arrays):
    arrays = [pltpu.with_memory_space_constraint(a, pltpu.HBM) for a in arrays]
    return pl.pallas_call(
        stage_body,
        in_specs=[pl.BlockSpec(memory_space=pltpu.HBM)] * len(arrays),
        out_specs=[pl.BlockSpec(memory_space=pltpu.VMEM)] * len(arrays),
        out_shape=[pltpu.VMEM(a.shape, a.dtype) for a in arrays],
        scratch_shapes=[pltpu.SemaphoreType.DMA((len(arrays),))],
        cost_estimate=pl.CostEstimate(
            flops=0, bytes_accessed=sum(2 * a.size * a.dtype.itemsize for a in arrays), transcendentals=0
        ),
        compiler_params=pltpu.CompilerParams(vmem_limit_bytes=VMEM),
    )(*arrays)


def sweep_weights(xc, yc):
    xr, xi = xc[:, 0], xc[:, 1]
    yr, yi = jnp.swapaxes(yc[:, 0], 1, 2), jnp.swapaxes(yc[:, 1], 1, 2)
    join = lambda a, b, c, d: jnp.concatenate([jnp.concatenate([a, b], 2), jnp.concatenate([c, d], 2)], 1)
    return join(xr, xi, -xi, xr), join(yr, -yi, yi, yr)


AXES = ("freq", "shot")
YS = 4
XS = 4
CORES = 2


def pairs(mesh_shape, move):
    freq, shot = mesh_shape
    at = lambda zh, y, zl, x, c: ((zh * YS + y) * shot) + (zl * XS + x) * CORES + c
    out = []
    for zh in range(freq // YS):
        for y in range(YS):
            for zl in range(shot // (XS * CORES)):
                for x in range(XS):
                    for c in range(CORES):
                        out.append((at(zh, y, zl, x, c), at(*move(zh, y, zl, x, c))))
    return out


def row_groups(mesh_shape):
    freq, shot = mesh_shape
    zhs, zls = freq // YS, shot // (XS * CORES)
    at = lambda zh, y, zl, x, c: ((zh * YS + y) * shot) + (zl * XS + x) * CORES + c
    out = [[at(zh, y, zl, x, 0) for zl in range(zls) for x in range(XS)] for zh in range(zhs) for y in range(YS)]
    return out + [[at(zh, y, zl, x, 1) for zl in range(zls) for y in range(YS)] for zh in range(zhs) for x in range(XS)]


def local(
    source_field,
    receiver_field,
    angular_freq,
    x_correction,
    y_correction,
    velocity,
    slab_owner,
    apertures,
    tile_order,
):
    freqs_dev, shots = lax.axis_size("freq"), lax.axis_size("shot")
    freq_total = angular_freq.shape[0] * freqs_dev
    height, width = velocity.shape[1:]
    f_id, s_id = lax.axis_index("freq"), lax.axis_index("shot")
    y = lax.rem(f_id, YS)
    zl, x, core = lax.div(s_id, XS * CORES), lax.rem(lax.div(s_id, CORES), XS), lax.rem(s_id, CORES)
    zhs, zls = freq // YS, shot // (XS * CORES)
    at = lambda zh, y, zl, x, c: ((zh * YS + y) * shot) + (zl * XS + x) * CORES + c
    every = [(zl, zh) for zl in range(zls) for zh in range(zhs)]
    out = [[at(zh, y, zl, x, 0) for zl, zh in every for x in range(XS)] for y in range(YS)]
    return out + [[at(zh, y, zl, x, 1) for zl, zh in every for y in range(YS)] for x in range(XS)]


def local(
    source_field,
    receiver_field,
    angular_freq,
    x_correction,
    y_correction,
    velocity,
    slab_owner,
    apertures,
    tile_order,
):
    freqs_dev, shots = lax.axis_size("freq"), lax.axis_size("shot")
    freq_total = angular_freq.shape[0] * freqs_dev
    height, width = velocity.shape[1:]
    f_id, s_id = lax.axis_index("freq"), lax.axis_index("shot")
    zh, y = f_id // YS, f_id % YS
    zl, x, core = s_id // (XS * CORES), (s_id // CORES) % XS, s_id % CORES
    zhs, zls = freqs_dev // YS, shots // (XS * CORES)
    first = core == 0
    cols = width // (CORES * XS)
    rows = height // (zls * XS)
    send = lambda v, move: lax.ppermute(v, AXES, pairs((freqs_dev, shots), move))

    outgoing = cut(y[None], velocity.reshape(zls, XS, rows, width), cols).reshape(shots, rows, cols)
    arrived = lax.all_to_all(outgoing, "shot", 0, 0, tiled=True)
    mine = jnp.stack([lax.dynamic_index_in_dim(arrived, slab_owner[d], 0, keepdims=False) for d in range(DEPTH)])

    groups = row_groups((freqs_dev, shots))
    members = len(groups[0])
    own = jnp.broadcast_to(mine[None], (members,) + mine.shape)
    own = lax.all_to_all(own, AXES, 0, 0, axis_index_groups=groups, tiled=True)

    column = jnp.where(first, y, x)
    partner_column = jnp.where(first, x, y)
    shift = lambda k: lambda zh, y, zl, x, c: (zh, (y + k) % YS, zl, x, c) if c == 0 else (zh, y, zl, (x + k) % XS, c)
    swap = lambda zh, y, zl, x, c: (zh, y, zl, x, 1 - c)
    place = lambda k: core * XS + lax.rem(column + XS - k, XS)
    partner_place = lambda k: (1 - core) * XS + lax.rem(partner_column + XS - k, XS)
    wx, wy = sweep_weights(x_correction, y_correction)
    turns = angular_freq * (0.5 / math.pi)
    src, rcv = stage(source_field, receiver_field)

    def forward(places, slabs, done=()):
        return march(jnp.stack(places).astype(jnp.int32), turns, slabs, wx, wy, src, rcv, tuple(done))

    own_p = send(own, swap)
    s1, s3 = send(own, shift(1)), send(own, shift(3))
    fields = forward([place(0), partner_place(0)], [own, own_p])
    s1, s3, later, *fields = lax.optimization_barrier((s1, s3, own, *fields))
    s2 = send(later, shift(2))
    s1_p, s3_p = send(s1, swap), send(s3, swap)
    fields = forward([place(1), place(3)], [s1, s3], fields)
    s2, *fields = lax.optimization_barrier((s2, *fields))
    s2_p = send(s2, swap)

    tiles = apertures[0]
    held = lax.div(tiles * (width // (TILE_DEV * shots)), cols)
    slabs = [own, own_p, s1, s3, s2, s1_p, s3_p, s2_p]
    places = jnp.stack([place(0), partner_place(0), place(1), place(3), place(2)] + [partner_place(k) for k in (1, 3, 2)])
    slot = jnp.argmax(places[None, :] == held[:, None], axis=1).astype(jnp.int32)
    terms = image_terms(tiles, slot, turns, wx, wy, src, rcv, slabs, 1.0 / freq_total, freqs_dev)
    length = terms.shape[3] * terms.shape[4]
    terms = lax.all_to_all(terms.reshape(freqs_dev, -1, BLOCK), "freq", 0, 0, tiled=True)
    fields = forward([partner_place(1), partner_place(3)], [s1_p, s3_p], fields)
    terms, *fields = lax.optimization_barrier((terms, *fields))
    dealt = lax.all_to_all(deal(tiles, terms, shots), "shot", 0, 0, tiled=True)
    fields = forward([place(2), partner_place(2)], [s2, s2_p], fields)
    entries = lax.dynamic_slice_in_dim(tile_order, s_id * TILE_DEV, TILE_DEV)
    image = collect(entries, dealt, tiles.shape[0], DEPTH, length)
    return (*fields, image)


def solution(mesh):
    in_specs = (
        P("freq", "shot", None, None, None),
        P("freq", "shot", None, None, None),
        P("freq"),
        P("freq", None, None, None),
        P("freq", None, None, None),
        P("shot", None, None),
        P(),
        P("shot", None),
        P(),
    )
    out_specs = (
        P("freq", "shot", None, None, None),
        P("freq", "shot", None, None, None),
        P("shot", None, "freq"),
    )
    return jax.shard_map(local, mesh=mesh, in_specs=in_specs, out_specs=out_specs, check_vma=False)
```

```python
import functools
import math

import jax
import jax.numpy as jnp
from jax import lax
from jax.experimental import pallas as pl
from jax.experimental.pallas import tpu as pltpu
from jax.sharding import PartitionSpec as P

DEPTH = 2
TILE_DEV = 4
BLOCK = 128
TILE = 512
VMEM = 24 * 1024 * 1024
NEAREST = 12582912.0
SIN = (4.442867755889893, -7.307443618774414, 3.594788074493408, -0.7843739986419678)
COS = (1.4142135381698608, -6.978850841522217, 5.7394609451293945, -1.8835630416870117, 0.31069818139076233)


def poly(u, coefs):
    total = coefs[-1] * u + coefs[-2]
    for c in coefs[-3::-1]:
        total = total * u + c
    return total


def sincos(turns):
    r = turns - ((turns + NEAREST) - NEAREST)
    u = r * r
    s = r * poly(u, SIN)
    c = poly(u, COS)
    return s * c, 1.0 - s * s


def rounded(parts):
    return tuple(v.astype(jnp.bfloat16) for v in parts)


def widened(parts):
    return tuple(v.astype(jnp.float32) for v in parts)


def quad(a, b, c, d):
    return jnp.concatenate([jnp.concatenate([a, b], 1), jnp.concatenate([c, d], 1)], 0)


def advance(parts, phases, wx, wy):
    freqs, blocks = len(parts), len(parts[0])
    height, width = parts[0][0][0].shape
    out = [[None] * blocks for _ in range(freqs)]
    for f in range(freqs):
        for b in range(blocks):
            sr, si, rr, ri = widened(parts[f][b])
            sin, cos = sincos(phases[f][b])
            out[f][b] = rounded(
                (sr * cos - si * sin, sr * sin + si * cos, rr * cos - ri * sin, rr * sin + ri * cos)
            )
    for f in range(freqs):
        left = jnp.concatenate([quad(*out[f][b]) for b in range(blocks)], 0)
        prod = jnp.dot(left, wx[f], preferred_element_type=jnp.float32)
        for b in range(blocks):
            x = prod[b * 2 * height : (b + 1) * 2 * height]
            sr, si, rr, ri = widened(out[f][b])
            out[f][b] = rounded(
                (
                    sr + x[:height, :width],
                    si + x[:height, width:],
                    rr + x[height:, :width],
                    ri + x[height:, width:],
                )
            )
    for f in range(freqs):
        right = jnp.concatenate([quad(v[0], v[2], v[1], v[3]) for v in out[f]], 1)
        prod = jnp.dot(wy[f], right, preferred_element_type=jnp.float32)
        for b in range(blocks):
            y = prod[:, b * 2 * width : (b + 1) * 2 * width]
            sr, si, rr, ri = widened(out[f][b])
            out[f][b] = (
                sr + y[:height, :width],
                si + y[height:, :width],
                rr + y[:height, width:],
                ri + y[height:, width:],
            )
    return out


def load_parts(src, rcv, starts):
    at = [slice(c, c + BLOCK) for c in starts]
    return [
        [(src[f, 0, 0, :, c], src[f, 0, 1, :, c], rcv[f, 0, 0, :, c], -rcv[f, 0, 1, :, c]) for c in at]
        for f in range(src.shape[0])
    ]


def slab_view(slab, d, cols):
    rows = slab[:, d, :, cols]
    return rows.reshape(rows.shape[0] * rows.shape[1], rows.shape[2])


def march_body(where, turns, wx, wy, src, rcv, *rest, count):
    slabs, so, ro = rest[:count], rest[-2], rest[-1]
    freqs, tile = src.shape[0], so.shape[-1]
    cols = [slice(c, c + BLOCK) for c in range(0, tile, BLOCK)]
    i = pl.program_id(0)

    def run(slab):
        parts = load_parts(src, rcv, [c.start for c in cols])
        for d in range(slab.shape[1]):
            views = [slab_view(slab, d, c) for c in cols]
            parts = advance(parts, [[v * turns[f] for v in views] for f in range(freqs)], wx, wy)
        for f in range(freqs):
            for b, c in enumerate(cols):
                sr, si, rr, ri = parts[f][b]
                so[f, 0, 0, :, c] = sr.astype(so.dtype)
                so[f, 0, 1, :, c] = si.astype(so.dtype)
                ro[f, 0, 0, :, c] = rr.astype(ro.dtype)
                ro[f, 0, 1, :, c] = (-ri).astype(ro.dtype)

    for k, slab in enumerate(slabs):

        @pl.when(i == k)
        def _():
            run(slab)


def march(where, turns, slabs, wx, wy, src, rcv, done=()):
    count, cols = len(slabs), slabs[0].shape[-1]
    freqs, height = src.shape[0], src.shape[3]
    field = pl.BlockSpec((freqs, 1, 2, height, cols), lambda i, w: (0, 0, 0, 0, w[i]))
    args = [turns, wx, wy, src, rcv, *slabs]
    vmem = pl.BlockSpec(memory_space=pltpu.VMEM)
    in_specs = [pl.BlockSpec(memory_space=pltpu.SMEM), vmem, vmem, field, field] + [vmem] * count
    alias = {len(args) + 1 + i: i for i in range(len(done))}
    cells = count * cols * height * freqs
    return pl.pallas_call(
        functools.partial(march_body, count=count),
        grid_spec=pltpu.PrefetchScalarGridSpec(
            num_scalar_prefetch=1,
            grid=(count,),
            in_specs=in_specs + [pl.BlockSpec(memory_space=pl.ANY)] * len(done),
            out_specs=[field, field],
        ),
        out_shape=[jax.ShapeDtypeStruct(src.shape, src.dtype), jax.ShapeDtypeStruct(rcv.shape, rcv.dtype)],
        input_output_aliases=alias,
        cost_estimate=pl.CostEstimate(
            flops=cells * DEPTH * 4 * 2 * 4 * BLOCK * 3, bytes_accessed=cells * 16, transcendentals=0
        ),
        compiler_params=pltpu.CompilerParams(vmem_limit_bytes=VMEM),
    )(where, *args, *done)


def image_body(tiles, slot, turns, wx, wy, *rest, scale, per, count):
    aper = tiles.shape[0]
    fields, slabs, out, held, lines = rest[: 2 * aper], rest[2 * aper : -3], rest[-3], rest[-2], rest[-1]
    for a in range(aper):
        column = pl.multiple_of(lax.rem(lax.div(tiles[a], 2), per) * BLOCK, BLOCK)
        for k, slab in enumerate(slabs):

            @pl.when(slot[a] == k)
            def _():
                held[a] = slab[:, :, :, pl.ds(column, BLOCK)]

    freqs = fields[0].shape[0]
    loaded = [load_parts(fields[2 * a], fields[2 * a + 1], [0]) for a in range(aper)]
    parts = [[loaded[a][f][0] for a in range(aper)] for f in range(freqs)]
    half = BLOCK // 2
    for d in range(held.shape[2]):
        views = [slab_view(held.at[a], d, slice(0, BLOCK)) for a in range(aper)]
        parts = advance(parts, [[v * turns[f] for v in views] for f in range(freqs)], wx, wy)
        for a in range(aper):
            sr, si, rr, ri = parts[0][a]
            term = sr * rr - si * ri
            for f in range(1, freqs):
                sr, si, rr, ri = parts[f][a]
                term += sr * rr - si * ri
            odd = lax.rem(tiles[a], 2) == 1
            lines[a, :, :half] = jnp.where(odd, term[:, half:], term[:, :half]) * scale
            pairs_of = lines.shape[1] // 2
            even_odd = [lines[a, pl.ds(k, pairs_of, stride=2), :half] for k in range(2)]
            both = jnp.concatenate(even_odd, 1)
            out[:, a, d] = both.reshape(count, pairs_of // count, BLOCK)


def image_terms(tiles, slot, turns, wx, wy, src, rcv, slabs, scale, count):
    steps, cols = slabs[0].shape[1], slabs[0].shape[-1]
    freqs, height = src.shape[0], src.shape[3]
    aper = tiles.shape[0]
    vmem = pl.BlockSpec(memory_space=pltpu.VMEM)
    field = lambda a: pl.BlockSpec((freqs, 1, 2, height, BLOCK), lambda i, t, s: (0, 0, 0, 0, lax.div(t[a], 2)))
    shape = (count, aper, steps, height // 2 // count, BLOCK)
    return pl.pallas_call(
        functools.partial(image_body, scale=scale, per=cols // BLOCK, count=count),
        grid_spec=pltpu.PrefetchScalarGridSpec(
            num_scalar_prefetch=2,
            grid=(1,),
            in_specs=[pl.BlockSpec(memory_space=pltpu.SMEM), vmem, vmem]
            + [field(a) for a in range(aper) for _ in range(2)]
            + [vmem] * len(slabs),
            out_specs=pl.BlockSpec(shape, lambda i, t, s: (0,) * len(shape)),
            scratch_shapes=[
                pltpu.VMEM((aper,) + slabs[0].shape[:3] + (BLOCK,), jnp.float32),
                pltpu.VMEM((aper, height, BLOCK), jnp.float32),
            ],
        ),
        out_shape=jax.ShapeDtypeStruct(shape, jnp.float32),
        cost_estimate=pl.CostEstimate(
            flops=aper * BLOCK * height * freqs * steps * 4 * 2 * 4 * BLOCK * 3, bytes_accessed=1 << 21, transcendentals=0
        ),
        compiler_params=pltpu.CompilerParams(vmem_limit_bytes=VMEM),
    )(tiles, slot, turns, wx, wy, *[v for _ in range(aper) for v in (src, rcv)], *slabs)


def deal_body(tiles, parts, out):
    total = jnp.sum(parts[...], axis=0)
    ids = [jnp.full((1, BLOCK), tiles[a], jnp.int32).astype(jnp.float32) for a in range(tiles.shape[0])]
    spare = out.shape[1] - total.shape[0] - len(ids)
    total = jnp.concatenate([total] + ids + [jnp.zeros((spare, BLOCK), jnp.float32)], 0)
    for j in range(out.shape[0]):
        out[j] = total


def deal(tiles, parts, shots):
    rows = parts.shape[1] + 8
    return pl.pallas_call(
        deal_body,
        in_specs=[pl.BlockSpec(memory_space=pltpu.SMEM), pl.BlockSpec(memory_space=pltpu.VMEM)],
        out_specs=pl.BlockSpec(memory_space=pltpu.VMEM),
        out_shape=jax.ShapeDtypeStruct((shots, rows, BLOCK), jnp.float32),
    )(tiles, pltpu.with_memory_space_constraint(parts, pltpu.VMEM))


def collect_body(entries, parts, out, *, aper):
    steps = out.shape[1]
    rows = out.shape[2] // BLOCK
    size = steps * rows
    for p in range(out.shape[0]):
        total = jnp.zeros((size, BLOCK), jnp.float32)
        for s in range(parts.shape[0]):
            for a in range(aper):
                at = aper * size + a
                named = parts[s, at : at + 1].astype(jnp.int32) == entries[p]
                total += jnp.where(named, parts[s, a * size : (a + 1) * size], 0.0)
        for d in range(steps):
            for r in range(rows):
                out[p, d, r * BLOCK : (r + 1) * BLOCK] = total[d * rows + r]


def collect(entries, parts, aper, steps, length):
    return pl.pallas_call(
        functools.partial(collect_body, aper=aper),
        in_specs=[pl.BlockSpec(memory_space=pltpu.SMEM), pl.BlockSpec(memory_space=pltpu.VMEM)],
        out_specs=pl.BlockSpec(memory_space=pltpu.VMEM),
        out_shape=jax.ShapeDtypeStruct((entries.shape[0], steps, length), jnp.float32),
    )(entries, pltpu.with_memory_space_constraint(parts, pltpu.VMEM))


def cut_body(spot, slab, out, sems, *, cols):
    y = spot[0]
    xs = out.shape[1]
    copies = [
        pltpu.make_async_copy(
            slab.at[:, :, :, pl.ds(pl.multiple_of(y * cols, BLOCK), cols)], out.at[:, :, 0], sems.at[xs]
        )
    ]
    for x in range(xs):
        copies.append(
            pltpu.make_async_copy(slab.at[:, y, :, pl.ds((xs + x) * cols, cols)], out.at[:, x, 1], sems.at[x])
        )
    for c in copies:
        c.start()
    for c in copies:
        c.wait()


def cut(y, slab, cols):
    zls, xs, rows, _ = slab.shape
    slab = pltpu.with_memory_space_constraint(slab, pltpu.HBM)
    return pl.pallas_call(
        functools.partial(cut_body, cols=cols),
        in_specs=[pl.BlockSpec(memory_space=pltpu.SMEM), pl.BlockSpec(memory_space=pltpu.HBM)],
        out_specs=pl.BlockSpec(memory_space=pltpu.VMEM),
        out_shape=jax.ShapeDtypeStruct((zls, xs, CORES, rows, cols), slab.dtype),
        scratch_shapes=[pltpu.SemaphoreType.DMA((xs + 1,))],
    )(y, slab)


def sweep_weights(xc, yc):
    xr, xi = xc[:, 0], xc[:, 1]
    yr, yi = jnp.swapaxes(yc[:, 0], 1, 2), jnp.swapaxes(yc[:, 1], 1, 2)
    join = lambda a, b, c, d: jnp.concatenate([jnp.concatenate([a, b], 2), jnp.concatenate([c, d], 2)], 1)
    return join(xr, xi, -xi, xr), join(yr, -yi, yi, yr)


AXES = ("freq", "shot")
YS = 4
XS = 4
CORES = 2


def pairs(mesh_shape, move):
    freq, shot = mesh_shape
    at = lambda zh, y, zl, x, c: ((zh * YS + y) * shot) + (zl * XS + x) * CORES + c
    out = []
    for zh in range(freq // YS):
        for y in range(YS):
            for zl in range(shot // (XS * CORES)):
                for x in range(XS):
                    for c in range(CORES):
                        out.append((at(zh, y, zl, x, c), at(*move(zh, y, zl, x, c))))
    return out


def row_groups(mesh_shape):
    freq, shot = mesh_shape
    zhs, zls = freq // YS, shot // (XS * CORES)
    at = lambda zh, y, zl, x, c: ((zh * YS + y) * shot) + (zl * XS + x) * CORES + c
    out = [[at(zh, y, zl, x, 0) for zl in range(zls) for x in range(XS)] for zh in range(zhs) for y in range(YS)]
    return out + [[at(zh, y, zl, x, 1) for zl in range(zls) for y in range(YS)] for zh in range(zhs) for x in range(XS)]


def local(
    source_field,
    receiver_field,
    angular_freq,
    x_correction,
    y_correction,
    velocity,
    slab_owner,
    apertures,
    tile_order,
):
    freqs_dev, shots = lax.axis_size("freq"), lax.axis_size("shot")
    freq_total = angular_freq.shape[0] * freqs_dev
    height, width = velocity.shape[1:]
    f_id, s_id = lax.axis_index("freq"), lax.axis_index("shot")
    y = lax.rem(f_id, YS)
    zl, x, core = lax.div(s_id, XS * CORES), lax.rem(lax.div(s_id, CORES), XS), lax.rem(s_id, CORES)
    zhs, zls = freq // YS, shot // (XS * CORES)
    at = lambda zh, y, zl, x, c: ((zh * YS + y) * shot) + (zl * XS + x) * CORES + c
    every = [(zl, zh) for zl in range(zls) for zh in range(zhs)]
    out = [[at(zh, y, zl, x, 0) for zl, zh in every for x in range(XS)] for y in range(YS)]
    return out + [[at(zh, y, zl, x, 1) for zl, zh in every for y in range(YS)] for x in range(XS)]


def local(
    source_field,
    receiver_field,
    angular_freq,
    x_correction,
    y_correction,
    velocity,
    slab_owner,
    apertures,
    tile_order,
):
    freqs_dev, shots = lax.axis_size("freq"), lax.axis_size("shot")
    freq_total = angular_freq.shape[0] * freqs_dev
    height, width = velocity.shape[1:]
    f_id, s_id = lax.axis_index("freq"), lax.axis_index("shot")
    zh, y = f_id // YS, f_id % YS
    zl, x, core = s_id // (XS * CORES), (s_id // CORES) % XS, s_id % CORES
    zhs, zls = freqs_dev // YS, shots // (XS * CORES)
    first = core == 0
    cols = width // (CORES * XS)
    rows = height // (zls * XS)
    send = lambda v, move: lax.ppermute(v, AXES, pairs((freqs_dev, shots), move))

    outgoing = cut(y[None], velocity.reshape(zls, XS, rows, width), cols).reshape(shots, rows, cols)
    arrived = lax.all_to_all(outgoing, "shot", 0, 0, tiled=True)
    mine = jnp.stack([lax.dynamic_index_in_dim(arrived, slab_owner[d], 0, keepdims=False) for d in range(DEPTH)])

    groups = row_groups((freqs_dev, shots))
    members = len(groups[0])
    own = jnp.broadcast_to(mine[None], (members,) + mine.shape)
    own = lax.all_to_all(own, AXES, 0, 0, axis_index_groups=groups, tiled=True)

    column = jnp.where(first, y, x)
    partner_column = jnp.where(first, x, y)
    shift = lambda k: lambda zh, y, zl, x, c: (zh, (y + k) % YS, zl, x, c) if c == 0 else (zh, y, zl, (x + k) % XS, c)
    swap = lambda zh, y, zl, x, c: (zh, y, zl, x, 1 - c)
    place = lambda k: core * XS + lax.rem(column + XS - k, XS)
    partner_place = lambda k: (1 - core) * XS + lax.rem(partner_column + XS - k, XS)
    wx, wy = sweep_weights(x_correction, y_correction)
    turns = angular_freq * (0.5 / math.pi)
    src = pltpu.with_memory_space_constraint(source_field, pltpu.HBM)
    rcv = pltpu.with_memory_space_constraint(receiver_field, pltpu.HBM)

    def forward(places, slabs, done=()):
        return march(jnp.stack(places).astype(jnp.int32), turns, slabs, wx, wy, src, rcv, tuple(done))

    own_p = send(own, swap)
    s1, s3 = send(own, shift(1)), send(own, shift(3))
    fields = forward([place(0), partner_place(0)], [own, own_p])
    s1, s3, later, *fields = lax.optimization_barrier((s1, s3, own, *fields))
    s2 = send(later, shift(2))
    s1_p, s3_p = send(s1, swap), send(s3, swap)
    fields = forward([place(1), place(3)], [s1, s3], fields)
    s2, *fields = lax.optimization_barrier((s2, *fields))
    s2_p = send(s2, swap)

    tiles = apertures[0]
    held = lax.div(tiles * (width // (TILE_DEV * shots)), cols)
    slabs = [own, own_p, s1, s3, s2, s1_p, s3_p, s2_p]
    places = jnp.stack([place(0), partner_place(0), place(1), place(3), place(2)] + [partner_place(k) for k in (1, 3, 2)])
    slot = jnp.argmax(places[None, :] == held[:, None], axis=1).astype(jnp.int32)
    terms = image_terms(tiles, slot, turns, wx, wy, src, rcv, slabs, 1.0 / freq_total, freqs_dev)
    length = terms.shape[3] * terms.shape[4]
    terms = lax.all_to_all(terms.reshape(freqs_dev, -1, BLOCK), "freq", 0, 0, tiled=True)
    fields = forward([partner_place(1), partner_place(3)], [s1_p, s3_p], fields)
    terms, *fields = lax.optimization_barrier((terms, *fields))
    dealt = lax.all_to_all(deal(tiles, terms, shots), "shot", 0, 0, tiled=True)
    fields = forward([place(2), partner_place(2)], [s2, s2_p], fields)
    entries = lax.dynamic_slice_in_dim(tile_order, s_id * TILE_DEV, TILE_DEV)
    image = collect(entries, dealt, tiles.shape[0], DEPTH, length)
    return (*fields, image)


def solution(mesh):
    in_specs = (
        P("freq", "shot", None, None, None),
        P("freq", "shot", None, None, None),
        P("freq"),
        P("freq", None, None, None),
        P("freq", None, None, None),
        P("shot", None, None),
        P(),
        P("shot", None),
        P(),
    )
    out_specs = (
        P("freq", "shot", None, None, None),
        P("freq", "shot", None, None, None),
        P("shot", None, "freq"),
    )
    return jax.shard_map(local, mesh=mesh, in_specs=in_specs, out_specs=out_specs, check_vma=False)
```

```python
import functools
import math

import jax
import jax.numpy as jnp
from jax import lax
from jax.experimental import pallas as pl
from jax.experimental.pallas import tpu as pltpu
from jax.sharding import PartitionSpec as P

DEPTH = 2
TILE_DEV = 4
BLOCK = 128
TILE = 512
VMEM = 24 * 1024 * 1024
NEAREST = 12582912.0
SIN = (4.442867755889893, -7.307443618774414, 3.594788074493408, -0.7843739986419678)
COS = (1.4142135381698608, -6.978850841522217, 5.7394609451293945, -1.8835630416870117, 0.31069818139076233)


def poly(u, coefs):
    total = coefs[-1] * u + coefs[-2]
    for c in coefs[-3::-1]:
        total = total * u + c
    return total


def sincos(turns):
    r = turns - ((turns + NEAREST) - NEAREST)
    u = r * r
    s = r * poly(u, SIN)
    c = poly(u, COS)
    return s * c, 1.0 - s * s


def rounded(parts):
    return tuple(v.astype(jnp.bfloat16) for v in parts)


def widened(parts):
    return tuple(v.astype(jnp.float32) for v in parts)


def quad(a, b, c, d):
    return jnp.concatenate([jnp.concatenate([a, b], 1), jnp.concatenate([c, d], 1)], 0)


def advance(parts, phases, wx, wy):
    height, width = parts[0][0].shape
    out = []
    for part, phase in zip(parts, phases):
        sr, si, rr, ri = widened(part)
        sin, cos = sincos(phase)
        out.append(rounded((sr * cos - si * sin, sr * sin + si * cos, rr * cos - ri * sin, rr * sin + ri * cos)))
    prod = jnp.dot(jnp.concatenate([quad(*v) for v in out], 0), wx, preferred_element_type=jnp.float32)
    for b, (sr, si, rr, ri) in enumerate(out):
        x = prod[b * 2 * height : (b + 1) * 2 * height]
        x = rounded((x[:height, :width], x[:height, width:], x[height:, :width], x[height:, width:]))
        out[b] = (sr + x[0], si + x[1], rr + x[2], ri + x[3])
    right = jnp.concatenate([quad(v[0], v[2], v[1], v[3]) for v in out], 1)
    prod = jnp.dot(wy, right, preferred_element_type=jnp.float32)
    for b, part in enumerate(out):
        y = prod[:, b * 2 * width : (b + 1) * 2 * width]
        sr, si, rr, ri = widened(part)
        out[b] = (
            sr + y[:height, :width],
            si + y[height:, :width],
            rr + y[:height, width:],
            ri + y[height:, width:],
        )
    return out


def slab_view(slab, d, cols):
    rows = slab[:, d, :, cols]
    return rows.reshape(rows.shape[0] * rows.shape[1], rows.shape[2])


def fetch_body(blocks, tiles, src, rcv, *rest, steps, cols):
    firsts, wanted, sems = rest[:steps], rest[steps], rest[steps + 1]
    copies = []

    def copy(source, target):
        copies.append(pltpu.make_async_copy(source, target, sems.at[len(copies)]))

    for k in range(steps):
        at = pl.ds(pl.multiple_of(blocks[k] * cols, BLOCK), cols)
        for i, field in enumerate((src, rcv)):
            copy(field.at[0, 0, :, :, at], firsts[k].at[i])
    for a in range(wanted.shape[0]):
        at = pl.ds(pl.multiple_of(lax.div(tiles[a], 2) * BLOCK, BLOCK), BLOCK)
        for i, field in enumerate((src, rcv)):
            copy(field.at[:, 0, :, :, at], wanted.at[a, i])
    for c in copies:
        c.start()
    for c in copies:
        c.wait()


def fetch(blocks, tiles, src, rcv, cols):
    steps, aper = blocks.shape[0], tiles.shape[0]
    freqs, _, _, height, _ = src.shape
    shapes = [(2, 2, height, cols)] * steps + [(aper, 2, freqs, 2, height, BLOCK)]
    vmem = pl.BlockSpec(memory_space=pltpu.VMEM)
    out = pl.pallas_call(
        functools.partial(fetch_body, steps=steps, cols=cols),
        in_specs=[pl.BlockSpec(memory_space=pltpu.SMEM)] * 2 + [pl.BlockSpec(memory_space=pltpu.HBM)] * 2,
        out_specs=[vmem] * len(shapes),
        out_shape=[pltpu.VMEM(s, src.dtype) for s in shapes],
        scratch_shapes=[pltpu.SemaphoreType.DMA((2 * (steps + aper),))],
        cost_estimate=pl.CostEstimate(flops=0, bytes_accessed=1 << 23, transcendentals=0),
        compiler_params=pltpu.CompilerParams(vmem_limit_bytes=VMEM),
    )(blocks, tiles, src, rcv)
    return out[:-1], out[-1]


def march_body(where, turns, wx, wy, first, src, rcv, *rest, count, freqs):
    slabs, (so, ro, held, sems) = rest[:count], rest[-4:]
    tile = so.shape[-1]
    cols = [slice(c, c + BLOCK) for c in range(0, tile, BLOCK)]
    unit = pl.program_id(0)
    block, f = lax.div(unit, freqs), lax.rem(unit, freqs)

    def copies(u):
        at = pl.ds(pl.multiple_of(where[lax.div(u, freqs)] * tile, BLOCK), tile)
        slot = lax.rem(u, 2)
        return [
            pltpu.make_async_copy(field.at[lax.rem(u, freqs), 0, :, :, at], held.at[slot, i], sems.at[slot, i])
            for i, field in enumerate((src, rcv))
        ]

    @pl.when(unit + 1 < count * freqs)
    def _():
        for c in copies(unit + 1):
            c.start()

    @pl.when(unit == 0)
    def _():
        held[0] = first[...]

    @pl.when(unit > 0)
    def _():
        for c in copies(unit):
            c.wait()

    slot = lax.rem(unit, 2)

    def run(slab):
        parts = [
            (held[slot, 0, 0, :, c], held[slot, 0, 1, :, c], held[slot, 1, 0, :, c], -held[slot, 1, 1, :, c])
            for c in cols
        ]
        for d in range(slab.shape[1]):
            parts = advance(parts, [slab_view(slab, d, c) * turns[f] for c in cols], wx[f], wy[f])
        for (sr, si, rr, ri), c in zip(parts, cols):
            so[0, 0, 0, :, c] = sr.astype(so.dtype)
            so[0, 0, 1, :, c] = si.astype(so.dtype)
            ro[0, 0, 0, :, c] = rr.astype(ro.dtype)
            ro[0, 0, 1, :, c] = (-ri).astype(ro.dtype)

    for k, slab in enumerate(slabs):

        @pl.when(block == k)
        def _():
            run(slab)


def march(where, turns, slabs, wx, wy, first, src, rcv, done=()):
    count, cols = len(slabs), slabs[0].shape[-1]
    freqs, height = src.shape[0], src.shape[3]
    vmem, hbm = pl.BlockSpec(memory_space=pltpu.VMEM), pl.BlockSpec(memory_space=pltpu.HBM)
    field = pl.BlockSpec(
        (1, 1, 2, height, cols), lambda u, w: (lax.rem(u, freqs), 0, 0, 0, w[lax.div(u, freqs)])
    )
    args = [turns, wx, wy, first, src, rcv, *slabs]
    in_specs = [pl.BlockSpec(memory_space=pltpu.SMEM), vmem, vmem, vmem, hbm, hbm] + [vmem] * count
    alias = {len(args) + 1 + i: i for i in range(len(done))}
    cells = count * cols * height * freqs
    return pl.pallas_call(
        functools.partial(march_body, count=count, freqs=freqs),
        grid_spec=pltpu.PrefetchScalarGridSpec(
            num_scalar_prefetch=1,
            grid=(count * freqs,),
            in_specs=in_specs + [pl.BlockSpec(memory_space=pl.ANY)] * len(done),
            out_specs=[field, field],
            scratch_shapes=[
                pltpu.VMEM((2, 2, 2, height, cols), src.dtype),
                pltpu.SemaphoreType.DMA((2, 2)),
            ],
        ),
        out_shape=[jax.ShapeDtypeStruct(src.shape, src.dtype), jax.ShapeDtypeStruct(rcv.shape, rcv.dtype)],
        input_output_aliases=alias,
        cost_estimate=pl.CostEstimate(
            flops=cells * DEPTH * 4 * 2 * 4 * BLOCK * 3, bytes_accessed=cells * 16, transcendentals=0
        ),
        compiler_params=pltpu.CompilerParams(vmem_limit_bytes=VMEM),
    )(where, *args, *done)


def image_body(tiles, places, turns, wx, wy, wanted, *rest, scale, per, count):
    slabs, out, held, lines = rest[:-3], rest[-3], rest[-2], rest[-1]
    aper = tiles.shape[0]
    for a in range(aper):
        x_block = lax.div(tiles[a], 2)
        column = pl.multiple_of(lax.rem(x_block, per) * BLOCK, BLOCK)
        for k, slab in enumerate(slabs):

            @pl.when(places[k] == lax.div(x_block, per))
            def _():
                held[a] = slab[:, :, :, pl.ds(column, BLOCK)]

    freqs = wanted.shape[2]
    parts = [
        [(wanted[a, 0, f, 0], wanted[a, 0, f, 1], wanted[a, 1, f, 0], -wanted[a, 1, f, 1]) for a in range(aper)]
        for f in range(freqs)
    ]
    half = BLOCK // 2
    for d in range(held.shape[2]):
        views = [slab_view(held.at[a], d, slice(0, BLOCK)) for a in range(aper)]
        parts = [advance(parts[f], [v * turns[f] for v in views], wx[f], wy[f]) for f in range(freqs)]
        for a in range(aper):
            term = sum(sr * rr - si * ri for sr, si, rr, ri in (widened(rounded(p[a])) for p in parts))
            odd = lax.rem(tiles[a], 2) == 1
            lines[a, :, :half] = jnp.where(odd, term[:, half:], term[:, :half]) * scale
            pairs_of = lines.shape[1] // 2
            even_odd = [lines[a, pl.ds(k, pairs_of, stride=2), :half] for k in range(2)]
            both = jnp.concatenate(even_odd, 1)
            out[:, a, d] = both.reshape(count, pairs_of // count, BLOCK)


def image_terms(tiles, places, turns, wx, wy, wanted, slabs, scale, count):
    steps, cols = slabs[0].shape[1], slabs[0].shape[-1]
    aper, _, freqs, _, height, _ = wanted.shape
    smem, vmem = pl.BlockSpec(memory_space=pltpu.SMEM), pl.BlockSpec(memory_space=pltpu.VMEM)
    shape = (count, aper, steps, height // 2 // count, BLOCK)
    return pl.pallas_call(
        functools.partial(image_body, scale=scale, per=cols // BLOCK, count=count),
        in_specs=[smem] * 3 + [vmem] * (3 + len(slabs)),
        out_specs=vmem,
        out_shape=jax.ShapeDtypeStruct(shape, jnp.float32),
        scratch_shapes=[
            pltpu.VMEM((aper,) + slabs[0].shape[:3] + (BLOCK,), jnp.float32),
            pltpu.VMEM((aper, height, BLOCK), jnp.float32),
        ],
        cost_estimate=pl.CostEstimate(
            flops=aper * BLOCK * height * freqs * steps * 4 * 2 * 4 * BLOCK * 3, bytes_accessed=1 << 21, transcendentals=0
        ),
        compiler_params=pltpu.CompilerParams(vmem_limit_bytes=VMEM),
    )(tiles, places, turns, wx, wy, wanted, *slabs)


def deal_body(tiles, parts, out):
    total = jnp.sum(parts[...], axis=0)
    ids = [jnp.full((1, BLOCK), tiles[a], jnp.int32).astype(jnp.float32) for a in range(tiles.shape[0])]
    spare = out.shape[1] - total.shape[0] - len(ids)
    total = jnp.concatenate([total] + ids + [jnp.zeros((spare, BLOCK), jnp.float32)], 0)
    for j in range(out.shape[0]):
        out[j] = total


def deal(tiles, parts, shots):
    rows = parts.shape[1] + 8
    return pl.pallas_call(
        deal_body,
        in_specs=[pl.BlockSpec(memory_space=pltpu.SMEM), pl.BlockSpec(memory_space=pltpu.VMEM)],
        out_specs=pl.BlockSpec(memory_space=pltpu.VMEM),
        out_shape=jax.ShapeDtypeStruct((shots, rows, BLOCK), jnp.float32),
        compiler_params=pltpu.CompilerParams(vmem_limit_bytes=VMEM),
    )(tiles, pltpu.with_memory_space_constraint(parts, pltpu.VMEM))


def collect_body(entries, parts, out, *, aper):
    steps = out.shape[1]
    rows = out.shape[2] // BLOCK
    size = steps * rows
    for p in range(out.shape[0]):
        total = jnp.zeros((size, BLOCK), jnp.float32)
        for s in range(parts.shape[0]):
            for a in range(aper):
                at = aper * size + a
                named = parts[s, at : at + 1].astype(jnp.int32) == entries[p]
                total += jnp.where(named, parts[s, a * size : (a + 1) * size], 0.0)
        for d in range(steps):
            for r in range(rows):
                out[p, d, r * BLOCK : (r + 1) * BLOCK] = total[d * rows + r]


def collect(entries, parts, aper, steps, length):
    return pl.pallas_call(
        functools.partial(collect_body, aper=aper),
        in_specs=[pl.BlockSpec(memory_space=pltpu.SMEM), pl.BlockSpec(memory_space=pltpu.VMEM)],
        out_specs=pl.BlockSpec(memory_space=pltpu.VMEM),
        out_shape=jax.ShapeDtypeStruct((entries.shape[0], steps, length), jnp.float32),
        compiler_params=pltpu.CompilerParams(vmem_limit_bytes=VMEM),
    )(entries, pltpu.with_memory_space_constraint(parts, pltpu.VMEM))


def cut_body(spot, slab, out, sems, *, cols):
    y = spot[0]
    xs = out.shape[1]
    copies = [
        pltpu.make_async_copy(
            slab.at[:, :, :, pl.ds(pl.multiple_of(y * cols, BLOCK), cols)], out.at[:, :, 0], sems.at[xs]
        )
    ]
    for x in range(xs):
        copies.append(
            pltpu.make_async_copy(slab.at[:, y, :, pl.ds((xs + x) * cols, cols)], out.at[:, x, 1], sems.at[x])
        )
    for c in copies:
        c.start()
    for c in copies:
        c.wait()


def cut(y, slab, cols):
    zls, xs, rows, _ = slab.shape
    slab = pltpu.with_memory_space_constraint(slab, pltpu.HBM)
    return pl.pallas_call(
        functools.partial(cut_body, cols=cols),
        in_specs=[pl.BlockSpec(memory_space=pltpu.SMEM), pl.BlockSpec(memory_space=pltpu.HBM)],
        out_specs=pl.BlockSpec(memory_space=pltpu.VMEM),
        out_shape=jax.ShapeDtypeStruct((zls, xs, CORES, rows, cols), slab.dtype),
        scratch_shapes=[pltpu.SemaphoreType.DMA((xs + 1,))],
        compiler_params=pltpu.CompilerParams(vmem_limit_bytes=VMEM),
    )(y, slab)


def sweep_weights(xc, yc):
    xr, xi = xc[:, 0], xc[:, 1]
    yr, yi = jnp.swapaxes(yc[:, 0], 1, 2), jnp.swapaxes(yc[:, 1], 1, 2)
    join = lambda a, b, c, d: jnp.concatenate([jnp.concatenate([a, b], 2), jnp.concatenate([c, d], 2)], 1)
    return join(xr, xi, -xi, xr), join(yr, -yi, yi, yr)


AXES = ("freq", "shot")
YS = 4
XS = 4
CORES = 2


def pairs(mesh_shape, move):
    freq, shot = mesh_shape
    at = lambda zh, y, zl, x, c: ((zh * YS + y) * shot) + (zl * XS + x) * CORES + c
    out = []
    for zh in range(freq // YS):
        for y in range(YS):
            for zl in range(shot // (XS * CORES)):
                for x in range(XS):
                    for c in range(CORES):
                        out.append((at(zh, y, zl, x, c), at(*move(zh, y, zl, x, c))))
    return out


def row_groups(mesh_shape):
    freq, shot = mesh_shape
    zhs, zls = freq // YS, shot // (XS * CORES)
    at = lambda zh, y, zl, x, c: ((zh * YS + y) * shot) + (zl * XS + x) * CORES + c
    out = [[at(zh, y, zl, x, 0) for zl in range(zls) for x in range(XS)] for zh in range(zhs) for y in range(YS)]
    return out + [[at(zh, y, zl, x, 1) for zl in range(zls) for y in range(YS)] for zh in range(zhs) for x in range(XS)]


def local(
    source_field,
    receiver_field,
    angular_freq,
    x_correction,
    y_correction,
    velocity,
    slab_owner,
    apertures,
    tile_order,
):
    freqs_dev, shots = lax.axis_size("freq"), lax.axis_size("shot")
    freq_total = angular_freq.shape[0] * freqs_dev
    height, width = velocity.shape[1:]
    f_id, s_id = lax.axis_index("freq"), lax.axis_index("shot")
    y = lax.rem(f_id, YS)
    zl, x, core = lax.div(s_id, XS * CORES), lax.rem(lax.div(s_id, CORES), XS), lax.rem(s_id, CORES)
    zhs, zls = freq // YS, shot // (XS * CORES)
    at = lambda zh, y, zl, x, c: ((zh * YS + y) * shot) + (zl * XS + x) * CORES + c
    every = [(zl, zh) for zl in range(zls) for zh in range(zhs)]
    out = [[at(zh, y, zl, x, 0) for zl, zh in every for x in range(XS)] for y in range(YS)]
    return out + [[at(zh, y, zl, x, 1) for zl, zh in every for y in range(YS)] for x in range(XS)]


def local(
    source_field,
    receiver_field,
    angular_freq,
    x_correction,
    y_correction,
    velocity,
    slab_owner,
    apertures,
    tile_order,
):
    freqs_dev, shots = lax.axis_size("freq"), lax.axis_size("shot")
    freq_total = angular_freq.shape[0] * freqs_dev
    height, width = velocity.shape[1:]
    f_id, s_id = lax.axis_index("freq"), lax.axis_index("shot")
    zh, y = f_id // YS, f_id % YS
    zl, x, core = s_id // (XS * CORES), (s_id // CORES) % XS, s_id % CORES
    zhs, zls = freqs_dev // YS, shots // (XS * CORES)
    first = core == 0
    cols = width // (CORES * XS)
    rows = height // (zls * XS)
    send = lambda v, move: lax.ppermute(v, AXES, pairs((freqs_dev, shots), move))

    outgoing = cut(y[None], velocity.reshape(zls, XS, rows, width), cols).reshape(shots, rows, cols)
    arrived = lax.all_to_all(outgoing, "shot", 0, 0, tiled=True)
    mine = jnp.stack([lax.dynamic_index_in_dim(arrived, slab_owner[d], 0, keepdims=False) for d in range(DEPTH)])

    groups = row_groups((freqs_dev, shots))
    members = len(groups[0])
    own = jnp.broadcast_to(mine[None], (members,) + mine.shape)
    own = lax.all_to_all(own, AXES, 0, 0, axis_index_groups=groups, tiled=True)

    column = jnp.where(first, y, x)
    partner_column = jnp.where(first, x, y)
    shift = lambda k: lambda zh, y, zl, x, c: (zh, (y + k) % YS, zl, x, c) if c == 0 else (zh, y, zl, (x + k) % XS, c)
    swap = lambda zh, y, zl, x, c: (zh, y, zl, x, 1 - c)
    place = lambda k: core * XS + lax.rem(column + XS - k, XS)
    partner_place = lambda k: (1 - core) * XS + lax.rem(partner_column + XS - k, XS)
    wx, wy = sweep_weights(x_correction, y_correction)
    turns = angular_freq * (0.5 / math.pi)
    src = pltpu.with_memory_space_constraint(source_field, pltpu.HBM)
    rcv = pltpu.with_memory_space_constraint(receiver_field, pltpu.HBM)

    tiles = apertures[0]
    order = [
        (place(0), partner_place(0)),
        (place(1), place(3)),
        (partner_place(1), partner_place(3)),
        (place(2), partner_place(2)),
    ]
    order = [jnp.stack(p).astype(jnp.int32) for p in order]
    firsts, wanted = fetch(jnp.stack([p[0] for p in order]), tiles, src, rcv, cols)

    def forward(call, slabs, done=()):
        return march(order[call], turns, slabs, wx, wy, firsts[call], src, rcv, tuple(done))

    own_p = send(own, swap)
    s1, s3 = send(own, shift(1)), send(own, shift(3))
    fields = forward(0, [own, own_p])
    s1, s3, later, *fields = lax.optimization_barrier((s1, s3, own, *fields))
    s2 = send(later, shift(2))
    s1_p, s3_p = send(s1, swap), send(s3, swap)
    fields = forward(1, [s1, s3], fields)
    s2, *fields = lax.optimization_barrier((s2, *fields))
    s2_p = send(s2, swap)

    slabs = [own, own_p, s1, s3, s1_p, s3_p, s2, s2_p]
    places = jnp.concatenate(order)
    terms = image_terms(tiles, places, turns, wx, wy, wanted, slabs, 1.0 / freq_total, freqs_dev)
    length = terms.shape[3] * terms.shape[4]
    terms = lax.all_to_all(terms.reshape(freqs_dev, -1, BLOCK), "freq", 0, 0, tiled=True)
    fields = forward(2, [s1_p, s3_p], fields)
    terms, *fields = lax.optimization_barrier((terms, *fields))
    dealt = lax.all_to_all(deal(tiles, terms, shots), "shot", 0, 0, tiled=True)
    fields = forward(3, [s2, s2_p], fields)
    entries = lax.dynamic_slice_in_dim(tile_order, s_id * TILE_DEV, TILE_DEV)
    image = collect(entries, dealt, tiles.shape[0], DEPTH, length)
    return (*fields, image)


def solution(mesh):
    in_specs = (
        P("freq", "shot", None, None, None),
        P("freq", "shot", None, None, None),
        P("freq"),
        P("freq", None, None, None),
        P("freq", None, None, None),
        P("shot", None, None),
        P(),
        P("shot", None),
        P(),
    )
    out_specs = (
        P("freq", "shot", None, None, None),
        P("freq", "shot", None, None, None),
        P("shot", None, "freq"),
    )
    return jax.shard_map(local, mesh=mesh, in_specs=in_specs, out_specs=out_specs, check_vma=False)
```

```python
import functools
import math

import jax
import jax.numpy as jnp
from jax import lax
from jax.experimental import pallas as pl
from jax.experimental.pallas import tpu as pltpu
from jax.sharding import PartitionSpec as P

DEPTH = 2
TILE_DEV = 4
AXES = ("freq", "shot")
YS = 4
XS = 4
CORES = 2
BLOCK = 128
VMEM = 24 * 1024 * 1024
NEAREST = 12582912.0
SIN = (4.442867755889893, -7.307443618774414, 3.594788074493408, -0.7843739986419678)
COS = (1.4142135381698608, -6.978850841522217, 5.7394609451293945, -1.8835630416870117, 0.31069818139076233)


def poly(u, coefs):
    total = coefs[-1] * u + coefs[-2]
    for c in coefs[-3::-1]:
        total = total * u + c
    return total


def sincos(turns):
    r = turns - ((turns + NEAREST) - NEAREST)
    u = r * r
    s = r * poly(u, SIN)
    c = poly(u, COS)
    return s * c, 1.0 - s * s


def rounded(parts):
    return tuple(v.astype(jnp.bfloat16) for v in parts)


def widened(parts):
    return tuple(v.astype(jnp.float32) for v in parts)


def quad(a, b, c, d):
    return jnp.concatenate([jnp.concatenate([a, b], 1), jnp.concatenate([c, d], 1)], 0)


def advance(parts, phases, wx, wy):
    height, width = parts[0][0].shape
    out = []
    for part, phase in zip(parts, phases):
        sr, si, rr, ri = widened(part)
        sin, cos = sincos(phase)
        out.append(rounded((sr * cos - si * sin, sr * sin + si * cos, rr * cos - ri * sin, rr * sin + ri * cos)))
    prod = jnp.dot(jnp.concatenate([quad(*v) for v in out], 0), wx, preferred_element_type=jnp.float32)
    for b, part in enumerate(out):
        x = prod[b * 2 * height : (b + 1) * 2 * height]
        sr, si, rr, ri = widened(part)
        out[b] = rounded(
            (
                sr + x[:height, :width],
                si + x[:height, width:],
                rr + x[height:, :width],
                ri + x[height:, width:],
            )
        )
    right = jnp.concatenate([quad(v[0], v[2], v[1], v[3]) for v in out], 1)
    prod = jnp.dot(wy, right, preferred_element_type=jnp.float32)
    for b, part in enumerate(out):
        y = prod[:, b * 2 * width : (b + 1) * 2 * width]
        sr, si, rr, ri = widened(part)
        out[b] = (
            sr + y[:height, :width],
            si + y[height:, :width],
            rr + y[:height, width:],
            ri + y[height:, width:],
        )
    return out


def slab_view(slab, d, cols):
    rows = slab[:, d, :, cols]
    return rows.reshape(rows.shape[0] * rows.shape[1], rows.shape[2])


def here():
    f_id, s_id = lax.axis_index("freq"), lax.axis_index("shot")
    return lax.rem(f_id, YS), lax.rem(lax.div(s_id, CORES), XS), lax.rem(s_id, CORES)


def column_blocks(k):
    y, x, core = here()
    first = core == 0
    mine = core * XS + lax.rem(jnp.where(first, y, x) + XS - k, XS)
    theirs = (1 - core) * XS + lax.rem(jnp.where(first, x, y) + XS - k, XS)
    return mine, theirs


def blocks_of(names):
    return [column_blocks(k)[theirs] for k, theirs in names]


def field_copies(src, rcv, target, sems, block, f):
    cols = target.shape[-1]
    at = pl.ds(pl.multiple_of(block * cols, BLOCK), cols)
    return [
        pltpu.make_async_copy(field.at[f, 0, :, :, at], target.at[i], sems.at[i])
        for i, field in enumerate((src, rcv))
    ]


def fetch_body(src, rcv, first, sems, *, name):
    copies = field_copies(src, rcv, first, sems, blocks_of([name])[0], 0)
    for c in copies:
        c.start()
    for c in copies:
        c.wait()


def fetch(name, src, rcv, cols):
    height = src.shape[3]
    hbm = pl.BlockSpec(memory_space=pltpu.HBM)
    return pl.pallas_call(
        functools.partial(fetch_body, name=name),
        in_specs=[hbm, hbm],
        out_specs=pl.BlockSpec(memory_space=pltpu.VMEM),
        out_shape=pltpu.VMEM((2, 2, height, cols), src.dtype),
        scratch_shapes=[pltpu.SemaphoreType.DMA((2,))],
        cost_estimate=pl.CostEstimate(flops=0, bytes_accessed=1 << 22, transcendentals=0),
        compiler_params=pltpu.CompilerParams(vmem_limit_bytes=VMEM),
    )(src, rcv)


def march_body(turns, wx, wy, src, rcv, *rest, names, freqs, given):
    count = len(names)
    slabs, rest = rest[:count], rest[count:]
    so, ro, held, made, in_sems, out_sems = rest[-6:]
    cols = [slice(c, c + BLOCK) for c in range(0, held.shape[-1], BLOCK)]
    unit = pl.program_id(0)
    units = count * freqs
    where = blocks_of(names)
    slot = lax.rem(unit, 2)

    def block_of(u):
        block, i = where[0], lax.div(u, freqs)
        for k in range(1, count):
            block = jnp.where(i == k, where[k], block)
        return block

    def loads(u):
        at = lax.rem(u, 2)
        return field_copies(src, rcv, held.at[at], in_sems.at[at], block_of(u), lax.rem(u, freqs))

    def stores(u):
        at = lax.rem(u, 2)
        width = made.shape[-1]
        spot = pl.ds(pl.multiple_of(block_of(u) * width, BLOCK), width)
        return [
            pltpu.make_async_copy(made.at[at, i], field.at[lax.rem(u, freqs), 0, :, :, spot], out_sems.at[at, i])
            for i, field in enumerate((so, ro))
        ]

    def each(copies, what):
        for c in copies:
            c.start() if what == "start" else c.wait()

    if not given:

        @pl.when(unit == 0)
        def _():
            each(loads(unit), "start")

    @pl.when(unit + 1 < units)
    def _():
        each(loads(unit + 1), "start")

    if given:
        first = rest[0]

        @pl.when(unit == 0)
        def _():
            held[0] = first[...]

        @pl.when(unit > 0)
        def _():
            each(loads(unit), "wait")

    else:
        each(loads(unit), "wait")

    @pl.when(unit >= 2)
    def _():
        each(stores(unit - 2), "wait")

    f = lax.rem(unit, freqs)

    def run(slab):
        parts = [
            (held[slot, 0, 0, :, c], held[slot, 0, 1, :, c], held[slot, 1, 0, :, c], -held[slot, 1, 1, :, c])
            for c in cols
        ]
        turn = turns[f]
        for d in range(slab.shape[1]):
            parts = advance(parts, [slab_view(slab, d, c) * turn for c in cols], wx[f], wy[f])
        for (sr, si, rr, ri), c in zip(parts, cols):
            made[slot, 0, 0, :, c] = sr.astype(made.dtype)
            made[slot, 0, 1, :, c] = si.astype(made.dtype)
            made[slot, 1, 0, :, c] = rr.astype(made.dtype)
            made[slot, 1, 1, :, c] = (-ri).astype(made.dtype)

    for k, slab in enumerate(slabs):

        @pl.when(lax.div(unit, freqs) == k)
        def _():
            run(slab)

    each(stores(unit), "start")

    @pl.when(unit == units - 1)
    def _():
        if units > 1:
            each(stores(unit - 1), "wait")
        each(stores(unit), "wait")


def march(names, turns, slabs, wx, wy, src, rcv, first=None, done=()):
    count, cols = len(slabs), slabs[0].shape[-1]
    freqs, height = src.shape[0], src.shape[3]
    vmem, hbm = pl.BlockSpec(memory_space=pltpu.VMEM), pl.BlockSpec(memory_space=pltpu.HBM)
    given = first is not None
    args = [turns, wx, wy, src, rcv, *slabs] + [first] * given
    in_specs = [vmem, vmem, vmem, hbm, hbm] + [vmem] * (count + given)
    cells = count * cols * height * freqs
    return pl.pallas_call(
        functools.partial(march_body, names=names, freqs=freqs, given=given),
        grid=(count * freqs,),
        in_specs=in_specs + [hbm] * len(done),
        out_specs=[hbm, hbm],
        scratch_shapes=[
            pltpu.VMEM((2, 2, 2, height, cols), src.dtype),
            pltpu.VMEM((2, 2, 2, height, cols), src.dtype),
            pltpu.SemaphoreType.DMA((2, 2)),
            pltpu.SemaphoreType.DMA((2, 2)),
        ],
        out_shape=[jax.ShapeDtypeStruct(src.shape, src.dtype), jax.ShapeDtypeStruct(rcv.shape, rcv.dtype)],
        input_output_aliases={len(args) + i: i for i in range(len(done))},
        cost_estimate=pl.CostEstimate(
            flops=cells * DEPTH * 4 * 2 * 4 * BLOCK * 3, bytes_accessed=cells * 16, transcendentals=0
        ),
        compiler_params=pltpu.CompilerParams(vmem_limit_bytes=VMEM),
    )(*args, *done)


def image_body(tiles, turns, wx, wy, src, rcv, *rest, names, scale, per, count):
    slabs, out, wanted, held, lines, sems = rest[:-5], *rest[-5:]
    aper = tiles.shape[0]
    x_blocks = [lax.div(tiles[a], 2) for a in range(aper)]
    copies = []
    for a in range(aper):
        at = pl.ds(pl.multiple_of(x_blocks[a] * BLOCK, BLOCK), BLOCK)
        for i, field in enumerate((src, rcv)):
            copies.append(pltpu.make_async_copy(field.at[:, 0, :, :, at], wanted.at[a, i], sems.at[a, i]))
    for c in copies:
        c.start()
    places = blocks_of(names)
    for a in range(aper):
        column = pl.multiple_of(lax.rem(x_blocks[a], per) * BLOCK, BLOCK)
        for k, slab in enumerate(slabs):

            @pl.when(places[k] == lax.div(x_blocks[a], per))
            def _():
                held[a] = slab[:, :, :, pl.ds(column, BLOCK)]

    for c in copies:
        c.wait()
    freqs = wanted.shape[2]
    parts = [
        [(wanted[a, 0, f, 0], wanted[a, 0, f, 1], wanted[a, 1, f, 0], -wanted[a, 1, f, 1]) for a in range(aper)]
        for f in range(freqs)
    ]
    half = BLOCK // 2
    for d in range(held.shape[2]):
        views = [slab_view(held.at[a], d, slice(0, BLOCK)) for a in range(aper)]
        parts = [advance(parts[f], [v * turns[f] for v in views], wx[f], wy[f]) for f in range(freqs)]
        for a in range(aper):
            term = sum(sr * rr - si * ri for sr, si, rr, ri in (p[a] for p in parts))
            odd = lax.rem(tiles[a], 2) == 1
            lines[a, :, :half] = jnp.where(odd, term[:, half:], term[:, :half]) * scale
            pairs_of = lines.shape[1] // 2
            even_odd = [lines[a, pl.ds(k, pairs_of, stride=2), :half] for k in range(2)]
            both = jnp.concatenate(even_odd, 1)
            out[:, a, d] = both.reshape(count, pairs_of // count, BLOCK)


def image_terms(tiles, names, turns, wx, wy, src, rcv, slabs, scale, count):
    steps, cols = slabs[0].shape[1], slabs[0].shape[-1]
    freqs, _, _, height, _ = src.shape
    aper = tiles.shape[0]
    vmem, hbm = pl.BlockSpec(memory_space=pltpu.VMEM), pl.BlockSpec(memory_space=pltpu.HBM)
    shape = (count, aper, steps, height // 2 // count, BLOCK)
    return pl.pallas_call(
        functools.partial(image_body, names=names, scale=scale, per=cols // BLOCK, count=count),
        in_specs=[pl.BlockSpec(memory_space=pltpu.SMEM), vmem, vmem, vmem, hbm, hbm] + [vmem] * len(slabs),
        out_specs=vmem,
        out_shape=jax.ShapeDtypeStruct(shape, jnp.float32),
        scratch_shapes=[
            pltpu.VMEM((aper, 2, freqs, 2, height, BLOCK), src.dtype),
            pltpu.VMEM((aper,) + slabs[0].shape[:3] + (BLOCK,), jnp.float32),
            pltpu.VMEM((aper, height, BLOCK), jnp.float32),
            pltpu.SemaphoreType.DMA((aper, 2)),
        ],
        cost_estimate=pl.CostEstimate(
            flops=aper * BLOCK * height * freqs * steps * 4 * 2 * 4 * BLOCK * 3, bytes_accessed=1 << 21, transcendentals=0
        ),
        compiler_params=pltpu.CompilerParams(vmem_limit_bytes=VMEM),
    )(tiles, turns, wx, wy, src, rcv, *slabs)


def deal_body(ids, parts, out):
    total = jnp.sum(parts[...], axis=0)
    spare = out.shape[1] - total.shape[0] - ids.shape[0]
    total = jnp.concatenate([total, ids[...], jnp.zeros((spare, BLOCK), jnp.float32)], 0)
    for j in range(out.shape[0]):
        out[j] = total


def deal(ids, parts, shots):
    rows = parts.shape[1] + 8
    return pl.pallas_call(
        deal_body,
        in_specs=[pl.BlockSpec(memory_space=pltpu.VMEM)] * 2,
        out_specs=pl.BlockSpec(memory_space=pltpu.VMEM),
        out_shape=jax.ShapeDtypeStruct((shots, rows, BLOCK), jnp.float32),
        compiler_params=pltpu.CompilerParams(vmem_limit_bytes=VMEM),
    )(ids, pltpu.with_memory_space_constraint(parts, pltpu.VMEM))


def collect_body(entries, parts, out, *, aper):
    steps = out.shape[1]
    rows = out.shape[2] // BLOCK
    size = steps * rows
    for p in range(out.shape[0]):
        total = jnp.zeros((size, BLOCK), jnp.float32)
        for s in range(parts.shape[0]):
            for a in range(aper):
                at = aper * size + a
                named = parts[s, at : at + 1] == entries[p : p + 1]
                total += jnp.where(named, parts[s, a * size : (a + 1) * size], 0.0)
        for d in range(steps):
            for r in range(rows):
                out[p, d, r * BLOCK : (r + 1) * BLOCK] = total[d * rows + r]


def collect(entries, parts, aper, steps, length):
    return pl.pallas_call(
        functools.partial(collect_body, aper=aper),
        in_specs=[pl.BlockSpec(memory_space=pltpu.VMEM)] * 2,
        out_specs=pl.BlockSpec(memory_space=pltpu.VMEM),
        out_shape=jax.ShapeDtypeStruct((entries.shape[0], steps, length), jnp.float32),
        compiler_params=pltpu.CompilerParams(vmem_limit_bytes=VMEM),
    )(entries, pltpu.with_memory_space_constraint(parts, pltpu.VMEM))


def cut_body(slab, out, sems, *, cols):
    y = here()[0]
    xs = out.shape[1]
    copies = [
        pltpu.make_async_copy(
            slab.at[:, :, :, pl.ds(pl.multiple_of(y * cols, BLOCK), cols)], out.at[:, :, 0], sems.at[xs]
        )
    ]
    for x in range(xs):
        copies.append(
            pltpu.make_async_copy(slab.at[:, y, :, pl.ds((xs + x) * cols, cols)], out.at[:, x, 1], sems.at[x])
        )
    for c in copies:
        c.start()
    for c in copies:
        c.wait()


def cut(slab, cols):
    zls, xs, rows, _ = slab.shape
    slab = pltpu.with_memory_space_constraint(slab, pltpu.HBM)
    return pl.pallas_call(
        functools.partial(cut_body, cols=cols),
        in_specs=[pl.BlockSpec(memory_space=pltpu.HBM)],
        out_specs=pl.BlockSpec(memory_space=pltpu.VMEM),
        out_shape=jax.ShapeDtypeStruct((zls, xs, CORES, rows, cols), slab.dtype),
        scratch_shapes=[pltpu.SemaphoreType.DMA((xs + 1,))],
        compiler_params=pltpu.CompilerParams(vmem_limit_bytes=VMEM),
    )(slab)


def sweep_weights(xc, yc):
    xr, xi = xc[:, 0], xc[:, 1]
    yr, yi = jnp.swapaxes(yc[:, 0], 1, 2), jnp.swapaxes(yc[:, 1], 1, 2)
    join = lambda a, b, c, d: jnp.concatenate([jnp.concatenate([a, b], 2), jnp.concatenate([c, d], 2)], 1)
    return join(xr, xi, -xi, xr), join(yr, -yi, yi, yr)


def pairs(mesh_shape, move):
    freq, shot = mesh_shape
    at = lambda zh, y, zl, x, c: ((zh * YS + y) * shot) + (zl * XS + x) * CORES + c
    out = []
    for zh in range(freq // YS):
        for y in range(YS):
            for zl in range(shot // (XS * CORES)):
                for x in range(XS):
                    for c in range(CORES):
                        out.append((at(zh, y, zl, x, c), at(*move(zh, y, zl, x, c))))
    return out


def row_groups(mesh_shape):
    freq, shot = mesh_shape
    zhs, zls = freq // YS, shot // (XS * CORES)
    at = lambda zh, y, zl, x, c: ((zh * YS + y) * shot) + (zl * XS + x) * CORES + c
    out = [[at(zh, y, zl, x, 0) for zl in range(zls) for x in range(XS)] for zh in range(zhs) for y in range(YS)]
    return out + [[at(zh, y, zl, x, 1) for zl in range(zls) for y in range(YS)] for zh in range(zhs) for x in range(XS)]


def local(
    source_field,
    receiver_field,
    angular_freq,
    x_correction,
    y_correction,
    velocity,
    slab_owner,
    apertures,
    tile_order,
):
    freqs_dev, shots = lax.axis_size("freq"), lax.axis_size("shot")
    freq_total = angular_freq.shape[0] * freqs_dev
    height, width = velocity.shape[1:]
    zls = shots // (XS * CORES)
    cols = width // (CORES * XS)
    rows = height // (zls * XS)
    send = lambda v, move: lax.ppermute(v, AXES, pairs((freqs_dev, shots), move))

    outgoing = cut(velocity.reshape(zls, XS, rows, width), cols).reshape(shots, rows, cols)
    arrived = lax.all_to_all(outgoing, "shot", 0, 0, tiled=True)
    mine = jnp.stack([lax.dynamic_index_in_dim(arrived, slab_owner[d], 0, keepdims=False) for d in range(DEPTH)])

    groups = row_groups((freqs_dev, shots))
    members = len(groups[0])
    own = jnp.broadcast_to(mine[None], (members,) + mine.shape)
    own = lax.all_to_all(own, AXES, 0, 0, axis_index_groups=groups, tiled=True)

    shift = lambda k: lambda zh, y, zl, x, c: (zh, (y + k) % YS, zl, x, c) if c == 0 else (zh, y, zl, (x + k) % XS, c)
    swap = lambda zh, y, zl, x, c: (zh, y, zl, x, 1 - c)
    wx, wy = sweep_weights(x_correction, y_correction)
    turns = jnp.broadcast_to((angular_freq * (0.5 / math.pi))[:, None, None], (angular_freq.shape[0], 1, BLOCK))
    src = pltpu.with_memory_space_constraint(source_field, pltpu.HBM)
    rcv = pltpu.with_memory_space_constraint(receiver_field, pltpu.HBM)

    order = [[(0, 0), (0, 1)], [(1, 0), (3, 0)], [(1, 1), (3, 1)], [(2, 0), (2, 1)]]
    first = fetch(order[0][0], src, rcv, cols)

    def forward(call, slabs, first=None, done=()):
        return march(order[call], turns, slabs, wx, wy, src, rcv, first, tuple(done))

    own_p = send(own, swap)
    s1, s3 = send(own, shift(1)), send(own, shift(3))
    fields = forward(0, [own, own_p], first)
    s1, s3, later, *fields = lax.optimization_barrier((s1, s3, own, *fields))
    s2 = send(later, shift(2))
    s1_p, s3_p = send(s1, swap), send(s3, swap)
    fields = forward(1, [s1, s3], done=fields)
    s2, *fields = lax.optimization_barrier((s2, *fields))
    s2_p = send(s2, swap)

    rows_of = lambda ids: jnp.broadcast_to(ids.astype(jnp.float32)[:, None], (ids.shape[0], BLOCK))
    slabs = [own, own_p, s1, s3, s1_p, s3_p, s2, s2_p]
    tiles = apertures[0]
    names = [name for names in order for name in names]
    terms = image_terms(tiles, names, turns, wx, wy, src, rcv, slabs, 1.0 / freq_total, freqs_dev)
    length = terms.shape[3] * terms.shape[4]
    terms = lax.all_to_all(terms.reshape(freqs_dev, -1, BLOCK), "freq", 0, 0, tiled=True)
    fields = forward(2, [s1_p, s3_p], done=fields)
    terms, *fields = lax.optimization_barrier((terms, *fields))
    dealt = lax.all_to_all(deal(rows_of(tiles), terms, shots), "shot", 0, 0, tiled=True)
    fields = forward(3, [s2, s2_p], done=fields)
    entries = lax.dynamic_slice_in_dim(tile_order, lax.axis_index("shot") * TILE_DEV, TILE_DEV)
    image = collect(rows_of(entries), dealt, tiles.shape[0], DEPTH, length)
    return (*fields, image)


def solution(mesh):
    in_specs = (
        P("freq", "shot", None, None, None),
        P("freq", "shot", None, None, None),
        P("freq"),
        P("freq", None, None, None),
        P("freq", None, None, None),
        P("shot", None, None),
        P(),
        P("shot", None),
        P(),
    )
    out_specs = (
        P("freq", "shot", None, None, None),
        P("freq", "shot", None, None, None),
        P("shot", None, "freq"),
    )
    return jax.shard_map(local, mesh=mesh, in_specs=in_specs, out_specs=out_specs, check_vma=False)
```

```python
import functools
import math

import jax
import jax.numpy as jnp
from jax import lax
from jax.experimental import pallas as pl
from jax.experimental.pallas import tpu as pltpu
from jax.sharding import PartitionSpec as P

DEPTH = 2
TILE_DEV = 4
AXES = ("freq", "shot")
YS = 4
XS = 4
CORES = 2
BLOCK = 128
EARLY = 2
VMEM = 24 * 1024 * 1024
NEAREST = 12582912.0
SIN = (4.442867755889893, -7.307443618774414, 3.594788074493408, -0.7843739986419678)
COS = (1.4142135381698608, -6.978850841522217, 5.7394609451293945, -1.8835630416870117, 0.31069818139076233)


def poly(u, coefs):
    total = coefs[-1] * u + coefs[-2]
    for c in coefs[-3::-1]:
        total = total * u + c
    return total


def sincos(turns):
    r = turns - ((turns + NEAREST) - NEAREST)
    u = r * r
    s = r * poly(u, SIN)
    c = poly(u, COS)
    return s * c, 1.0 - s * s


def rounded(parts):
    return tuple(v.astype(jnp.bfloat16) for v in parts)


def widened(parts):
    return tuple(v.astype(jnp.float32) for v in parts)


def quad(a, b, c, d):
    return jnp.concatenate([jnp.concatenate([a, b], 1), jnp.concatenate([c, d], 1)], 0)


def advance(parts, phases, wx, wy):
    height, width = parts[0][0].shape
    out = []
    for part, phase in zip(parts, phases):
        sr, si, rr, ri = widened(part)
        sin, cos = sincos(phase)
        out.append(rounded((sr * cos - si * sin, sr * sin + si * cos, rr * cos - ri * sin, rr * sin + ri * cos)))
    prod = jnp.dot(jnp.concatenate([quad(*v) for v in out], 0), wx, preferred_element_type=jnp.float32)
    for b, part in enumerate(out):
        x = prod[b * 2 * height : (b + 1) * 2 * height]
        sr, si, rr, ri = widened(part)
        out[b] = rounded(
            (
                sr + x[:height, :width],
                si + x[:height, width:],
                rr + x[height:, :width],
                ri + x[height:, width:],
            )
        )
    right = jnp.concatenate([quad(v[0], v[2], v[1], v[3]) for v in out], 1)
    prod = jnp.dot(wy, right, preferred_element_type=jnp.float32)
    for b, part in enumerate(out):
        y = prod[:, b * 2 * width : (b + 1) * 2 * width]
        sr, si, rr, ri = widened(part)
        out[b] = (
            sr + y[:height, :width],
            si + y[height:, :width],
            rr + y[:height, width:],
            ri + y[height:, width:],
        )
    return out


def slab_view(slab, d, cols):
    rows = slab[:, d, :, cols]
    return rows.reshape(rows.shape[0] * rows.shape[1], rows.shape[2])


def in_vmem(arrays):
    return [pltpu.with_memory_space_constraint(a, pltpu.VMEM) for a in arrays]


def here():
    f_id, s_id = lax.axis_index("freq"), lax.axis_index("shot")
    return lax.rem(f_id, YS), lax.rem(lax.div(s_id, CORES), XS), lax.rem(s_id, CORES)


def column_blocks(k):
    y, x, core = here()
    first = core == 0
    mine = core * XS + lax.rem(jnp.where(first, y, x) + XS - k, XS)
    theirs = (1 - core) * XS + lax.rem(jnp.where(first, x, y) + XS - k, XS)
    return mine, theirs


def blocks_of(names):
    return [column_blocks(k)[theirs] for k, theirs in names]


def field_copies(src, rcv, target, sems, block, f):
    cols = target.shape[-1]
    at = pl.ds(pl.multiple_of(block * cols, BLOCK), cols)
    return [
        pltpu.make_async_copy(field.at[f, 0, :, :, at], target.at[i], sems.at[i])
        for i, field in enumerate((src, rcv))
    ]


def fetch_body(src, rcv, first, sems, *, name):
    copies = field_copies(src, rcv, first, sems, blocks_of([name])[0], 0)
    for c in copies:
        c.start()
    for c in copies:
        c.wait()


def fetch(name, src, rcv, cols):
    height = src.shape[3]
    hbm = pl.BlockSpec(memory_space=pltpu.HBM)
    return pl.pallas_call(
        functools.partial(fetch_body, name=name),
        in_specs=[hbm, hbm],
        out_specs=pl.BlockSpec(memory_space=pltpu.VMEM),
        out_shape=pltpu.VMEM((2, 2, height, cols), src.dtype),
        scratch_shapes=[pltpu.SemaphoreType.DMA((2,))],
        cost_estimate=pl.CostEstimate(flops=0, bytes_accessed=1 << 22, transcendentals=0),
        compiler_params=pltpu.CompilerParams(vmem_limit_bytes=VMEM),
    )(src, rcv)


def march_body(turns, wx, wy, src, rcv, *rest, names, freqs, given):
    count = len(names)
    slabs, rest = rest[:count], rest[count:]
    so, ro, held, made, in_sems, out_sems = rest[-6:]
    cols = [slice(c, c + BLOCK) for c in range(0, held.shape[-1], BLOCK)]
    unit = pl.program_id(0)
    units = count * freqs
    where = blocks_of(names)
    slot = lax.rem(unit, 2)

    def block_of(u):
        block, i = where[0], lax.div(u, freqs)
        for k in range(1, count):
            block = jnp.where(i == k, where[k], block)
        return block

    def loads(u):
        at = lax.rem(u, 2)
        return field_copies(src, rcv, held.at[at], in_sems.at[at], block_of(u), lax.rem(u, freqs))

    def stores(u):
        at = lax.rem(u, 2)
        width = made.shape[-1]
        spot = pl.ds(pl.multiple_of(block_of(u) * width, BLOCK), width)
        return [
            pltpu.make_async_copy(made.at[at, i], field.at[lax.rem(u, freqs), 0, :, :, spot], out_sems.at[at, i])
            for i, field in enumerate((so, ro))
        ]

    def each(copies, what):
        for c in copies:
            c.start() if what == "start" else c.wait()

    if not given:

        @pl.when(unit == 0)
        def _():
            each(loads(unit), "start")

    @pl.when(unit + 1 < units)
    def _():
        each(loads(unit + 1), "start")

    if given:
        first = rest[0]

        @pl.when(unit == 0)
        def _():
            held[0] = first[...]

        @pl.when(unit > 0)
        def _():
            each(loads(unit), "wait")

    else:
        each(loads(unit), "wait")

    @pl.when(unit >= 2)
    def _():
        each(stores(unit - 2), "wait")

    f = lax.rem(unit, freqs)

    def run(slab):
        parts = [
            (held[slot, 0, 0, :, c], held[slot, 0, 1, :, c], held[slot, 1, 0, :, c], -held[slot, 1, 1, :, c])
            for c in cols
        ]
        turn = turns[f]
        for d in range(slab.shape[1]):
            parts = advance(parts, [slab_view(slab, d, c) * turn for c in cols], wx[f], wy[f])
        for (sr, si, rr, ri), c in zip(parts, cols):
            made[slot, 0, 0, :, c] = sr.astype(made.dtype)
            made[slot, 0, 1, :, c] = si.astype(made.dtype)
            made[slot, 1, 0, :, c] = rr.astype(made.dtype)
            made[slot, 1, 1, :, c] = (-ri).astype(made.dtype)

    for k, slab in enumerate(slabs):

        @pl.when(lax.div(unit, freqs) == k)
        def _():
            run(slab)

    each(stores(unit), "start")

    @pl.when(unit == units - 1)
    def _():
        if units > 1:
            each(stores(unit - 1), "wait")
        each(stores(unit), "wait")


def march(names, turns, slabs, wx, wy, src, rcv, first=None, done=()):
    count, cols = len(slabs), slabs[0].shape[-1]
    freqs, height = src.shape[0], src.shape[3]
    vmem, hbm = pl.BlockSpec(memory_space=pltpu.VMEM), pl.BlockSpec(memory_space=pltpu.HBM)
    given = first is not None
    slabs = in_vmem(slabs)
    args = [turns, wx, wy, src, rcv, *slabs] + [first] * given
    in_specs = [vmem, vmem, vmem, hbm, hbm] + [vmem] * (count + given)
    cells = count * cols * height * freqs
    return pl.pallas_call(
        functools.partial(march_body, names=names, freqs=freqs, given=given),
        grid=(count * freqs,),
        in_specs=in_specs + [hbm] * len(done),
        out_specs=[hbm, hbm],
        scratch_shapes=[
            pltpu.VMEM((2, 2, 2, height, cols), src.dtype),
            pltpu.VMEM((2, 2, 2, height, cols), src.dtype),
            pltpu.SemaphoreType.DMA((2, 2)),
            pltpu.SemaphoreType.DMA((2, 2)),
        ],
        out_shape=[jax.ShapeDtypeStruct(src.shape, src.dtype), jax.ShapeDtypeStruct(rcv.shape, rcv.dtype)],
        input_output_aliases={len(args) + i: i for i in range(len(done))},
        cost_estimate=pl.CostEstimate(
            flops=cells * DEPTH * 4 * 2 * 4 * BLOCK * 3, bytes_accessed=cells * 16, transcendentals=0
        ),
        compiler_params=pltpu.CompilerParams(vmem_limit_bytes=VMEM),
    )(*args, *done)


def image_body(tiles, turns, wx, wy, src, rcv, *rest, names, scale, per, count):
    slabs, out, wanted, held, lines, sems = rest[:-5], *rest[-5:]
    aper = tiles.shape[0]
    x_blocks = [lax.div(tiles[a], 2) for a in range(aper)]
    copies = []
    for a in range(aper):
        at = pl.ds(pl.multiple_of(x_blocks[a] * BLOCK, BLOCK), BLOCK)
        for i, field in enumerate((src, rcv)):
            copies.append(pltpu.make_async_copy(field.at[:, 0, :, :, at], wanted.at[a, i], sems.at[a, i]))
    for c in copies:
        c.start()
    places = blocks_of(names)
    for a in range(aper):
        column = pl.multiple_of(lax.rem(x_blocks[a], per) * BLOCK, BLOCK)
        for k, slab in enumerate(slabs):

            @pl.when(places[k] == lax.div(x_blocks[a], per))
            def _():
                held[a] = slab[:, :, :, pl.ds(column, BLOCK)]

    for c in copies:
        c.wait()
    freqs = wanted.shape[2]
    parts = [
        [(wanted[a, 0, f, 0], wanted[a, 0, f, 1], wanted[a, 1, f, 0], -wanted[a, 1, f, 1]) for a in range(aper)]
        for f in range(freqs)
    ]
    half = BLOCK // 2
    for d in range(held.shape[2]):
        views = [slab_view(held.at[a], d, slice(0, BLOCK)) for a in range(aper)]
        parts = [advance(parts[f], [v * turns[f] for v in views], wx[f], wy[f]) for f in range(freqs)]
        for a in range(aper):
            term = sum(sr * rr - si * ri for sr, si, rr, ri in (p[a] for p in parts))
            odd = lax.rem(tiles[a], 2) == 1
            lines[a, :, :half] = jnp.where(odd, term[:, half:], term[:, :half]) * scale
            pairs_of = lines.shape[1] // 2
            even_odd = [lines[a, pl.ds(k, pairs_of, stride=2), :half] for k in range(2)]
            both = jnp.concatenate(even_odd, 1)
            out[:, a, d] = both.reshape(count, pairs_of // count, BLOCK)


def image_terms(tiles, names, turns, wx, wy, src, rcv, slabs, scale, count):
    steps, cols = slabs[0].shape[1], slabs[0].shape[-1]
    slabs = in_vmem(slabs)
    freqs, _, _, height, _ = src.shape
    aper = tiles.shape[0]
    vmem, hbm = pl.BlockSpec(memory_space=pltpu.VMEM), pl.BlockSpec(memory_space=pltpu.HBM)
    shape = (count, aper, steps, height // 2 // count, BLOCK)
    return pl.pallas_call(
        functools.partial(image_body, names=names, scale=scale, per=cols // BLOCK, count=count),
        in_specs=[pl.BlockSpec(memory_space=pltpu.SMEM), vmem, vmem, vmem, hbm, hbm] + [vmem] * len(slabs),
        out_specs=vmem,
        out_shape=jax.ShapeDtypeStruct(shape, jnp.float32),
        scratch_shapes=[
            pltpu.VMEM((aper, 2, freqs, 2, height, BLOCK), src.dtype),
            pltpu.VMEM((aper,) + slabs[0].shape[:3] + (BLOCK,), jnp.float32),
            pltpu.VMEM((aper, height, BLOCK), jnp.float32),
            pltpu.SemaphoreType.DMA((aper, 2)),
        ],
        cost_estimate=pl.CostEstimate(
            flops=aper * BLOCK * height * freqs * steps * 4 * 2 * 4 * BLOCK * 3, bytes_accessed=1 << 21, transcendentals=0
        ),
        compiler_params=pltpu.CompilerParams(vmem_limit_bytes=VMEM),
    )(tiles, turns, wx, wy, src, rcv, *slabs)


def deal_body(ids, parts, out):
    total = jnp.sum(parts[...], axis=0)
    spare = out.shape[1] - total.shape[0] - ids.shape[0]
    total = jnp.concatenate([total, ids[...], jnp.zeros((spare, BLOCK), jnp.float32)], 0)
    for j in range(out.shape[0]):
        out[j] = total


def deal(ids, parts, shots):
    rows = parts.shape[1] + 8
    return pl.pallas_call(
        deal_body,
        in_specs=[pl.BlockSpec(memory_space=pltpu.VMEM)] * 2,
        out_specs=pl.BlockSpec(memory_space=pltpu.VMEM),
        out_shape=jax.ShapeDtypeStruct((shots, rows, BLOCK), jnp.float32),
        compiler_params=pltpu.CompilerParams(vmem_limit_bytes=VMEM),
    )(ids, pltpu.with_memory_space_constraint(parts, pltpu.VMEM))


def collect_body(entries, parts, out, *, aper):
    steps = out.shape[1]
    rows = out.shape[2] // BLOCK
    size = steps * rows
    for p in range(out.shape[0]):
        total = jnp.zeros((size, BLOCK), jnp.float32)
        for s in range(parts.shape[0]):
            for a in range(aper):
                at = aper * size + a
                named = parts[s, at : at + 1] == entries[p : p + 1]
                total += jnp.where(named, parts[s, a * size : (a + 1) * size], 0.0)
        for d in range(steps):
            for r in range(rows):
                out[p, d, r * BLOCK : (r + 1) * BLOCK] = total[d * rows + r]


def collect(entries, parts, aper, steps, length):
    return pl.pallas_call(
        functools.partial(collect_body, aper=aper),
        in_specs=[pl.BlockSpec(memory_space=pltpu.VMEM)] * 2,
        out_specs=pl.BlockSpec(memory_space=pltpu.VMEM),
        out_shape=jax.ShapeDtypeStruct((entries.shape[0], steps, length), jnp.float32),
        compiler_params=pltpu.CompilerParams(vmem_limit_bytes=VMEM),
    )(entries, pltpu.with_memory_space_constraint(parts, pltpu.VMEM))


def cut_body(slab, out, sems, *, cols):
    y = here()[0]
    xs = out.shape[1]
    copies = [
        pltpu.make_async_copy(
            slab.at[:, :, :, pl.ds(pl.multiple_of(y * cols, BLOCK), cols)], out.at[:, :, 0], sems.at[xs]
        )
    ]
    for x in range(xs):
        copies.append(
            pltpu.make_async_copy(slab.at[:, y, :, pl.ds((xs + x) * cols, cols)], out.at[:, x, 1], sems.at[x])
        )
    for c in copies:
        c.start()
    for c in copies:
        c.wait()


def cut(slab, cols):
    zls, xs, rows, _ = slab.shape
    slab = pltpu.with_memory_space_constraint(slab, pltpu.HBM)
    return pl.pallas_call(
        functools.partial(cut_body, cols=cols),
        in_specs=[pl.BlockSpec(memory_space=pltpu.HBM)],
        out_specs=pl.BlockSpec(memory_space=pltpu.VMEM),
        out_shape=jax.ShapeDtypeStruct((zls, xs, CORES, rows, cols), slab.dtype),
        scratch_shapes=[pltpu.SemaphoreType.DMA((xs + 1,))],
        compiler_params=pltpu.CompilerParams(vmem_limit_bytes=VMEM),
    )(slab)


def sweep_weights(xc, yc):
    xr, xi = xc[:, 0], xc[:, 1]
    yr, yi = jnp.swapaxes(yc[:, 0], 1, 2), jnp.swapaxes(yc[:, 1], 1, 2)
    join = lambda a, b, c, d: jnp.concatenate([jnp.concatenate([a, b], 2), jnp.concatenate([c, d], 2)], 1)
    return join(xr, xi, -xi, xr), join(yr, -yi, yi, yr)


def pairs(mesh_shape, move):
    freq, shot = mesh_shape
    at = lambda zh, y, zl, x, c: ((zh * YS + y) * shot) + (zl * XS + x) * CORES + c
    out = []
    for zh in range(freq // YS):
        for y in range(YS):
            for zl in range(shot // (XS * CORES)):
                for x in range(XS):
                    for c in range(CORES):
                        out.append((at(zh, y, zl, x, c), at(*move(zh, y, zl, x, c))))
    return out


def row_groups(mesh_shape):
    freq, shot = mesh_shape
    zhs, zls = freq // YS, shot // (XS * CORES)
    at = lambda zh, y, zl, x, c: ((zh * YS + y) * shot) + (zl * XS + x) * CORES + c
    out = [[at(zh, y, zl, x, 0) for zl in range(zls) for x in range(XS)] for zh in range(zhs) for y in range(YS)]
    return out + [[at(zh, y, zl, x, 1) for zl in range(zls) for y in range(YS)] for zh in range(zhs) for x in range(XS)]


def local(
    source_field,
    receiver_field,
    angular_freq,
    x_correction,
    y_correction,
    velocity,
    slab_owner,
    apertures,
    tile_order,
):
    freqs_dev, shots = lax.axis_size("freq"), lax.axis_size("shot")
    freq_total = angular_freq.shape[0] * freqs_dev
    height, width = velocity.shape[1:]
    zls = shots // (XS * CORES)
    cols = width // (CORES * XS)
    rows = height // (zls * XS)
    send = lambda v, move: lax.ppermute(v, AXES, pairs((freqs_dev, shots), move))

    outgoing = cut(velocity.reshape(zls, XS, rows, width), cols).reshape(shots, rows, cols)
    arrived = lax.all_to_all(outgoing, "shot", 0, 0, tiled=True)
    mine = jnp.stack([lax.dynamic_index_in_dim(arrived, slab_owner[d], 0, keepdims=False) for d in range(DEPTH)])

    groups = row_groups((freqs_dev, shots))
    members = len(groups[0])
    own = jnp.broadcast_to(mine[None], (members,) + mine.shape)
    own = lax.all_to_all(own, AXES, 0, 0, axis_index_groups=groups, tiled=True)

    shift = lambda k: lambda zh, y, zl, x, c: (zh, (y + k) % YS, zl, x, c) if c == 0 else (zh, y, zl, (x + k) % XS, c)
    swap = lambda zh, y, zl, x, c: (zh, y, zl, x, 1 - c)
    wx, wy = sweep_weights(x_correction, y_correction)
    turns = jnp.broadcast_to((angular_freq * (0.5 / math.pi))[:, None, None], (angular_freq.shape[0], 1, BLOCK))
    src = pltpu.with_memory_space_constraint(source_field, pltpu.HBM)
    rcv = pltpu.with_memory_space_constraint(receiver_field, pltpu.HBM)

    tiles = apertures[0]
    rows_of = lambda ids: jnp.broadcast_to(ids.astype(jnp.float32)[:, None], (ids.shape[0], BLOCK))
    entries = lax.dynamic_slice_in_dim(tile_order, lax.axis_index("shot") * TILE_DEV, TILE_DEV)
    order = [[(0, 0), (0, 1)], [(1, 0), (3, 0)], [(1, 1), (3, 1)], [(2, 0), (2, 1)]]
    firsts = [fetch(blocks[0], src, rcv, cols) for blocks in order[:EARLY]]
    own, wx, wy, turns, named, entries, *firsts = lax.optimization_barrier(
        (own, wx, wy, turns, rows_of(tiles), rows_of(entries), *firsts)
    )
    firsts += [None] * (len(order) - len(firsts))

    def forward(call, slabs, done=()):
        return march(order[call], turns, slabs, wx, wy, src, rcv, firsts[call], tuple(done))

    own_p = send(own, swap)
    s1, s3 = send(own, shift(1)), send(own, shift(3))
    fields = forward(0, [own, own_p])
    s1, s3, later, *fields = lax.optimization_barrier((s1, s3, own, *fields))
    s2 = send(later, shift(2))
    s1_p, s3_p = send(s1, swap), send(s3, swap)
    fields = forward(1, [s1, s3], fields)
    s2, *fields = lax.optimization_barrier((s2, *fields))
    s2_p = send(s2, swap)

    slabs = [own, own_p, s1, s3, s1_p, s3_p, s2, s2_p]
    names = [name for names in order for name in names]
    terms = image_terms(tiles, names, turns, wx, wy, src, rcv, slabs, 1.0 / freq_total, freqs_dev)
    length = terms.shape[3] * terms.shape[4]
    terms = lax.all_to_all(terms.reshape(freqs_dev, -1, BLOCK), "freq", 0, 0, tiled=True)
    fields = forward(2, [s1_p, s3_p], fields)
    terms, *fields = lax.optimization_barrier((terms, *fields))
    dealt = lax.all_to_all(deal(named, terms, shots), "shot", 0, 0, tiled=True)
    fields = forward(3, [s2, s2_p], fields)
    image = collect(entries, dealt, tiles.shape[0], DEPTH, length)
    return (*fields, image)


def solution(mesh):
    in_specs = (
        P("freq", "shot", None, None, None),
        P("freq", "shot", None, None, None),
        P("freq"),
        P("freq", None, None, None),
        P("freq", None, None, None),
        P("shot", None, None),
        P(),
        P("shot", None),
        P(),
    )
    out_specs = (
        P("freq", "shot", None, None, None),
        P("freq", "shot", None, None, None),
        P("shot", None, "freq"),
    )
    return jax.shard_map(local, mesh=mesh, in_specs=in_specs, out_specs=out_specs, check_vma=False)
```

```python
import functools
import math

import jax
import jax.numpy as jnp
from jax import lax
from jax.experimental import pallas as pl
from jax.experimental.pallas import tpu as pltpu
from jax.sharding import PartitionSpec as P

DEPTH = 2
TILE_DEV = 4
AXES = ("freq", "shot")
YS = 4
XS = 4
CORES = 2
BLOCK = 128
EARLY = 1
AHEAD = (0,)
VMEM = 24 * 1024 * 1024
NEAREST = 12582912.0
SIN = (4.442867755889893, -7.307443618774414, 3.594788074493408, -0.7843739986419678)
COS = (1.4142135381698608, -6.978850841522217, 5.7394609451293945, -1.8835630416870117, 0.31069818139076233)


def poly(u, coefs):
    total = coefs[-1] * u + coefs[-2]
    for c in coefs[-3::-1]:
        total = total * u + c
    return total


def sincos(turns):
    r = turns - ((turns + NEAREST) - NEAREST)
    u = r * r
    s = r * poly(u, SIN)
    c = poly(u, COS)
    return s * c, 1.0 - s * s


def rounded(parts):
    return tuple(v.astype(jnp.bfloat16) for v in parts)


def widened(parts):
    return tuple(v.astype(jnp.float32) for v in parts)


def quad(a, b, c, d):
    return jnp.concatenate([jnp.concatenate([a, b], 1), jnp.concatenate([c, d], 1)], 0)


def advance(parts, phases, wx, wy):
    height, width = parts[0][0].shape
    out = []
    for part, phase in zip(parts, phases):
        sr, si, rr, ri = widened(part)
        sin, cos = sincos(phase)
        out.append(rounded((sr * cos - si * sin, sr * sin + si * cos, rr * cos - ri * sin, rr * sin + ri * cos)))
    prod = jnp.dot(jnp.concatenate([quad(*v) for v in out], 0), wx, preferred_element_type=jnp.float32)
    for b, part in enumerate(out):
        x = prod[b * 2 * height : (b + 1) * 2 * height]
        sr, si, rr, ri = widened(part)
        out[b] = rounded(
            (
                sr + x[:height, :width],
                si + x[:height, width:],
                rr + x[height:, :width],
                ri + x[height:, width:],
            )
        )
    right = jnp.concatenate([quad(v[0], v[2], v[1], v[3]) for v in out], 1)
    prod = jnp.dot(wy, right, preferred_element_type=jnp.float32)
    for b, part in enumerate(out):
        y = prod[:, b * 2 * width : (b + 1) * 2 * width]
        sr, si, rr, ri = widened(part)
        out[b] = (
            sr + y[:height, :width],
            si + y[height:, :width],
            rr + y[:height, width:],
            ri + y[height:, width:],
        )
    return out


def slab_view(slab, d, cols):
    rows = slab[:, d, :, cols]
    return rows.reshape(rows.shape[0] * rows.shape[1], rows.shape[2])


def in_vmem(arrays):
    return [pltpu.with_memory_space_constraint(a, pltpu.VMEM) for a in arrays]


def here():
    f_id, s_id = lax.axis_index("freq"), lax.axis_index("shot")
    return lax.rem(f_id, YS), lax.rem(lax.div(s_id, CORES), XS), lax.rem(s_id, CORES)


def column_blocks(k):
    y, x, core = here()
    first = core == 0
    mine = core * XS + lax.rem(jnp.where(first, y, x) + XS - k, XS)
    theirs = (1 - core) * XS + lax.rem(jnp.where(first, x, y) + XS - k, XS)
    return mine, theirs


def blocks_of(names):
    return [column_blocks(k)[theirs] for k, theirs in names]


def field_copies(src, rcv, target, sems, block, f):
    cols = target.shape[-1]
    at = pl.ds(pl.multiple_of(block * cols, BLOCK), cols)
    return [
        pltpu.make_async_copy(field.at[f, 0, :, :, at], target.at[i], sems.at[i])
        for i, field in enumerate((src, rcv))
    ]


def fetch_body(src, rcv, first, sems, *, name):
    copies = field_copies(src, rcv, first, sems, blocks_of([name])[0], 0)
    for c in copies:
        c.start()
    for c in copies:
        c.wait()


def fetch(name, src, rcv, cols):
    height = src.shape[3]
    hbm = pl.BlockSpec(memory_space=pltpu.HBM)
    return pl.pallas_call(
        functools.partial(fetch_body, name=name),
        in_specs=[hbm, hbm],
        out_specs=pl.BlockSpec(memory_space=pltpu.VMEM),
        out_shape=pltpu.VMEM((2, 2, height, cols), src.dtype),
        scratch_shapes=[pltpu.SemaphoreType.DMA((2,))],
        cost_estimate=pl.CostEstimate(flops=0, bytes_accessed=1 << 22, transcendentals=0),
        compiler_params=pltpu.CompilerParams(vmem_limit_bytes=VMEM),
    )(src, rcv)


def march_body(turns, wx, wy, src, rcv, *rest, names, freqs, given, ahead):
    count = len(names)
    slabs, rest = rest[:count], rest[count:]
    held, made, in_sems, out_sems, ahead_sems = rest[-5:]
    so, ro = rest[-7 - (ahead is not None) :][:2]
    cols = [slice(c, c + BLOCK) for c in range(0, held.shape[-1], BLOCK)]
    unit = pl.program_id(0)
    units = count * freqs
    where = blocks_of(names)
    slot = lax.rem(unit, 2)

    def block_of(u):
        block, i = where[0], lax.div(u, freqs)
        for k in range(1, count):
            block = jnp.where(i == k, where[k], block)
        return block

    def loads(u):
        at = lax.rem(u, 2)
        return field_copies(src, rcv, held.at[at], in_sems.at[at], block_of(u), lax.rem(u, freqs))

    def stores(u):
        at = lax.rem(u, 2)
        width = made.shape[-1]
        spot = pl.ds(pl.multiple_of(block_of(u) * width, BLOCK), width)
        return [
            pltpu.make_async_copy(made.at[at, i], field.at[lax.rem(u, freqs), 0, :, :, spot], out_sems.at[at, i])
            for i, field in enumerate((so, ro))
        ]

    def each(copies, what):
        for c in copies:
            c.start() if what == "start" else c.wait()

    def looks_ahead():
        return field_copies(src, rcv, rest[-6], ahead_sems, blocks_of([ahead])[0], 0)

    if not given:

        @pl.when(unit == 0)
        def _():
            each(loads(unit), "start")

    @pl.when(unit + 1 < units)
    def _():
        each(loads(unit + 1), "start")

    if ahead is not None:

        @pl.when(unit == 0)
        def _():
            each(looks_ahead(), "start")

    if given:
        first = rest[0]

        @pl.when(unit == 0)
        def _():
            held[0] = first[...]

        @pl.when(unit > 0)
        def _():
            each(loads(unit), "wait")

    else:
        each(loads(unit), "wait")

    @pl.when(unit >= 2)
    def _():
        each(stores(unit - 2), "wait")

    f = lax.rem(unit, freqs)

    def run(slab):
        parts = [
            (held[slot, 0, 0, :, c], held[slot, 0, 1, :, c], held[slot, 1, 0, :, c], -held[slot, 1, 1, :, c])
            for c in cols
        ]
        turn = turns[f]
        for d in range(slab.shape[1]):
            parts = advance(parts, [slab_view(slab, d, c) * turn for c in cols], wx[f], wy[f])
        for (sr, si, rr, ri), c in zip(parts, cols):
            made[slot, 0, 0, :, c] = sr.astype(made.dtype)
            made[slot, 0, 1, :, c] = si.astype(made.dtype)
            made[slot, 1, 0, :, c] = rr.astype(made.dtype)
            made[slot, 1, 1, :, c] = (-ri).astype(made.dtype)

    for k, slab in enumerate(slabs):

        @pl.when(lax.div(unit, freqs) == k)
        def _():
            run(slab)

    each(stores(unit), "start")

    @pl.when(unit == units - 1)
    def _():
        if units > 1:
            each(stores(unit - 1), "wait")
        each(stores(unit), "wait")
        if ahead is not None:
            each(looks_ahead(), "wait")


def march(names, turns, slabs, wx, wy, src, rcv, first=None, done=(), ahead=None):
    count, cols = len(slabs), slabs[0].shape[-1]
    freqs, height = src.shape[0], src.shape[3]
    vmem, hbm = pl.BlockSpec(memory_space=pltpu.VMEM), pl.BlockSpec(memory_space=pltpu.HBM)
    given = first is not None
    slabs = in_vmem(slabs)
    args = [turns, wx, wy, src, rcv, *slabs] + [first] * given
    in_specs = [vmem, vmem, vmem, hbm, hbm] + [vmem] * (count + given)
    cells = count * cols * height * freqs
    return pl.pallas_call(
        functools.partial(march_body, names=names, freqs=freqs, given=given, ahead=ahead),
        grid=(count * freqs,),
        in_specs=in_specs + [hbm] * len(done),
        out_specs=[hbm, hbm] + [vmem] * (ahead is not None),
        scratch_shapes=[
            pltpu.VMEM((2, 2, 2, height, cols), src.dtype),
            pltpu.VMEM((2, 2, 2, height, cols), src.dtype),
            pltpu.SemaphoreType.DMA((2, 2)),
            pltpu.SemaphoreType.DMA((2, 2)),
            pltpu.SemaphoreType.DMA((2,)),
        ],
        out_shape=[jax.ShapeDtypeStruct(src.shape, src.dtype), jax.ShapeDtypeStruct(rcv.shape, rcv.dtype)]
        + [pltpu.VMEM((2, 2, height, cols), src.dtype)] * (ahead is not None),
        input_output_aliases={len(args) + i: i for i in range(len(done))},
        cost_estimate=pl.CostEstimate(
            flops=cells * DEPTH * 4 * 2 * 4 * BLOCK * 3, bytes_accessed=cells * 16, transcendentals=0
        ),
        compiler_params=pltpu.CompilerParams(vmem_limit_bytes=VMEM),
    )(*args, *done)


def image_body(tiles, turns, wx, wy, src, rcv, *rest, names, scale, per, count):
    slabs, out, wanted, held, lines, sems = rest[:-5], *rest[-5:]
    aper = tiles.shape[0]
    x_blocks = [lax.div(tiles[a], 2) for a in range(aper)]
    copies = []
    for a in range(aper):
        at = pl.ds(pl.multiple_of(x_blocks[a] * BLOCK, BLOCK), BLOCK)
        for i, field in enumerate((src, rcv)):
            copies.append(pltpu.make_async_copy(field.at[:, 0, :, :, at], wanted.at[a, i], sems.at[a, i]))
    for c in copies:
        c.start()
    places = blocks_of(names)
    for a in range(aper):
        column = pl.multiple_of(lax.rem(x_blocks[a], per) * BLOCK, BLOCK)
        for k, slab in enumerate(slabs):

            @pl.when(places[k] == lax.div(x_blocks[a], per))
            def _():
                held[a] = slab[:, :, :, pl.ds(column, BLOCK)]

    for c in copies:
        c.wait()
    freqs = wanted.shape[2]
    parts = [
        [(wanted[a, 0, f, 0], wanted[a, 0, f, 1], wanted[a, 1, f, 0], -wanted[a, 1, f, 1]) for a in range(aper)]
        for f in range(freqs)
    ]
    half = BLOCK // 2
    for d in range(held.shape[2]):
        views = [slab_view(held.at[a], d, slice(0, BLOCK)) for a in range(aper)]
        parts = [advance(parts[f], [v * turns[f] for v in views], wx[f], wy[f]) for f in range(freqs)]
        for a in range(aper):
            term = sum(sr * rr - si * ri for sr, si, rr, ri in (p[a] for p in parts))
            odd = lax.rem(tiles[a], 2) == 1
            lines[a, :, :half] = jnp.where(odd, term[:, half:], term[:, :half]) * scale
            pairs_of = lines.shape[1] // 2
            even_odd = [lines[a, pl.ds(k, pairs_of, stride=2), :half] for k in range(2)]
            both = jnp.concatenate(even_odd, 1)
            out[:, a, d] = both.reshape(count, pairs_of // count, BLOCK)


def image_terms(tiles, names, turns, wx, wy, src, rcv, slabs, scale, count):
    steps, cols = slabs[0].shape[1], slabs[0].shape[-1]
    slabs = in_vmem(slabs)
    freqs, _, _, height, _ = src.shape
    aper = tiles.shape[0]
    vmem, hbm = pl.BlockSpec(memory_space=pltpu.VMEM), pl.BlockSpec(memory_space=pltpu.HBM)
    shape = (count, aper, steps, height // 2 // count, BLOCK)
    return pl.pallas_call(
        functools.partial(image_body, names=names, scale=scale, per=cols // BLOCK, count=count),
        in_specs=[pl.BlockSpec(memory_space=pltpu.SMEM), vmem, vmem, vmem, hbm, hbm] + [vmem] * len(slabs),
        out_specs=vmem,
        out_shape=jax.ShapeDtypeStruct(shape, jnp.float32),
        scratch_shapes=[
            pltpu.VMEM((aper, 2, freqs, 2, height, BLOCK), src.dtype),
            pltpu.VMEM((aper,) + slabs[0].shape[:3] + (BLOCK,), jnp.float32),
            pltpu.VMEM((aper, height, BLOCK), jnp.float32),
            pltpu.SemaphoreType.DMA((aper, 2)),
        ],
        cost_estimate=pl.CostEstimate(
            flops=aper * BLOCK * height * freqs * steps * 4 * 2 * 4 * BLOCK * 3, bytes_accessed=1 << 21, transcendentals=0
        ),
        compiler_params=pltpu.CompilerParams(vmem_limit_bytes=VMEM),
    )(tiles, turns, wx, wy, src, rcv, *slabs)


def deal_body(ids, parts, out):
    total = jnp.sum(parts[...], axis=0)
    spare = out.shape[1] - total.shape[0] - ids.shape[0]
    total = jnp.concatenate([total, ids[...], jnp.zeros((spare, BLOCK), jnp.float32)], 0)
    for j in range(out.shape[0]):
        out[j] = total


def deal(ids, parts, shots):
    rows = parts.shape[1] + 8
    return pl.pallas_call(
        deal_body,
        in_specs=[pl.BlockSpec(memory_space=pltpu.VMEM)] * 2,
        out_specs=pl.BlockSpec(memory_space=pltpu.VMEM),
        out_shape=jax.ShapeDtypeStruct((shots, rows, BLOCK), jnp.float32),
        compiler_params=pltpu.CompilerParams(vmem_limit_bytes=VMEM),
    )(ids, pltpu.with_memory_space_constraint(parts, pltpu.VMEM))


def collect_body(entries, parts, out, *, aper):
    steps = out.shape[1]
    rows = out.shape[2] // BLOCK
    size = steps * rows
    for p in range(out.shape[0]):
        total = jnp.zeros((size, BLOCK), jnp.float32)
        for s in range(parts.shape[0]):
            for a in range(aper):
                at = aper * size + a
                named = parts[s, at : at + 1] == entries[p : p + 1]
                total += jnp.where(named, parts[s, a * size : (a + 1) * size], 0.0)
        for d in range(steps):
            for r in range(rows):
                out[p, d, r * BLOCK : (r + 1) * BLOCK] = total[d * rows + r]


def collect(entries, parts, aper, steps, length):
    return pl.pallas_call(
        functools.partial(collect_body, aper=aper),
        in_specs=[pl.BlockSpec(memory_space=pltpu.VMEM)] * 2,
        out_specs=pl.BlockSpec(memory_space=pltpu.VMEM),
        out_shape=jax.ShapeDtypeStruct((entries.shape[0], steps, length), jnp.float32),
        compiler_params=pltpu.CompilerParams(vmem_limit_bytes=VMEM),
    )(entries, pltpu.with_memory_space_constraint(parts, pltpu.VMEM))


def cut_body(slab, out, sems, *, cols):
    y = here()[0]
    xs = out.shape[1]
    copies = [
        pltpu.make_async_copy(
            slab.at[:, :, :, pl.ds(pl.multiple_of(y * cols, BLOCK), cols)], out.at[:, :, 0], sems.at[xs]
        )
    ]
    for x in range(xs):
        copies.append(
            pltpu.make_async_copy(slab.at[:, y, :, pl.ds((xs + x) * cols, cols)], out.at[:, x, 1], sems.at[x])
        )
    for c in copies:
        c.start()
    for c in copies:
        c.wait()


def cut(slab, cols):
    zls, xs, rows, _ = slab.shape
    slab = pltpu.with_memory_space_constraint(slab, pltpu.HBM)
    return pl.pallas_call(
        functools.partial(cut_body, cols=cols),
        in_specs=[pl.BlockSpec(memory_space=pltpu.HBM)],
        out_specs=pl.BlockSpec(memory_space=pltpu.VMEM),
        out_shape=jax.ShapeDtypeStruct((zls, xs, CORES, rows, cols), slab.dtype),
        scratch_shapes=[pltpu.SemaphoreType.DMA((xs + 1,))],
        compiler_params=pltpu.CompilerParams(vmem_limit_bytes=VMEM),
    )(slab)


def sweep_weights(xc, yc):
    xr, xi = xc[:, 0], xc[:, 1]
    yr, yi = jnp.swapaxes(yc[:, 0], 1, 2), jnp.swapaxes(yc[:, 1], 1, 2)
    join = lambda a, b, c, d: jnp.concatenate([jnp.concatenate([a, b], 2), jnp.concatenate([c, d], 2)], 1)
    return join(xr, xi, -xi, xr), join(yr, -yi, yi, yr)


def pairs(mesh_shape, move):
    freq, shot = mesh_shape
    at = lambda zh, y, zl, x, c: ((zh * YS + y) * shot) + (zl * XS + x) * CORES + c
    out = []
    for zh in range(freq // YS):
        for y in range(YS):
            for zl in range(shot // (XS * CORES)):
                for x in range(XS):
                    for c in range(CORES):
                        out.append((at(zh, y, zl, x, c), at(*move(zh, y, zl, x, c))))
    return out


def row_groups(mesh_shape):
    freq, shot = mesh_shape
    zhs, zls = freq // YS, shot // (XS * CORES)
    at = lambda zh, y, zl, x, c: ((zh * YS + y) * shot) + (zl * XS + x) * CORES + c
    out = [[at(zh, y, zl, x, 0) for zl in range(zls) for x in range(XS)] for zh in range(zhs) for y in range(YS)]
    return out + [[at(zh, y, zl, x, 1) for zl in range(zls) for y in range(YS)] for zh in range(zhs) for x in range(XS)]


def local(
    source_field,
    receiver_field,
    angular_freq,
    x_correction,
    y_correction,
    velocity,
    slab_owner,
    apertures,
    tile_order,
):
    freqs_dev, shots = lax.axis_size("freq"), lax.axis_size("shot")
    freq_total = angular_freq.shape[0] * freqs_dev
    height, width = velocity.shape[1:]
    zls = shots // (XS * CORES)
    cols = width // (CORES * XS)
    rows = height // (zls * XS)
    send = lambda v, move: lax.ppermute(v, AXES, pairs((freqs_dev, shots), move))

    outgoing = cut(velocity.reshape(zls, XS, rows, width), cols).reshape(shots, rows, cols)
    arrived = lax.all_to_all(outgoing, "shot", 0, 0, tiled=True)
    mine = jnp.stack([lax.dynamic_index_in_dim(arrived, slab_owner[d], 0, keepdims=False) for d in range(DEPTH)])

    groups = row_groups((freqs_dev, shots))
    members = len(groups[0])
    own = jnp.broadcast_to(mine[None], (members,) + mine.shape)
    own = lax.all_to_all(own, AXES, 0, 0, axis_index_groups=groups, tiled=True)

    shift = lambda k: lambda zh, y, zl, x, c: (zh, (y + k) % YS, zl, x, c) if c == 0 else (zh, y, zl, (x + k) % XS, c)
    cross = lambda k: lambda zh, y, zl, x, c: (zh, y, zl, (x + k) % XS, c) if c == 0 else (zh, (y + k) % YS, zl, x, c)
    swap = lambda zh, y, zl, x, c: (zh, y, zl, x, 1 - c)
    wx, wy = sweep_weights(x_correction, y_correction)
    turns = jnp.broadcast_to((angular_freq * (0.5 / math.pi))[:, None, None], (angular_freq.shape[0], 1, BLOCK))
    src = pltpu.with_memory_space_constraint(source_field, pltpu.HBM)
    rcv = pltpu.with_memory_space_constraint(receiver_field, pltpu.HBM)

    tiles = apertures[0]
    rows_of = lambda ids: jnp.broadcast_to(ids.astype(jnp.float32)[:, None], (ids.shape[0], BLOCK))
    entries = lax.dynamic_slice_in_dim(tile_order, lax.axis_index("shot") * TILE_DEV, TILE_DEV)
    order = [[(0, 0), (0, 1)], [(1, 0), (3, 0)], [(1, 1), (3, 1)], [(2, 0), (2, 1)]]
    firsts = [fetch(blocks[0], src, rcv, cols) for blocks in order[:EARLY]]
    own, wx, wy, turns, named, entries, *firsts = lax.optimization_barrier(
        (own, wx, wy, turns, rows_of(tiles), rows_of(entries), *firsts)
    )

    def forward(call, slabs, done=()):
        ahead = order[call + 1][0] if call in AHEAD else None
        out = march(order[call], turns, slabs, wx, wy, src, rcv, firsts[call], tuple(done), ahead)
        firsts.append(out[2] if ahead else None)
        return out[:2]

    own_p = send(own, swap)
    s1, s3 = send(own, shift(1)), send(own, shift(3))
    fields = forward(0, [own, own_p])
    s1, s3, later, later_p, *fields = lax.optimization_barrier((s1, s3, own, own_p, *fields))
    s2, s2_p = send(later, shift(2)), send(later_p, cross(2))
    s1_p, s3_p = send(s1, swap), send(s3, swap)
    fields = forward(1, [s1, s3], fields)
    s2, s2_p, *fields = lax.optimization_barrier((s2, s2_p, *fields))

    slabs = [own, own_p, s1, s3, s1_p, s3_p, s2, s2_p]
    names = [name for names in order for name in names]
    terms = image_terms(tiles, names, turns, wx, wy, src, rcv, slabs, 1.0 / freq_total, freqs_dev)
    length = terms.shape[3] * terms.shape[4]
    terms = lax.all_to_all(terms.reshape(freqs_dev, -1, BLOCK), "freq", 0, 0, tiled=True)
    fields = forward(2, [s1_p, s3_p], fields)
    terms, *fields = lax.optimization_barrier((terms, *fields))
    dealt = lax.all_to_all(deal(named, terms, shots), "shot", 0, 0, tiled=True)
    fields = forward(3, [s2, s2_p], fields)
    image = collect(entries, dealt, tiles.shape[0], DEPTH, length)
    return (*fields, image)


def solution(mesh):
    in_specs = (
        P("freq", "shot", None, None, None),
        P("freq", "shot", None, None, None),
        P("freq"),
        P("freq", None, None, None),
        P("freq", None, None, None),
        P("shot", None, None),
        P(),
        P("shot", None),
        P(),
    )
    out_specs = (
        P("freq", "shot", None, None, None),
        P("freq", "shot", None, None, None),
        P("shot", None, "freq"),
    )
    return jax.shard_map(local, mesh=mesh, in_specs=in_specs, out_specs=out_specs, check_vma=False)
```

```python
import functools
import math

import jax
import jax.numpy as jnp
from jax import lax
from jax.experimental import pallas as pl
from jax.experimental.pallas import tpu as pltpu
from jax.sharding import PartitionSpec as P

DEPTH = 2
TILE_DEV = 4
AXES = ("freq", "shot")
YS = 4
XS = 4
CORES = 2
BLOCK = 128
EARLY = 2
VMEM = 24 * 1024 * 1024
NEAREST = 12582912.0
SIN = (4.442867755889893, -7.307443618774414, 3.594788074493408, -0.7843739986419678)
COS = (1.4142135381698608, -6.978850841522217, 5.7394609451293945, -1.8835630416870117, 0.31069818139076233)


def poly(u, coefs):
    total = coefs[-1] * u + coefs[-2]
    for c in coefs[-3::-1]:
        total = total * u + c
    return total


def sincos(turns):
    r = turns - ((turns + NEAREST) - NEAREST)
    u = r * r
    s = r * poly(u, SIN)
    c = poly(u, COS)
    return s * c, 1.0 - s * s


def rounded(parts):
    return tuple(v.astype(jnp.bfloat16) for v in parts)


def widened(parts):
    return tuple(v.astype(jnp.float32) for v in parts)


def quad(a, b, c, d):
    return jnp.concatenate([jnp.concatenate([a, b], 1), jnp.concatenate([c, d], 1)], 0)


def advance(parts, phases, wx, wy):
    height, width = parts[0][0].shape
    out = []
    for part, phase in zip(parts, phases):
        sr, si, rr, ri = widened(part)
        sin, cos = sincos(phase)
        out.append(rounded((sr * cos - si * sin, sr * sin + si * cos, rr * cos - ri * sin, rr * sin + ri * cos)))
    prod = jnp.dot(jnp.concatenate([quad(*v) for v in out], 0), wx, preferred_element_type=jnp.float32)
    for b, part in enumerate(out):
        x = prod[b * 2 * height : (b + 1) * 2 * height]
        sr, si, rr, ri = widened(part)
        out[b] = rounded(
            (
                sr + x[:height, :width],
                si + x[:height, width:],
                rr + x[height:, :width],
                ri + x[height:, width:],
            )
        )
    right = jnp.concatenate([quad(v[0], v[2], v[1], v[3]) for v in out], 1)
    prod = jnp.dot(wy, right, preferred_element_type=jnp.float32)
    for b, part in enumerate(out):
        y = prod[:, b * 2 * width : (b + 1) * 2 * width]
        sr, si, rr, ri = widened(part)
        out[b] = (
            sr + y[:height, :width],
            si + y[height:, :width],
            rr + y[:height, width:],
            ri + y[height:, width:],
        )
    return out


def slab_view(slab, d, cols):
    rows = slab[:, d, :, cols]
    return rows.reshape(rows.shape[0] * rows.shape[1], rows.shape[2])


def in_vmem(arrays):
    return [pltpu.with_memory_space_constraint(a, pltpu.VMEM) for a in arrays]


def here():
    f_id, s_id = lax.axis_index("freq"), lax.axis_index("shot")
    return lax.rem(f_id, YS), lax.rem(lax.div(s_id, CORES), XS), lax.rem(s_id, CORES)


def column_blocks(k):
    y, x, core = here()
    first = core == 0
    mine = core * XS + lax.rem(jnp.where(first, y, x) + XS - k, XS)
    theirs = (1 - core) * XS + lax.rem(jnp.where(first, x, y) + XS - k, XS)
    return mine, theirs


def blocks_of(names):
    return [column_blocks(k)[theirs] for k, theirs in names]


def field_copies(src, rcv, target, sems, block, f):
    cols = target.shape[-1]
    at = pl.ds(pl.multiple_of(block * cols, BLOCK), cols)
    return [
        pltpu.make_async_copy(field.at[f, 0, :, :, at], target.at[i], sems.at[i])
        for i, field in enumerate((src, rcv))
    ]


def fetch_body(src, rcv, first, sems, *, name):
    copies = field_copies(src, rcv, first, sems, blocks_of([name])[0], 0)
    for c in copies:
        c.start()
    for c in copies:
        c.wait()


def fetch(name, src, rcv, cols):
    height = src.shape[3]
    hbm = pl.BlockSpec(memory_space=pltpu.HBM)
    return pl.pallas_call(
        functools.partial(fetch_body, name=name),
        in_specs=[hbm, hbm],
        out_specs=pl.BlockSpec(memory_space=pltpu.VMEM),
        out_shape=pltpu.VMEM((2, 2, height, cols), src.dtype),
        scratch_shapes=[pltpu.SemaphoreType.DMA((2,))],
        cost_estimate=pl.CostEstimate(flops=0, bytes_accessed=1 << 22, transcendentals=0),
        compiler_params=pltpu.CompilerParams(vmem_limit_bytes=VMEM),
    )(src, rcv)


def march_body(turns, wx, wy, src, rcv, *rest, names, freqs, given):
    count = len(names)
    slabs, rest = rest[:count], rest[count:]
    so, ro, held, made, in_sems, out_sems = rest[-6:]
    cols = [slice(c, c + BLOCK) for c in range(0, held.shape[-1], BLOCK)]
    unit = pl.program_id(0)
    units = count * freqs
    where = blocks_of(names)
    slot = lax.rem(unit, 2)

    def block_of(u):
        block, i = where[0], lax.div(u, freqs)
        for k in range(1, count):
            block = jnp.where(i == k, where[k], block)
        return block

    def loads(u):
        at = lax.rem(u, 2)
        return field_copies(src, rcv, held.at[at], in_sems.at[at], block_of(u), lax.rem(u, freqs))

    def stores(u):
        at = lax.rem(u, 2)
        width = made.shape[-1]
        spot = pl.ds(pl.multiple_of(block_of(u) * width, BLOCK), width)
        return [
            pltpu.make_async_copy(made.at[at, i], field.at[lax.rem(u, freqs), 0, :, :, spot], out_sems.at[at, i])
            for i, field in enumerate((so, ro))
        ]

    def each(copies, what):
        for c in copies:
            c.start() if what == "start" else c.wait()

    if not given:

        @pl.when(unit == 0)
        def _():
            each(loads(unit), "start")

    @pl.when(unit + 1 < units)
    def _():
        each(loads(unit + 1), "start")

    if given:
        first = rest[0]

        @pl.when(unit == 0)
        def _():
            held[0] = first[...]

        @pl.when(unit > 0)
        def _():
            each(loads(unit), "wait")

    else:
        each(loads(unit), "wait")

    @pl.when(unit >= 2)
    def _():
        each(stores(unit - 2), "wait")

    f = lax.rem(unit, freqs)

    def run(slab):
        parts = [
            (held[slot, 0, 0, :, c], held[slot, 0, 1, :, c], held[slot, 1, 0, :, c], -held[slot, 1, 1, :, c])
            for c in cols
        ]
        turn = turns[f]
        for d in range(slab.shape[1]):
            parts = advance(parts, [slab_view(slab, d, c) * turn for c in cols], wx[f], wy[f])
        for (sr, si, rr, ri), c in zip(parts, cols):
            made[slot, 0, 0, :, c] = sr.astype(made.dtype)
            made[slot, 0, 1, :, c] = si.astype(made.dtype)
            made[slot, 1, 0, :, c] = rr.astype(made.dtype)
            made[slot, 1, 1, :, c] = (-ri).astype(made.dtype)

    for k, slab in enumerate(slabs):

        @pl.when(lax.div(unit, freqs) == k)
        def _():
            run(slab)

    each(stores(unit), "start")

    @pl.when(unit == units - 1)
    def _():
        if units > 1:
            each(stores(unit - 1), "wait")
        each(stores(unit), "wait")


def march(names, turns, slabs, wx, wy, src, rcv, first=None, done=()):
    count, cols = len(slabs), slabs[0].shape[-1]
    freqs, height = src.shape[0], src.shape[3]
    vmem, hbm = pl.BlockSpec(memory_space=pltpu.VMEM), pl.BlockSpec(memory_space=pltpu.HBM)
    given = first is not None
    slabs = in_vmem(slabs)
    args = [turns, wx, wy, src, rcv, *slabs] + [first] * given
    in_specs = [vmem, vmem, vmem, hbm, hbm] + [vmem] * (count + given)
    cells = count * cols * height * freqs
    return pl.pallas_call(
        functools.partial(march_body, names=names, freqs=freqs, given=given),
        grid=(count * freqs,),
        in_specs=in_specs + [hbm] * len(done),
        out_specs=[hbm, hbm],
        scratch_shapes=[
            pltpu.VMEM((2, 2, 2, height, cols), src.dtype),
            pltpu.VMEM((2, 2, 2, height, cols), src.dtype),
            pltpu.SemaphoreType.DMA((2, 2)),
            pltpu.SemaphoreType.DMA((2, 2)),
        ],
        out_shape=[jax.ShapeDtypeStruct(src.shape, src.dtype), jax.ShapeDtypeStruct(rcv.shape, rcv.dtype)],
        input_output_aliases={len(args) + i: i for i in range(len(done))},
        cost_estimate=pl.CostEstimate(
            flops=cells * DEPTH * 4 * 2 * 4 * BLOCK * 3, bytes_accessed=cells * 16, transcendentals=0
        ),
        compiler_params=pltpu.CompilerParams(vmem_limit_bytes=VMEM),
    )(*args, *done)


def image_body(ids, turns, wx, wy, src, rcv, *rest, names, scale, per, count):
    slabs, out, wanted, held, lines, sems = rest[:-5], *rest[-5:]
    aper = ids.shape[0]
    tiles = [jnp.max(ids[a : a + 1]).astype(jnp.int32) for a in range(aper)]
    x_blocks = [lax.div(tiles[a], 2) for a in range(aper)]
    copies = []
    for a in range(aper):
        at = pl.ds(pl.multiple_of(x_blocks[a] * BLOCK, BLOCK), BLOCK)
        for i, field in enumerate((src, rcv)):
            copies.append(pltpu.make_async_copy(field.at[:, 0, :, :, at], wanted.at[a, i], sems.at[a, i]))
    for c in copies:
        c.start()
    places = blocks_of(names)
    for a in range(aper):
        column = pl.multiple_of(lax.rem(x_blocks[a], per) * BLOCK, BLOCK)
        for k, slab in enumerate(slabs):

            @pl.when(places[k] == lax.div(x_blocks[a], per))
            def _():
                held[a] = slab[:, :, :, pl.ds(column, BLOCK)]

    for c in copies:
        c.wait()
    freqs = wanted.shape[2]
    parts = [
        [(wanted[a, 0, f, 0], wanted[a, 0, f, 1], wanted[a, 1, f, 0], -wanted[a, 1, f, 1]) for a in range(aper)]
        for f in range(freqs)
    ]
    half = BLOCK // 2
    for d in range(held.shape[2]):
        views = [slab_view(held.at[a], d, slice(0, BLOCK)) for a in range(aper)]
        parts = [advance(parts[f], [v * turns[f] for v in views], wx[f], wy[f]) for f in range(freqs)]
        for a in range(aper):
            term = sum(sr * rr - si * ri for sr, si, rr, ri in (p[a] for p in parts))
            odd = lax.rem(tiles[a], 2) == 1
            lines[a, :, :half] = jnp.where(odd, term[:, half:], term[:, :half]) * scale
            pairs_of = lines.shape[1] // 2
            even_odd = [lines[a, pl.ds(k, pairs_of, stride=2), :half] for k in range(2)]
            both = jnp.concatenate(even_odd, 1)
            out[:, a, d] = both.reshape(count, pairs_of // count, BLOCK)


def image_terms(ids, names, turns, wx, wy, src, rcv, slabs, scale, count):
    steps, cols = slabs[0].shape[1], slabs[0].shape[-1]
    slabs = in_vmem(slabs)
    freqs, _, _, height, _ = src.shape
    aper = ids.shape[0]
    vmem, hbm = pl.BlockSpec(memory_space=pltpu.VMEM), pl.BlockSpec(memory_space=pltpu.HBM)
    shape = (count, aper, steps, height // 2 // count, BLOCK)
    return pl.pallas_call(
        functools.partial(image_body, names=names, scale=scale, per=cols // BLOCK, count=count),
        in_specs=[vmem, vmem, vmem, vmem, hbm, hbm] + [vmem] * len(slabs),
        out_specs=vmem,
        out_shape=jax.ShapeDtypeStruct(shape, jnp.float32),
        scratch_shapes=[
            pltpu.VMEM((aper, 2, freqs, 2, height, BLOCK), src.dtype),
            pltpu.VMEM((aper,) + slabs[0].shape[:3] + (BLOCK,), jnp.float32),
            pltpu.VMEM((aper, height, BLOCK), jnp.float32),
            pltpu.SemaphoreType.DMA((aper, 2)),
        ],
        cost_estimate=pl.CostEstimate(
            flops=aper * BLOCK * height * freqs * steps * 4 * 2 * 4 * BLOCK * 3, bytes_accessed=1 << 21, transcendentals=0
        ),
        compiler_params=pltpu.CompilerParams(vmem_limit_bytes=VMEM),
    )(ids, turns, wx, wy, src, rcv, *slabs)


def deal_body(ids, parts, out):
    total = jnp.sum(parts[...], axis=0)
    spare = out.shape[1] - total.shape[0] - ids.shape[0]
    total = jnp.concatenate([total, ids[...], jnp.zeros((spare, BLOCK), jnp.float32)], 0)
    for j in range(out.shape[0]):
        out[j] = total


def deal(ids, parts, shots):
    rows = parts.shape[1] + 8
    return pl.pallas_call(
        deal_body,
        in_specs=[pl.BlockSpec(memory_space=pltpu.VMEM)] * 2,
        out_specs=pl.BlockSpec(memory_space=pltpu.VMEM),
        out_shape=jax.ShapeDtypeStruct((shots, rows, BLOCK), jnp.float32),
        compiler_params=pltpu.CompilerParams(vmem_limit_bytes=VMEM),
    )(ids, pltpu.with_memory_space_constraint(parts, pltpu.VMEM))


def collect_body(entries, parts, out, *, aper):
    steps = out.shape[1]
    rows = out.shape[2] // BLOCK
    size = steps * rows
    for p in range(out.shape[0]):
        total = jnp.zeros((size, BLOCK), jnp.float32)
        for s in range(parts.shape[0]):
            for a in range(aper):
                at = aper * size + a
                named = parts[s, at : at + 1] == entries[p : p + 1]
                total += jnp.where(named, parts[s, a * size : (a + 1) * size], 0.0)
        for d in range(steps):
            for r in range(rows):
                out[p, d, r * BLOCK : (r + 1) * BLOCK] = total[d * rows + r]


def collect(entries, parts, aper, steps, length):
    return pl.pallas_call(
        functools.partial(collect_body, aper=aper),
        in_specs=[pl.BlockSpec(memory_space=pltpu.VMEM)] * 2,
        out_specs=pl.BlockSpec(memory_space=pltpu.VMEM),
        out_shape=jax.ShapeDtypeStruct((entries.shape[0], steps, length), jnp.float32),
        compiler_params=pltpu.CompilerParams(vmem_limit_bytes=VMEM),
    )(entries, pltpu.with_memory_space_constraint(parts, pltpu.VMEM))


def cut_body(slab, out, held, in_sems, out_sems, *, cols):
    y = here()[0]
    xs = out.shape[1]
    first = pl.ds(pl.multiple_of(y * cols, BLOCK), cols)
    parts = [(slab.at[:, x, :, first], (slice(None), x, 0)) for x in range(xs)]
    parts += [(slab.at[:, y, :, pl.ds((xs + x) * cols, cols)], (slice(None), x, 1)) for x in range(xs)]
    loads = [pltpu.make_async_copy(part, held.at[at], in_sems.at[i]) for i, (part, at) in enumerate(parts)]
    stores = [pltpu.make_async_copy(held.at[at], out.at[at], out_sems.at[i]) for i, (_, at) in enumerate(parts)]
    for c in loads:
        c.start()
    for load, store in zip(loads, stores):
        load.wait()
        store.start()
    for c in stores:
        c.wait()


def cut(slab, cols):
    zls, xs, rows, _ = slab.shape
    slab = pltpu.with_memory_space_constraint(slab, pltpu.HBM)
    shape = (zls, xs, CORES, rows, cols)
    return pl.pallas_call(
        functools.partial(cut_body, cols=cols),
        in_specs=[pl.BlockSpec(memory_space=pltpu.HBM)],
        out_specs=pl.BlockSpec(memory_space=pltpu.HBM),
        out_shape=jax.ShapeDtypeStruct(shape, slab.dtype),
        scratch_shapes=[
            pltpu.VMEM(shape, slab.dtype),
            pltpu.SemaphoreType.DMA((2 * xs,)),
            pltpu.SemaphoreType.DMA((2 * xs,)),
        ],
        compiler_params=pltpu.CompilerParams(vmem_limit_bytes=VMEM),
    )(slab)


def sweep_weights(xc, yc):
    xr, xi = xc[:, 0], xc[:, 1]
    yr, yi = jnp.swapaxes(yc[:, 0], 1, 2), jnp.swapaxes(yc[:, 1], 1, 2)
    join = lambda a, b, c, d: jnp.concatenate([jnp.concatenate([a, b], 2), jnp.concatenate([c, d], 2)], 1)
    return join(xr, xi, -xi, xr), join(yr, -yi, yi, yr)


def pairs(mesh_shape, move):
    freq, shot = mesh_shape
    at = lambda zh, y, zl, x, c: ((zh * YS + y) * shot) + (zl * XS + x) * CORES + c
    out = []
    for zh in range(freq // YS):
        for y in range(YS):
            for zl in range(shot // (XS * CORES)):
                for x in range(XS):
                    for c in range(CORES):
                        out.append((at(zh, y, zl, x, c), at(*move(zh, y, zl, x, c))))
    return out


def row_groups(mesh_shape):
    freq, shot = mesh_shape
    zhs, zls = freq // YS, shot // (XS * CORES)
    at = lambda zh, y, zl, x, c: ((zh * YS + y) * shot) + (zl * XS + x) * CORES + c
    out = [[at(zh, y, zl, x, 0) for zl in range(zls) for x in range(XS)] for zh in range(zhs) for y in range(YS)]
    return out + [[at(zh, y, zl, x, 1) for zl in range(zls) for y in range(YS)] for zh in range(zhs) for x in range(XS)]


def local(
    source_field,
    receiver_field,
    angular_freq,
    x_correction,
    y_correction,
    velocity,
    slab_owner,
    apertures,
    tile_order,
):
    freqs_dev, shots = lax.axis_size("freq"), lax.axis_size("shot")
    freq_total = angular_freq.shape[0] * freqs_dev
    height, width = velocity.shape[1:]
    zls = shots // (XS * CORES)
    cols = width // (CORES * XS)
    rows = height // (zls * XS)
    send = lambda v, move: lax.ppermute(v, AXES, pairs((freqs_dev, shots), move))

    outgoing = cut(velocity.reshape(zls, XS, rows, width), cols).reshape(shots, rows, cols)
    arrived = lax.all_to_all(outgoing, "shot", 0, 0, tiled=True)
    mine = jnp.stack([lax.dynamic_index_in_dim(arrived, slab_owner[d], 0, keepdims=False) for d in range(DEPTH)])

    groups = row_groups((freqs_dev, shots))
    members = len(groups[0])
    own = jnp.broadcast_to(mine[None], (members,) + mine.shape)
    own = lax.all_to_all(own, AXES, 0, 0, axis_index_groups=groups, tiled=True)

    shift = lambda k: lambda zh, y, zl, x, c: (zh, (y + k) % YS, zl, x, c) if c == 0 else (zh, y, zl, (x + k) % XS, c)
    swap = lambda zh, y, zl, x, c: (zh, y, zl, x, 1 - c)
    wx, wy = sweep_weights(x_correction, y_correction)
    turns = jnp.broadcast_to((angular_freq * (0.5 / math.pi))[:, None, None], (angular_freq.shape[0], 1, BLOCK))
    src = pltpu.with_memory_space_constraint(source_field, pltpu.HBM)
    rcv = pltpu.with_memory_space_constraint(receiver_field, pltpu.HBM)

    tiles = apertures[0]
    rows_of = lambda ids: jnp.broadcast_to(ids.astype(jnp.float32)[:, None], (ids.shape[0], BLOCK))
    entries = lax.dynamic_slice_in_dim(tile_order, lax.axis_index("shot") * TILE_DEV, TILE_DEV)
    order = [[(0, 0), (0, 1)], [(1, 0), (3, 0)], [(1, 1), (3, 1)], [(2, 0), (2, 1)]]
    firsts = [fetch(blocks[0], src, rcv, cols) for blocks in order[:EARLY]]
    own, wx, wy, turns, named, entries, *firsts = lax.optimization_barrier(
        (own, wx, wy, turns, rows_of(tiles), rows_of(entries), *firsts)
    )
    firsts += [None] * (len(order) - len(firsts))

    def forward(call, slabs, done=()):
        return march(order[call], turns, slabs, wx, wy, src, rcv, firsts[call], tuple(done))

    own_p = send(own, swap)
    s1, s3 = send(own, shift(1)), send(own, shift(3))
    fields = forward(0, [own, own_p])
    s1, s3, later, *fields = lax.optimization_barrier((s1, s3, own, *fields))
    s2 = send(later, shift(2))
    s1_p, s3_p = send(s1, swap), send(s3, swap)
    fields = forward(1, [s1, s3], fields)
    s2, *fields = lax.optimization_barrier((s2, *fields))
    s2_p = send(s2, swap)

    slabs = [own, own_p, s1, s3, s1_p, s3_p, s2, s2_p]
    names = [name for names in order for name in names]
    terms = image_terms(named, names, turns, wx, wy, src, rcv, slabs, 1.0 / freq_total, freqs_dev)
    length = terms.shape[3] * terms.shape[4]
    terms = lax.all_to_all(terms.reshape(freqs_dev, -1, BLOCK), "freq", 0, 0, tiled=True)
    fields = forward(2, [s1_p, s3_p], fields)
    terms, *fields = lax.optimization_barrier((terms, *fields))
    dealt = lax.all_to_all(deal(named, terms, shots), "shot", 0, 0, tiled=True)
    fields = forward(3, [s2, s2_p], fields)
    image = collect(entries, dealt, tiles.shape[0], DEPTH, length)
    return (*fields, image)


def solution(mesh):
    in_specs = (
        P("freq", "shot", None, None, None),
        P("freq", "shot", None, None, None),
        P("freq"),
        P("freq", None, None, None),
        P("freq", None, None, None),
        P("shot", None, None),
        P(),
        P("shot", None),
        P(),
    )
    out_specs = (
        P("freq", "shot", None, None, None),
        P("freq", "shot", None, None, None),
        P("shot", None, "freq"),
    )
    return jax.shard_map(local, mesh=mesh, in_specs=in_specs, out_specs=out_specs, check_vma=False)
```

```python
import functools
import math

import jax
import jax.numpy as jnp
from jax import lax
from jax.experimental import pallas as pl
from jax.experimental.pallas import tpu as pltpu
from jax.sharding import PartitionSpec as P

DEPTH = 2
TILE_DEV = 4
AXES = ("freq", "shot")
YS = 4
XS = 4
CORES = 2
BLOCK = 128
EARLY = 2
VMEM = 24 * 1024 * 1024
NEAREST = 12582912.0
SIN = (4.442867755889893, -7.307443618774414, 3.594788074493408, -0.7843739986419678)
COS = (1.4142135381698608, -6.978850841522217, 5.7394609451293945, -1.8835630416870117, 0.31069818139076233)


def poly(u, coefs):
    total = coefs[-1] * u + coefs[-2]
    for c in coefs[-3::-1]:
        total = total * u + c
    return total


def sincos(turns):
    r = turns - ((turns + NEAREST) - NEAREST)
    u = r * r
    s = r * poly(u, SIN)
    c = poly(u, COS)
    return s * c, 1.0 - s * s


def rounded(parts):
    return tuple(v.astype(jnp.bfloat16) for v in parts)


def widened(parts):
    return tuple(v.astype(jnp.float32) for v in parts)


def quad(a, b, c, d):
    return jnp.concatenate([jnp.concatenate([a, b], 1), jnp.concatenate([c, d], 1)], 0)


def advance(parts, phases, wx, wy):
    height, width = parts[0][0].shape
    out = []
    for part, phase in zip(parts, phases):
        sr, si, rr, ri = widened(part)
        sin, cos = sincos(phase)
        out.append(rounded((sr * cos - si * sin, sr * sin + si * cos, rr * cos - ri * sin, rr * sin + ri * cos)))
    prod = jnp.dot(jnp.concatenate([quad(*v) for v in out], 0), wx, preferred_element_type=jnp.float32)
    for b, part in enumerate(out):
        x = prod[b * 2 * height : (b + 1) * 2 * height]
        sr, si, rr, ri = widened(part)
        out[b] = rounded(
            (
                sr + x[:height, :width],
                si + x[:height, width:],
                rr + x[height:, :width],
                ri + x[height:, width:],
            )
        )
    right = jnp.concatenate([quad(v[0], v[2], v[1], v[3]) for v in out], 1)
    prod = jnp.dot(wy, right, preferred_element_type=jnp.float32)
    for b, part in enumerate(out):
        y = prod[:, b * 2 * width : (b + 1) * 2 * width]
        sr, si, rr, ri = widened(part)
        out[b] = (
            sr + y[:height, :width],
            si + y[height:, :width],
            rr + y[:height, width:],
            ri + y[height:, width:],
        )
    return out


def slab_view(slab, d, cols):
    rows = slab[:, d, :, cols]
    return rows.reshape(rows.shape[0] * rows.shape[1], rows.shape[2])


def in_vmem(arrays):
    return [pltpu.with_memory_space_constraint(a, pltpu.VMEM) for a in arrays]


def here():
    f_id, s_id = lax.axis_index("freq"), lax.axis_index("shot")
    return lax.rem(f_id, YS), lax.rem(lax.div(s_id, CORES), XS), lax.rem(s_id, CORES)


def column_blocks(k):
    y, x, core = here()
    first = core == 0
    mine = core * XS + lax.rem(jnp.where(first, y, x) + XS - k, XS)
    theirs = (1 - core) * XS + lax.rem(jnp.where(first, x, y) + XS - k, XS)
    return mine, theirs


def blocks_of(names):
    return [column_blocks(k)[theirs] for k, theirs in names]


def field_copies(src, rcv, target, sems, block, f):
    cols = target.shape[-1]
    at = pl.ds(pl.multiple_of(block * cols, BLOCK), cols)
    return [
        pltpu.make_async_copy(field.at[f, 0, :, :, at], target.at[i], sems.at[i])
        for i, field in enumerate((src, rcv))
    ]


def fetch_body(src, rcv, first, sems, *, name):
    copies = field_copies(src, rcv, first, sems, blocks_of([name])[0], 0)
    for c in copies:
        c.start()
    for c in copies:
        c.wait()


def fetch(name, src, rcv, cols):
    height = src.shape[3]
    hbm = pl.BlockSpec(memory_space=pltpu.HBM)
    return pl.pallas_call(
        functools.partial(fetch_body, name=name),
        in_specs=[hbm, hbm],
        out_specs=pl.BlockSpec(memory_space=pltpu.VMEM),
        out_shape=pltpu.VMEM((2, 2, height, cols), src.dtype),
        scratch_shapes=[pltpu.SemaphoreType.DMA((2,))],
        cost_estimate=pl.CostEstimate(flops=0, bytes_accessed=1 << 22, transcendentals=0),
        compiler_params=pltpu.CompilerParams(vmem_limit_bytes=VMEM),
    )(src, rcv)


def march_body(turns, wx, wy, src, rcv, *rest, names, freqs, given):
    count = len(names)
    slabs, rest = rest[:count], rest[count:]
    so, ro, held, made, in_sems, out_sems = rest[-6:]
    cols = [slice(c, c + BLOCK) for c in range(0, held.shape[-1], BLOCK)]
    unit = pl.program_id(0)
    units = count * freqs
    where = blocks_of(names)
    slot = lax.rem(unit, 2)

    def block_of(u):
        block, i = where[0], lax.div(u, freqs)
        for k in range(1, count):
            block = jnp.where(i == k, where[k], block)
        return block

    def loads(u):
        at = lax.rem(u, 2)
        return field_copies(src, rcv, held.at[at], in_sems.at[at], block_of(u), lax.rem(u, freqs))

    def stores(u):
        at = lax.rem(u, 2)
        width = made.shape[-1]
        spot = pl.ds(pl.multiple_of(block_of(u) * width, BLOCK), width)
        return [
            pltpu.make_async_copy(made.at[at, i], field.at[lax.rem(u, freqs), 0, :, :, spot], out_sems.at[at, i])
            for i, field in enumerate((so, ro))
        ]

    def each(copies, what):
        for c in copies:
            c.start() if what == "start" else c.wait()

    if not given:

        @pl.when(unit == 0)
        def _():
            each(loads(unit), "start")

    @pl.when(unit + 1 < units)
    def _():
        each(loads(unit + 1), "start")

    if given:
        first = rest[0]

        @pl.when(unit == 0)
        def _():
            held[0] = first[...]

        @pl.when(unit > 0)
        def _():
            each(loads(unit), "wait")

    else:
        each(loads(unit), "wait")

    @pl.when(unit >= 2)
    def _():
        each(stores(unit - 2), "wait")

    f = lax.rem(unit, freqs)

    def run(slab):
        parts = [
            (held[slot, 0, 0, :, c], held[slot, 0, 1, :, c], held[slot, 1, 0, :, c], -held[slot, 1, 1, :, c])
            for c in cols
        ]
        turn = turns[f]
        for d in range(slab.shape[1]):
            parts = advance(parts, [slab_view(slab, d, c) * turn for c in cols], wx[f], wy[f])
        for (sr, si, rr, ri), c in zip(parts, cols):
            made[slot, 0, 0, :, c] = sr.astype(made.dtype)
            made[slot, 0, 1, :, c] = si.astype(made.dtype)
            made[slot, 1, 0, :, c] = rr.astype(made.dtype)
            made[slot, 1, 1, :, c] = (-ri).astype(made.dtype)

    for k, slab in enumerate(slabs):

        @pl.when(lax.div(unit, freqs) == k)
        def _():
            run(slab)

    each(stores(unit), "start")

    @pl.when(unit == units - 1)
    def _():
        if units > 1:
            each(stores(unit - 1), "wait")
        each(stores(unit), "wait")


def march(names, turns, slabs, wx, wy, src, rcv, first=None, done=()):
    count, cols = len(slabs), slabs[0].shape[-1]
    freqs, height = src.shape[0], src.shape[3]
    vmem, hbm = pl.BlockSpec(memory_space=pltpu.VMEM), pl.BlockSpec(memory_space=pltpu.HBM)
    given = first is not None
    slabs = in_vmem(slabs)
    args = [turns, wx, wy, src, rcv, *slabs] + [first] * given
    in_specs = [vmem, vmem, vmem, hbm, hbm] + [vmem] * (count + given)
    cells = count * cols * height * freqs
    return pl.pallas_call(
        functools.partial(march_body, names=names, freqs=freqs, given=given),
        grid=(count * freqs,),
        in_specs=in_specs + [hbm] * len(done),
        out_specs=[hbm, hbm],
        scratch_shapes=[
            pltpu.VMEM((2, 2, 2, height, cols), src.dtype),
            pltpu.VMEM((2, 2, 2, height, cols), src.dtype),
            pltpu.SemaphoreType.DMA((2, 2)),
            pltpu.SemaphoreType.DMA((2, 2)),
        ],
        out_shape=[jax.ShapeDtypeStruct(src.shape, src.dtype), jax.ShapeDtypeStruct(rcv.shape, rcv.dtype)],
        input_output_aliases={len(args) + i: i for i in range(len(done))},
        cost_estimate=pl.CostEstimate(
            flops=cells * DEPTH * 4 * 2 * 4 * BLOCK * 3, bytes_accessed=cells * 16, transcendentals=0
        ),
        compiler_params=pltpu.CompilerParams(vmem_limit_bytes=VMEM),
    )(*args, *done)


def image_body(ids, turns, wx, wy, src, rcv, *rest, names, scale, per, count):
    slabs, out, wanted, held, lines, sems = rest[:-5], *rest[-5:]
    aper = ids.shape[0]
    tiles = [jnp.max(ids[a : a + 1]).astype(jnp.int32) for a in range(aper)]
    x_blocks = [lax.div(tiles[a], 2) for a in range(aper)]
    copies = []
    for a in range(aper):
        at = pl.ds(pl.multiple_of(x_blocks[a] * BLOCK, BLOCK), BLOCK)
        for i, field in enumerate((src, rcv)):
            copies.append(pltpu.make_async_copy(field.at[:, 0, :, :, at], wanted.at[a, i], sems.at[a, i]))
    for c in copies:
        c.start()
    places = blocks_of(names)
    for a in range(aper):
        column = pl.multiple_of(lax.rem(x_blocks[a], per) * BLOCK, BLOCK)
        for k, slab in enumerate(slabs):

            @pl.when(places[k] == lax.div(x_blocks[a], per))
            def _():
                held[a] = slab[:, :, :, pl.ds(column, BLOCK)]

    for c in copies:
        c.wait()
    freqs = wanted.shape[2]
    parts = [
        [(wanted[a, 0, f, 0], wanted[a, 0, f, 1], wanted[a, 1, f, 0], -wanted[a, 1, f, 1]) for a in range(aper)]
        for f in range(freqs)
    ]
    half = BLOCK // 2
    for d in range(held.shape[2]):
        views = [slab_view(held.at[a], d, slice(0, BLOCK)) for a in range(aper)]
        parts = [advance(parts[f], [v * turns[f] for v in views], wx[f], wy[f]) for f in range(freqs)]
        for a in range(aper):
            term = sum(sr * rr - si * ri for sr, si, rr, ri in (p[a] for p in parts))
            odd = lax.rem(tiles[a], 2) == 1
            lines[a, :, :half] = jnp.where(odd, term[:, half:], term[:, :half]) * scale
            pairs_of = lines.shape[1] // 2
            even_odd = [lines[a, pl.ds(k, pairs_of, stride=2), :half] for k in range(2)]
            both = jnp.concatenate(even_odd, 1)
            out[:, a, d] = both.reshape(count, pairs_of // count, BLOCK)


def image_terms(ids, names, turns, wx, wy, src, rcv, slabs, scale, count):
    steps, cols = slabs[0].shape[1], slabs[0].shape[-1]
    slabs = in_vmem(slabs)
    freqs, _, _, height, _ = src.shape
    aper = ids.shape[0]
    vmem, hbm = pl.BlockSpec(memory_space=pltpu.VMEM), pl.BlockSpec(memory_space=pltpu.HBM)
    shape = (count, aper, steps, height // 2 // count, BLOCK)
    return pl.pallas_call(
        functools.partial(image_body, names=names, scale=scale, per=cols // BLOCK, count=count),
        in_specs=[vmem, vmem, vmem, vmem, hbm, hbm] + [vmem] * len(slabs),
        out_specs=vmem,
        out_shape=jax.ShapeDtypeStruct(shape, jnp.float32),
        scratch_shapes=[
            pltpu.VMEM((aper, 2, freqs, 2, height, BLOCK), src.dtype),
            pltpu.VMEM((aper,) + slabs[0].shape[:3] + (BLOCK,), jnp.float32),
            pltpu.VMEM((aper, height, BLOCK), jnp.float32),
            pltpu.SemaphoreType.DMA((aper, 2)),
        ],
        cost_estimate=pl.CostEstimate(
            flops=aper * BLOCK * height * freqs * steps * 4 * 2 * 4 * BLOCK * 3, bytes_accessed=1 << 21, transcendentals=0
        ),
        compiler_params=pltpu.CompilerParams(vmem_limit_bytes=VMEM),
    )(ids, turns, wx, wy, src, rcv, *slabs)


def deal_body(ids, parts, out):
    total = jnp.sum(parts[...], axis=0)
    spare = out.shape[1] - total.shape[0] - ids.shape[0]
    total = jnp.concatenate([total, ids[...], jnp.zeros((spare, BLOCK), jnp.float32)], 0)
    for j in range(out.shape[0]):
        out[j] = total


def deal(ids, parts, shots):
    rows = parts.shape[1] + 8
    return pl.pallas_call(
        deal_body,
        in_specs=[pl.BlockSpec(memory_space=pltpu.VMEM)] * 2,
        out_specs=pl.BlockSpec(memory_space=pltpu.VMEM),
        out_shape=jax.ShapeDtypeStruct((shots, rows, BLOCK), jnp.float32),
        compiler_params=pltpu.CompilerParams(vmem_limit_bytes=VMEM),
    )(ids, pltpu.with_memory_space_constraint(parts, pltpu.VMEM))


def collect_body(entries, parts, out, *, aper):
    steps = out.shape[1]
    rows = out.shape[2] // BLOCK
    size = steps * rows
    for p in range(out.shape[0]):
        total = jnp.zeros((size, BLOCK), jnp.float32)
        for s in range(parts.shape[0]):
            for a in range(aper):
                at = aper * size + a
                named = parts[s, at : at + 1] == entries[p : p + 1]
                total += jnp.where(named, parts[s, a * size : (a + 1) * size], 0.0)
        for d in range(steps):
            for r in range(rows):
                out[p, d, r * BLOCK : (r + 1) * BLOCK] = total[d * rows + r]


def collect(entries, parts, aper, steps, length):
    return pl.pallas_call(
        functools.partial(collect_body, aper=aper),
        in_specs=[pl.BlockSpec(memory_space=pltpu.VMEM)] * 2,
        out_specs=pl.BlockSpec(memory_space=pltpu.VMEM),
        out_shape=jax.ShapeDtypeStruct((entries.shape[0], steps, length), jnp.float32),
        compiler_params=pltpu.CompilerParams(vmem_limit_bytes=VMEM),
    )(entries, pltpu.with_memory_space_constraint(parts, pltpu.VMEM))


def cut_body(slab, out, held, in_sems, out_sems, *, cols):
    y = here()[0]
    xs = out.shape[1]
    first = pl.ds(pl.multiple_of(y * cols, BLOCK), cols)
    parts = [(slab.at[:, x, :, first], (slice(None), x, 0)) for x in range(xs)]
    parts += [(slab.at[:, y, :, pl.ds((xs + x) * cols, cols)], (slice(None), x, 1)) for x in range(xs)]
    loads = [pltpu.make_async_copy(part, held.at[at], in_sems.at[i]) for i, (part, at) in enumerate(parts)]
    stores = [pltpu.make_async_copy(held.at[at], out.at[at], out_sems.at[i]) for i, (_, at) in enumerate(parts)]
    for c in loads:
        c.start()
    for load, store in zip(loads, stores):
        load.wait()
        store.start()
    for c in stores:
        c.wait()


def cut(slab, cols):
    zls, xs, rows, _ = slab.shape
    slab = pltpu.with_memory_space_constraint(slab, pltpu.HBM)
    shape = (zls, xs, CORES, rows, cols)
    return pl.pallas_call(
        functools.partial(cut_body, cols=cols),
        in_specs=[pl.BlockSpec(memory_space=pltpu.HBM)],
        out_specs=pl.BlockSpec(memory_space=pltpu.HBM),
        out_shape=jax.ShapeDtypeStruct(shape, slab.dtype),
        scratch_shapes=[
            pltpu.VMEM(shape, slab.dtype),
            pltpu.SemaphoreType.DMA((2 * xs,)),
            pltpu.SemaphoreType.DMA((2 * xs,)),
        ],
        compiler_params=pltpu.CompilerParams(vmem_limit_bytes=VMEM),
    )(slab)


def sweep_weights(xc, yc):
    xr, xi = xc[:, 0], xc[:, 1]
    yr, yi = jnp.swapaxes(yc[:, 0], 1, 2), jnp.swapaxes(yc[:, 1], 1, 2)
    join = lambda a, b, c, d: jnp.concatenate([jnp.concatenate([a, b], 2), jnp.concatenate([c, d], 2)], 1)
    return join(xr, xi, -xi, xr), join(yr, -yi, yi, yr)


def pairs(mesh_shape, move):
    freq, shot = mesh_shape
    at = lambda zh, y, zl, x, c: ((zh * YS + y) * shot) + (zl * XS + x) * CORES + c
    out = []
    for zh in range(freq // YS):
        for y in range(YS):
            for zl in range(shot // (XS * CORES)):
                for x in range(XS):
                    for c in range(CORES):
                        out.append((at(zh, y, zl, x, c), at(*move(zh, y, zl, x, c))))
    return out


def row_groups(mesh_shape):
    freq, shot = mesh_shape
    zhs, zls = freq // YS, shot // (XS * CORES)
    at = lambda zh, y, zl, x, c: ((zh * YS + y) * shot) + (zl * XS + x) * CORES + c
    out = [[at(zh, y, zl, x, 0) for zl in range(zls) for x in range(XS)] for zh in range(zhs) for y in range(YS)]
    return out + [[at(zh, y, zl, x, 1) for zl in range(zls) for y in range(YS)] for zh in range(zhs) for x in range(XS)]


def local(
    source_field,
    receiver_field,
    angular_freq,
    x_correction,
    y_correction,
    velocity,
    slab_owner,
    apertures,
    tile_order,
):
    freqs_dev, shots = lax.axis_size("freq"), lax.axis_size("shot")
    freq_total = angular_freq.shape[0] * freqs_dev
    height, width = velocity.shape[1:]
    zls = shots // (XS * CORES)
    cols = width // (CORES * XS)
    rows = height // (zls * XS)
    send = lambda v, move: lax.ppermute(v, AXES, pairs((freqs_dev, shots), move))

    outgoing = cut(velocity.reshape(zls, XS, rows, width), cols).reshape(shots, rows, cols)
    arrived = lax.all_to_all(outgoing, "shot", 0, 0, tiled=True)
    mine = jnp.stack([lax.dynamic_index_in_dim(arrived, slab_owner[d], 0, keepdims=False) for d in range(DEPTH)])

    groups = row_groups((freqs_dev, shots))
    members = len(groups[0])
    own = jnp.broadcast_to(mine[None], (members,) + mine.shape)
    own = lax.all_to_all(own, AXES, 0, 0, axis_index_groups=groups, tiled=True)

    shift = lambda k: lambda zh, y, zl, x, c: (zh, (y + k) % YS, zl, x, c) if c == 0 else (zh, y, zl, (x + k) % XS, c)
    swap = lambda zh, y, zl, x, c: (zh, y, zl, x, 1 - c)
    wx, wy = sweep_weights(x_correction, y_correction)
    turns = jnp.broadcast_to((angular_freq * (0.5 / math.pi))[:, None, None], (angular_freq.shape[0], 1, BLOCK))
    src = pltpu.with_memory_space_constraint(source_field, pltpu.HBM)
    rcv = pltpu.with_memory_space_constraint(receiver_field, pltpu.HBM)

    tiles = apertures[0]
    rows_of = lambda ids: jnp.broadcast_to(ids.astype(jnp.float32)[:, None], (ids.shape[0], BLOCK))
    entries = lax.dynamic_slice_in_dim(tile_order, lax.axis_index("shot") * TILE_DEV, TILE_DEV)
    order = [[(0, 0), (0, 1)], [(1, 0), (3, 0), (1, 1)], [(3, 1)], [(2, 0), (2, 1)]]
    firsts = [fetch(blocks[0], src, rcv, cols) for blocks in order[:EARLY]]
    own, wx, wy, turns, named, entries, *firsts = lax.optimization_barrier(
        (own, wx, wy, turns, rows_of(tiles), rows_of(entries), *firsts)
    )
    firsts += [None] * (len(order) - len(firsts))

    def forward(call, slabs, done=()):
        return march(order[call], turns, slabs, wx, wy, src, rcv, firsts[call], tuple(done))

    own_p = send(own, swap)
    s1, s3 = send(own, shift(1)), send(own, shift(3))
    fields = forward(0, [own, own_p])
    s1, *fields = lax.optimization_barrier((s1, *fields))
    s1_p = send(s1, swap)
    s3, later, *fields = lax.optimization_barrier((s3, own, *fields))
    s2 = send(later, shift(2))
    s3_p = send(s3, swap)
    fields = forward(1, [s1, s3, s1_p], fields)
    s2, *fields = lax.optimization_barrier((s2, *fields))
    s2_p = send(s2, swap)

    slabs = [own, own_p, s1, s3, s1_p, s3_p, s2, s2_p]
    names = [name for names in order for name in names]
    terms = image_terms(named, names, turns, wx, wy, src, rcv, slabs, 1.0 / freq_total, freqs_dev)
    length = terms.shape[3] * terms.shape[4]
    terms = lax.all_to_all(terms.reshape(freqs_dev, -1, BLOCK), "freq", 0, 0, tiled=True)
    fields = forward(2, [s3_p], fields)
    terms, *fields = lax.optimization_barrier((terms, *fields))
    dealt = lax.all_to_all(deal(named, terms, shots), "shot", 0, 0, tiled=True)
    fields = forward(3, [s2, s2_p], fields)
    image = collect(entries, dealt, tiles.shape[0], DEPTH, length)
    return (*fields, image)


def solution(mesh):
    in_specs = (
        P("freq", "shot", None, None, None),
        P("freq", "shot", None, None, None),
        P("freq"),
        P("freq", None, None, None),
        P("freq", None, None, None),
        P("shot", None, None),
        P(),
        P("shot", None),
        P(),
    )
    out_specs = (
        P("freq", "shot", None, None, None),
        P("freq", "shot", None, None, None),
        P("shot", None, "freq"),
    )
    return jax.shard_map(local, mesh=mesh, in_specs=in_specs, out_specs=out_specs, check_vma=False)
```
